1024 devices in a mesh: gx: 8 (over x), gy: 8 (over y), gz: 16 (over z, core).
Axes of the slice: x: 8, y: 8, z: 8, core: 2. Of those that a mesh axis runs over, the one named last changes fastest.
Arguments:
- source: float32 [4, 128, 128, 2048], P(None, 'gx', 'gy', 'gz'), may hold values from -6 to 6
- material_ids: int32 [16, 16, 256], P('gx', 'gy', 'gz'), may hold values from 0 to 7
- material_table: float32 [8], replicated, may hold values from 0.1 to 10
- roughness: float32 [128, 128, 2048], P('gx', 'gy', 'gz'), may hold values from 0.5 to 2
Outputs:
- correction: float32 [4, 128, 128, 2048], P(None, 'gx', 'gy', 'gz')
The draws below stay inside these ranges and needn't reach their ends.
All inputs are finite; a program needn't handle non-finite values.
Results may differ from the reference program's by a relative error of at most 0.0001.
Values sent between devices are 32-bit elements; how exact they have to be, the bound alone decides.
No kernel may reach another device: no remote copies, remote signals or barrier semaphores. Data moves between devices by JAX's collectives and lax.ppermute only.
A program may use at most 128 MiB of HBM per device.

```python
import math
import jax
import jax.numpy as jnp

FIELDS = 4
SWEEPS = 2
COARSE_ITERS = 8
MATERIALS = 8
NX = 128
NY = 128
NZ = 2048


def with_ends(array, key, least, high):
    dims = array.shape
    place = [jax.random.randint(jax.random.fold_in(key, axis), (), 0, dims[axis]) for axis in range(len(dims))]
    array = array.at[tuple(place)].set(least)
    longest = dims.index(max(dims))
    place[longest] = (place[longest] + 1) % dims[longest]
    return array.at[tuple(place)].set(high)


def level_of(key, extent, shards, least, largest):
    level = 1.0
    for axis_at, blocks in shards:
        heights = jax.random.uniform(jax.random.fold_in(jax.random.fold_in(key, 6), axis_at), (blocks,), jnp.float32, least / len(shards), largest / len(shards))
        level = level * jnp.repeat(jnp.exp(heights), extent[axis_at] // blocks).reshape((-1,) + (1,) * (len(extent) - 1 - axis_at))
    return level


def centred(rng, shape, spread, bound, split=(), dtype=jnp.bfloat16):
    loudness = level_of(rng, shape, split, -0.22, 0.18) if split else 1.0
    drawn = jax.random.normal(rng, shape, jnp.float32) * spread * loudness
    return jnp.minimum(jnp.maximum(drawn, -bound), bound).astype(dtype)


def setup_inputs(seed: int = 0) -> dict:
    streams_of = jax.random.split(jax.random.key(seed), 5)
    return {
        "source": centred(streams_of[0], (FIELDS, NX, NY, NZ), 1.0, 6.0, ((1, 8), (2, 8), (3, 16)), jnp.float32),
        "material_ids": with_ends(jax.random.randint(streams_of[1], (NX // 8, NY // 8, NZ // 8), 0, MATERIALS), jax.random.fold_in(streams_of[1], 1), 0, MATERIALS - 1).astype(jnp.int32),
        "material_table": jnp.clip(jnp.exp(jax.random.uniform(streams_of[2], (MATERIALS,), jnp.float32, math.log(0.1), math.log(10.0))), 0.1, 10.0),
        "roughness": jnp.clip(jnp.exp(math.log(2.0) - 1.3862944 * jax.random.uniform(streams_of[3], (NX, NY, NZ), jnp.float32) ** level_of(streams_of[3], (NX, NY, NZ), ((0, 8), (1, 8), (2, 16)), -0.2, 0.2)), 0.5, 2.0),
    }


OMEGA = 0.8

def neighbours(padded):
    total = padded[:, 2:, 1:-1, 1:-1] + padded[:, :-2, 1:-1, 1:-1]
    total = total + padded[:, 1:-1, 2:, 1:-1] + padded[:, 1:-1, :-2, 1:-1]
    total = total + padded[:, 1:-1, 1:-1, 2:] + padded[:, 1:-1, 1:-1, :-2]
    return total

def local_pad(weighted):
    return jnp.pad(weighted, ((0, 0), (1, 1), (1, 1), (1, 1)))

def operate(field, root_coef, pad_func):
    weighted = root_coef * field
    return root_coef * (6.0 * weighted - neighbours(pad_func(weighted)))

def relax(field, right_side, root_coef, step_scale, pad_func):
    return field + step_scale * (right_side - operate(field, root_coef, pad_func))

def coarsen(values):
    fields, size_a, size_b, size_c = values.shape
    shaped = values.reshape(fields, size_a // 2, 2, size_b // 2, 2, size_c // 2, 2)
    return shaped.sum(axis=(2, 4, 6))

def refine(values):
    return jnp.repeat(jnp.repeat(jnp.repeat(values, 2, axis=1), 2, axis=2), 2, axis=3)

def level_cycle(right_side, coefficient, pad_func, coarse_solve):
    root_coef = jnp.sqrt(coefficient)
    step_scale = OMEGA / (6.0 * coefficient)
    field = step_scale * right_side
    for sweep_index in range(SWEEPS - 1):
        field = relax(field, right_side, root_coef, step_scale, pad_func)
    residual = right_side - operate(field, root_coef, pad_func)
    field = field + refine(coarse_solve(0.5 * coarsen(residual)))
    for sweep_index in range(SWEEPS):
        field = relax(field, right_side, root_coef, step_scale, pad_func)
    return field

def coarsest(right_side, coefficient):
    root_coef = jnp.sqrt(coefficient)
    step_scale = OMEGA / (6.0 * coefficient)
    field = step_scale * right_side
    for iter_index in range(COARSE_ITERS - 1):
        field = relax(field, right_side, root_coef, step_scale, local_pad)
    return field

def expand_blocks(blocks):
    return jnp.repeat(jnp.repeat(jnp.repeat(blocks, 8, axis=0), 8, axis=1), 8, axis=2)

def reference(source, material_ids, material_table, roughness):
    viscosity = expand_blocks(material_table[material_ids]) * roughness
    coefficients = [jnp.stack([viscosity, viscosity, viscosity, 1.0 / viscosity])]
    for level_index in range(4):
        coefficients.append(coarsen(coefficients[-1]) * 0.125)

    def solve_level(level_index, right_side):
        if level_index == 4:
            return coarsest(right_side, coefficients[4])

        def deeper(coarse_side):
            return solve_level(level_index + 1, coarse_side)
        return level_cycle(right_side, coefficients[level_index], local_pad, deeper)
    return solve_level(0, source)
```

```python
import functools

import jax
import jax.numpy as jnp
import numpy as np
from jax import lax
from jax.experimental import pallas as pl
from jax.experimental.pallas import tpu as pltpu
from jax.sharding import PartitionSpec as P

F32 = jnp.float32
COARSE_ITERS = 8
TAU = 0.8 / 6.0
LANES = 128
HX0, HY0, HZ0 = 10, 3, 16
Y0 = 16 + 2 * HY0
Y1 = 16
HZ2 = 10
HZ3 = 20


def mm(a, b):
    return jnp.dot(a, b, precision=lax.Precision.HIGHEST, preferred_element_type=F32)


def lane_of(n):
    return lax.broadcasted_iota(jnp.int32, (n, LANES), 1)


def lane_roll(x, shift):
    return pltpu.roll(x, shift % LANES, 1) if shift % LANES else x


def around(ref, x, row, n):
    mid = ref[x, pl.ds(row, n), :]
    total = ref[x - 1, pl.ds(row, n), :] + ref[x + 1, pl.ds(row, n), :]
    total = total + (ref[x, pl.ds(row - 1, n), :] + ref[x, pl.ds(row + 1, n), :])
    return mid, total + (lane_roll(mid, 1) + lane_roll(mid, -1))


def around_whole(ref, x, row, n, width):
    mid = ref[x, pl.ds(row, n), :]
    total = ref[x - 1, pl.ds(row, n), :] + ref[x + 1, pl.ds(row, n), :]
    total = total + (ref[x, pl.ds(row - 1, n), :] + ref[x, pl.ds(row + 1, n), :])
    place = lane_of(n) % width
    total = total + jnp.where(place == 0, 0.0, lane_roll(mid, 1))
    return mid, total + jnp.where(place == width - 1, 0.0, lane_roll(mid, -1))


def chunks(n, size):
    return [(r, min(size, n - r)) for r in range(0, n, size)]


def roots_of(c):
    live = c > 0.0
    inv = lax.rsqrt(jnp.where(live, c, 1.0))
    return jnp.where(live, c * inv, 0.0), jnp.where(live, inv, 0.0)


def inverse(root):
    live = root > 0.0
    return jnp.where(live, 1.0 / jnp.where(live, root, 1.0), 0.0)


def jacobi(live, mid, beta, total):
    return jnp.where(live, 0.2 * mid + beta + TAU * total, 0.0)


def pair_lanes(width, start, fields, out_width, out_start, scale, first=0):
    m = np.zeros((LANES, LANES), np.float32)
    for k, f in enumerate(fields):
        for j in range(out_width):
            for i in range(2):
                m[f * width + start + 2 * j + i, out_start + k * out_width + j] = scale
    return m


def repeat_lanes(width, shift, out_width, out_shift):
    m = np.zeros((LANES, LANES), np.float32)
    for f in range(4):
        for j in range(out_width):
            i = shift + (j - out_shift) // 2
            if 0 <= i < width:
                m[f * width + i, f * out_width + j] = 1.0
    return m


def rows_kernel(xlo, source, visc, xhi, rows, ylo, yhi):
    def put(x, f, plane):
        rows[x, pl.ds(f * Y0 + HY0, 16), :] = plane
        ylo[x, pl.ds(f * HY0, HY0), :] = plane[0:HY0]
        yhi[x, pl.ds(f * HY0, HY0), :] = plane[16 - HY0 : 16]

    def edge(x, carry):
        for f in range(5):
            put(x, f, xlo[f, x])
            put(x + HX0 + 16, f, xhi[f, x])
        return carry

    def own(x, carry):
        for f in range(4):
            put(x + HX0, f, source[f, x])
        put(x + HX0, 4, visc[x])
        return carry

    lax.fori_loop(0, HX0, edge, 0)
    lax.fori_loop(0, 16, own, 0)


def turn_kernel(rows, ylo, yhi, turned, zlo, zhi, stage):
    stage[...] = jnp.zeros_like(stage)

    def body(x, carry):
        stage[pl.ds(0, 5 * Y0), :] = rows[x, pl.ds(0, 5 * Y0), :]
        for f in range(5):
            stage[pl.ds(f * Y0, HY0), :] = ylo[x, pl.ds(f * HY0, HY0), :]
            stage[pl.ds(f * Y0 + HY0 + 16, HY0), :] = yhi[x, pl.ds(f * HY0, HY0), :]
        t = stage[...].T
        turned[x] = t
        zlo[x] = t[0:HZ0]
        zhi[x] = t[128 - HZ0 : 128]
        return carry

    lax.fori_loop(0, 16 + 2 * HX0, body, 0)


def down0_kernel(turned, zlo, zhi, qb, qc, out, ylo, yhi, w_kept, beta_kept, root_kept, beta, w, root, rsum, csum, rz, cz, stage):
    planes = 16 + 2 * HX0
    depth = 128 + 2 * HZ0
    beta[:, pl.ds(0, 8), :] = jnp.zeros((planes, 8, LANES), F32)
    beta[:, pl.ds(8 + depth, 8), :] = jnp.zeros((planes, 8, LANES), F32)
    w[:, pl.ds(0, 8), :] = jnp.zeros((planes, 8, LANES), F32)
    w[:, pl.ds(8 + depth, 8), :] = jnp.zeros((planes, 8, LANES), F32)

    def prepare(x, t, row, n):
        lane = lane_of(n)
        v = jnp.zeros_like(t)
        for f in range(4):
            v = jnp.where((lane >= f * Y0) & (lane < (f + 1) * Y0), lane_roll(t, f * Y0 - 4 * Y0), v)
        root_v, inv_v = roots_of(v)
        pressure = lane >= 3 * Y0
        root_x = jnp.where(pressure, inv_v, root_v)
        inv_x = jnp.where(pressure, root_v, inv_v)
        root[x, pl.ds(row, n), :] = root_x
        beta[x, pl.ds(8 + row, n), :] = TAU * t * inv_x

    def setup(x, carry):
        prepare(x, zlo[x], 0, HZ0)
        for r, n in chunks(128, 32):
            prepare(x, turned[x, pl.ds(r, n), :], HZ0 + r, n)
        prepare(x, zhi[x], HZ0 + 128, HZ0)
        return carry

    lax.fori_loop(0, planes, setup, 0)

    def smooth(x, carry):
        for r, n in chunks(depth, 32):
            mid, total = around(beta, x, 8 + r, n)
            w[x, pl.ds(8 + r, n), :] = jnp.where(root[x, pl.ds(r, n), :] > 0.0, 1.2 * mid + TAU * total, 0.0)
        return carry

    lax.fori_loop(1, planes - 1, smooth, 0)

    def restrict(k, carry):
        for r, n in chunks(depth, 32):
            res = jnp.zeros((n, LANES), F32)
            coef = jnp.zeros((n, LANES), F32)
            for i in range(2):
                x = 2 + 2 * k + i
                mid, total = around(w, x, 8 + r, n)
                root_x = root[x, pl.ds(r, n), :]
                res = res + root_x * ((1.0 / TAU) * beta[x, pl.ds(8 + r, n), :] - 6.0 * mid + total)
                coef = coef + root_x * root_x
            rsum[pl.ds(r, n), :] = res
            csum[pl.ds(r, n), :] = coef
        half = depth // 2
        rz[k] = rsum[pl.ds(0, half, stride=2), :] + rsum[pl.ds(1, half, stride=2), :]
        cz[k] = csum[pl.ds(0, half, stride=2), :] + csum[pl.ds(1, half, stride=2), :]
        return carry

    lax.fori_loop(0, 16, restrict, 0)
    stage[...] = jnp.zeros_like(stage)

    def coarse(k, carry):
        stage[pl.ds(0, depth // 2), :] = mm(rz[k], qb[...]) + mm(cz[k], qc[...])
        t = stage[...].T
        out[k] = t[0:48]
        for a in range(6):
            ylo[k, pl.ds(a * 4, 4), :] = t[a * 8 : a * 8 + 4]
            yhi[k, pl.ds(a * 4, 4), :] = t[a * 8 + 4 : a * 8 + 8]
        return carry

    lax.fori_loop(0, 16, coarse, 0)

    def keep(x, carry):
        w_kept[x] = w[x + 8, pl.ds(16, 144), :]
        beta_kept[x] = beta[x + 8, pl.ds(16, 144), :]
        root_kept[x] = root[x + 8, pl.ds(8, 144), :]
        return carry

    lax.fori_loop(0, 20, keep, 0)


def down1_kernel(own, ylo, yhi, qb, qc, block, w, beta, root, stage, rz, cz, rsum, csum):
    beta[...] = jnp.zeros_like(beta)
    w[...] = jnp.zeros_like(w)
    stage[...] = jnp.zeros_like(stage)

    def setup(x, carry):
        for a in range(6):
            stage[pl.ds(a * Y1 + 4, 8), :] = own[x, pl.ds(a * 8, 8), :]
            stage[pl.ds(a * Y1, 4), :] = ylo[x, pl.ds(a * 4, 4), :]
            stage[pl.ds(a * Y1 + 12, 4), :] = yhi[x, pl.ds(a * 4, 4), :]
        t = stage[...].T[0:80]
        lane = lane_of(80)
        c = jnp.where(lane < Y1, lane_roll(t, 64), jnp.where(lane < 2 * Y1, lane_roll(t, 80), lane_roll(t, 96)))
        c = jnp.where(lane < 4 * Y1, c, 0.0)
        root_x, inv_x = roots_of(c)
        root[x] = root_x
        beta[x, pl.ds(8, 80), :] = TAU * t * inv_x
        return carry

    lax.fori_loop(0, 16, setup, 0)

    def smooth(x, carry):
        for r, n in chunks(80, 40):
            mid, total = around(beta, x, 8 + r, n)
            w[x, pl.ds(8 + r, n), :] = jnp.where(root[x, pl.ds(r, n), :] > 0.0, 1.2 * mid + TAU * total, 0.0)
        return carry

    lax.fori_loop(1, 15, smooth, 0)
    for k in range(4):
        for r, n in chunks(64, 32):
            res = jnp.zeros((n, LANES), F32)
            coef = jnp.zeros((n, LANES), F32)
            for i in range(2):
                x = 4 + 2 * k + i
                mid, total = around(w, x, 16 + r, n)
                root_x = root[x, pl.ds(8 + r, n), :]
                res = res + root_x * ((1.0 / TAU) * beta[x, pl.ds(16 + r, n), :] - 6.0 * mid + total)
                coef = coef + root_x * root_x
            rsum[pl.ds(r, n), :] = res
            csum[pl.ds(r, n), :] = coef
        rz[pl.ds(k * 32, 32), :] = rsum[pl.ds(0, 32, stride=2), :] + rsum[pl.ds(1, 32, stride=2), :]
        cz[pl.ds(k * 32, 32), :] = csum[pl.ds(0, 32, stride=2), :] + csum[pl.ds(1, 32, stride=2), :]
    block[...] = (mm(rz[...], qb[...]) + mm(cz[...], qc[...])).T[0:24]


def plane_kernel(gx, gy, got, b, c, zlo, zhi, stage_b, stage_c):
    width = 4 * gy
    stage_b[...] = jnp.zeros_like(stage_b)
    stage_c[...] = jnp.zeros_like(stage_c)
    lane = lane_of(LANES)

    def body(i, carry):
        for j in range(gy):
            for a in range(4):
                stage_b[pl.ds(a * width + 4 * j, 4), :] = got[i * gy + j, pl.ds(4 * a, 4), :]
            for a in range(2):
                stage_c[pl.ds(a * width + 4 * j, 4), :] = got[i * gy + j, pl.ds(16 + 4 * a, 4), :]
        tb = stage_b[...].T
        tc = stage_c[...].T
        c_all = jnp.where(lane < width, tc, jnp.where(lane < 2 * width, lane_roll(tc, width), lane_roll(tc, 2 * width)))
        c_all = jnp.where(lane < 4 * width, c_all, 0.0)
        for x in range(4):
            at = 4 * i + x
            b[at] = tb[x * 32 : (x + 1) * 32]
            c[at] = c_all[x * 32 : (x + 1) * 32]
            for which, t in ((0, tb), (1, c_all)):
                zlo[which, at] = t[x * 32 : x * 32 + HZ2]
                zhi[which, at] = t[(x + 1) * 32 - HZ2 : (x + 1) * 32]
        return carry

    lax.fori_loop(0, gx, body, 0)


def down2_kernel(gx, gy, b, c, zlo, zhi, qb, qc, out, zup, zdown, w, beta, root, plane_b, plane_c, rsum, csum, rz, cz):
    size_x, width = 4 * gx, 4 * gy
    beta[...] = jnp.zeros_like(beta)
    w[...] = jnp.zeros_like(w)
    plane_b[...] = jnp.zeros_like(plane_b)
    plane_c[...] = jnp.zeros_like(plane_c)

    def setup(x, carry):
        for which, plane, own in ((0, plane_b, b), (1, plane_c, c)):
            plane[pl.ds(16 - HZ2, HZ2), :] = zlo[which, x]
            plane[pl.ds(16, 32), :] = own[x]
            plane[pl.ds(48, HZ2), :] = zhi[which, x]
        root_x, inv_x = roots_of(plane_c[...])
        root[x] = root_x
        beta[x + 1, pl.ds(8, 64), :] = TAU * plane_b[...] * inv_x
        return carry

    lax.fori_loop(0, size_x, setup, 0)

    def smooth(x, carry):
        for r, n in chunks(64, 32):
            mid, total = around_whole(beta, x + 1, 8 + r, n, width)
            w[x + 1, pl.ds(8 + r, n), :] = jnp.where(root[x, pl.ds(r, n), :] > 0.0, 1.2 * mid + TAU * total, 0.0)
        return carry

    lax.fori_loop(0, size_x, smooth, 0)
    restrict_whole(size_x, width, w, beta, root, rsum, csum, rz, cz)

    def coarse(k, carry):
        t = mm(rz[k], qb[...]) + mm(cz[k], qc[...])
        out[k] = t
        zup[k] = t[24 - HZ3 : 24]
        zdown[k] = t[8 : 8 + HZ3]
        return carry

    lax.fori_loop(0, size_x // 2, coarse, 0)


def restrict_whole(size_x, width, w, beta, root, rsum, csum, rz, cz):
    def body(k, carry):
        for r, n in chunks(64, 32):
            res = jnp.zeros((n, LANES), F32)
            coef = jnp.zeros((n, LANES), F32)
            for i in range(2):
                x = 2 * k + i
                mid, total = around_whole(w, x + 1, 8 + r, n, width)
                root_x = root[x, pl.ds(r, n), :]
                res = res + root_x * ((1.0 / TAU) * beta[x + 1, pl.ds(8 + r, n), :] - 6.0 * mid + total)
                coef = coef + root_x * root_x
            rsum[pl.ds(r, n), :] = res
            csum[pl.ds(r, n), :] = coef
        rz[k] = rsum[pl.ds(0, 32, stride=2), :] + rsum[pl.ds(1, 32, stride=2), :]
        cz[k] = csum[pl.ds(0, 32, stride=2), :] + csum[pl.ds(1, 32, stride=2), :]
        return carry

    lax.fori_loop(0, size_x // 2, body, 0)


def relax_whole(size_x, depth, width, src, dst, beta, root):
    def body(x, carry):
        for r, n in chunks(depth, 32):
            mid, total = around_whole(src, x + 1, 8 + r, n, width)
            live = root[x, pl.ds(r, n), :] > 0.0
            dst[x + 1, pl.ds(8 + r, n), :] = jacobi(live, mid, beta[x + 1, pl.ds(8 + r, n), :], total)
        return carry

    lax.fori_loop(0, size_x, body, 0)


def coarse_kernel(gx, gy, own, zlo, zhi, w2, beta2, root2, q3b, q3c, u4, u3, e2, beta3, w3, v3, root3, beta4, w4, v4, root4, plane, fine, rsum, csum, rz, cz, v2, w2b):
    size_x, width = 2 * gx, 2 * gy
    for ref in (beta3, w3, v3, beta4, w4, v4, plane, v2, w2b):
        ref[...] = jnp.zeros_like(ref)

    def setup(x, carry):
        plane[pl.ds(24 - HZ3, HZ3), :] = zlo[x]
        plane[pl.ds(24, 16), :] = own[x, pl.ds(8, 16), :]
        plane[pl.ds(40, HZ3), :] = zhi[x]
        t = plane[...]
        root_x, inv_x = roots_of(jnp.where(lane_of(64) < 4 * width, lane_roll(t, 64), 0.0))
        root3[x] = root_x
        beta3[x + 1, pl.ds(8, 64), :] = TAU * t * inv_x
        return carry

    lax.fori_loop(0, size_x, setup, 0)

    def smooth(x, carry):
        for r, n in chunks(64, 32):
            mid, total = around_whole(beta3, x + 1, 8 + r, n, width)
            w3[x + 1, pl.ds(8 + r, n), :] = jnp.where(root3[x, pl.ds(r, n), :] > 0.0, 1.2 * mid + TAU * total, 0.0)
        return carry

    lax.fori_loop(0, size_x, smooth, 0)
    restrict_whole(size_x, width, w3, beta3, root3, rsum, csum, rz, cz)

    def start4(x, carry):
        t = mm(rz[x], q3b[...]) + mm(cz[x], q3c[...])
        root_x, inv_x = roots_of(jnp.where(lane_of(32) < 4 * gy, lane_roll(t, 64), 0.0))
        root4[x] = root_x
        beta4[x + 1, pl.ds(8, 32), :] = TAU * t * inv_x
        w4[x + 1, pl.ds(8, 32), :] = TAU * t * inv_x
        return carry

    lax.fori_loop(0, gx, start4, 0)
    here, there = w4, v4
    for step in range(COARSE_ITERS - 1):
        relax_whole(gx, 32, gy, here, there, beta4, root4)
        here, there = there, here

    def up3(x, carry):
        e = mm(here[x + 1, pl.ds(8, 32), :] * inverse(root4[x]), u4[...])
        fine[pl.ds(0, 32, stride=2), :] = e
        fine[pl.ds(1, 32, stride=2), :] = e
        for i in range(2):
            at = 2 * x + i
            w3[at + 1, pl.ds(8, 64), :] = w3[at + 1, pl.ds(8, 64), :] + root3[at] * fine[...]
        return carry

    lax.fori_loop(0, gx, up3, 0)
    relax_whole(size_x, 64, width, w3, v3, beta3, root3)
    relax_whole(size_x, 64, width, v3, w3, beta3, root3)

    def up2(x, carry):
        e = mm(w3[x + 1, pl.ds(24, 32), :] * inverse(root3[x, pl.ds(16, 32), :]), u3[...])
        fine[pl.ds(0, 32, stride=2), :] = e
        fine[pl.ds(1, 32, stride=2), :] = e
        for i in range(2):
            at = 2 * x + i
            w2b[at + 1, pl.ds(8, 64), :] = w2[at + 1, pl.ds(8, 64), :] + root2[at] * fine[...]
        return carry

    lax.fori_loop(0, size_x, up2, 0)
    relax_whole(2 * size_x, 64, 2 * width, w2b, v2, beta2, root2)
    relax_whole(2 * size_x, 64, 2 * width, v2, w2b, beta2, root2)
    e2[pl.ds(0, 2), :, :] = jnp.zeros((2, 40, LANES), F32)
    e2[pl.ds(2 * size_x + 2, 2), :, :] = jnp.zeros((2, 40, LANES), F32)

    def finish(x, carry):
        e2[x + 2] = w2b[x + 1, pl.ds(20, 40), :] * inverse(root2[x, pl.ds(12, 40), :])
        return carry

    lax.fori_loop(0, 2 * size_x, finish, 0)


def up_kernel(place, e2, w1, beta1, root1, w0, beta0, root0, u2, u1, out, w1b, v1, w0b, v0, fine1, fine0):
    for ref in (w1b, v1, w0b, v0):
        ref[...] = jnp.zeros_like(ref)
    first = 4 * place[0]

    def up1(k, carry):
        e = mm(e2[first + k], u2[...])
        fine1[pl.ds(0, 40, stride=2), :] = e
        fine1[pl.ds(1, 40, stride=2), :] = e
        for i in range(2):
            x = 2 * k + i
            w1b[x, pl.ds(8, 80), :] = w1[x, pl.ds(8, 80), :] + root1[x] * fine1[...]
        return carry

    lax.fori_loop(0, 8, up1, 0)

    def relax1(src, dst, begin, end):
        def body(x, carry):
            for r, n in chunks(80, 40):
                mid, total = around(src, x, 8 + r, n)
                live = root1[x, pl.ds(r, n), :] > 0.0
                dst[x, pl.ds(8 + r, n), :] = jacobi(live, mid, beta1[x, pl.ds(8 + r, n), :], total)
            return carry

        lax.fori_loop(begin, end, body, 0)

    relax1(w1b, v1, 2, 14)
    relax1(v1, w1b, 3, 13)

    def up0(k, carry):
        x1 = k + 3
        e = mm(w1b[x1, pl.ds(12, 72), :] * inverse(root1[x1, pl.ds(4, 72), :]), u1[...])
        fine0[pl.ds(0, 72, stride=2), :] = e
        fine0[pl.ds(1, 72, stride=2), :] = e
        for i in range(2):
            x = 2 * k + i
            for r, n in chunks(144, 48):
                w0b[x, pl.ds(8 + r, n), :] = w0[x, pl.ds(r, n), :] + root0[x, pl.ds(r, n), :] * fine0[pl.ds(r, n), :]
        return carry

    lax.fori_loop(0, 10, up0, 0)

    def first0(x, carry):
        for r, n in chunks(144, 24):
            mid, total = around(w0b, x, 8 + r, n)
            live = root0[x, pl.ds(r, n), :] > 0.0
            v0[x, pl.ds(8 + r, n), :] = jacobi(live, mid, beta0[x, pl.ds(r, n), :], total)
        return carry

    lax.fori_loop(1, 19, first0, 0)

    def last0(k, carry):
        x = k + 2
        for r, n in chunks(128, 32):
            mid, total = around(v0, x, 16 + r, n)
            root_x = root0[x, pl.ds(8 + r, n), :]
            fine0[pl.ds(r, n), :] = jacobi(root_x > 0.0, mid, beta0[x, pl.ds(8 + r, n), :], total) * inverse(root_x)
        t = fine0[pl.ds(0, 128), :].T
        for f in range(4):
            out[f, k] = t[f * Y0 + HY0 : f * Y0 + HY0 + 16]
        return carry

    lax.fori_loop(0, 16, last0, 0)


def call(kernel, args, outs, scratch, smem=0):
    vmem = pl.BlockSpec(memory_space=pltpu.VMEM)
    scalar = pl.BlockSpec(memory_space=pltpu.SMEM)
    return pl.pallas_call(
        kernel,
        out_shape=[jax.ShapeDtypeStruct(s, F32) for s in outs],
        in_specs=[scalar] * smem + [vmem] * (len(args) - smem),
        out_specs=[vmem] * len(outs),
        scratch_shapes=[pltpu.VMEM(s, F32) for s in scratch],
        compiler_params=pltpu.CompilerParams(vmem_limit_bytes=60 * 1024 * 1024),
    )(*args)


def swap(to_up, to_down, axis):
    n = lax.axis_size(axis)
    from_below = lax.ppermute(to_up, axis, [(i, i + 1) for i in range(n - 1)])
    from_above = lax.ppermute(to_down, axis, [(i + 1, i) for i in range(n - 1)])
    return from_below, from_above


def shards(source, material_ids, material_table, roughness):
    gx, gy = lax.axis_size("gx"), lax.axis_size("gy")
    choices_of = jnp.arange(material_table.shape[0], dtype=jnp.int32)
    matches = (material_ids[..., None] == choices_of).astype(F32)
    block_visc = jnp.sum(matches * material_table, axis=-1)
    along_z = jnp.repeat(block_visc, 8, axis=2)
    visc = (jnp.broadcast_to(along_z[:, None, :, None, :], (2, 8, 2, 8, 128)).reshape(16, 16, 128)) * roughness

    low = jnp.concatenate([source[:, :HX0], visc[None, :HX0]], axis=0)
    high = jnp.concatenate([source[:, 16 - HX0 :], visc[None, 16 - HX0 :]], axis=0)
    xlo, xhi = swap(high, low, "gx")
    planes = 16 + 2 * HX0
    rows, ysend_lo, ysend_hi = call(
        rows_kernel, (xlo, source, visc, xhi), [(planes, 112, LANES), (planes, 16, LANES), (planes, 16, LANES)], []
    )
    ylo, yhi = swap(ysend_hi, ysend_lo, "gy")
    turned, zsend_lo, zsend_hi = call(
        turn_kernel,
        (rows, ylo, yhi),
        [(planes, 128, LANES), (planes, HZ0, LANES), (planes, HZ0, LANES)],
        [(LANES, LANES)],
    )
    zlo, zhi = swap(zsend_hi, zsend_lo, "gz")

    q0b = pair_lanes(Y0, HY0, (0, 1, 2, 3), 8, 0, 0.5)
    q0c = pair_lanes(Y0, HY0, (0, 3), 8, 32, 0.125)
    depth = 128 + 2 * HZ0
    own1, ysend_lo, ysend_hi, w0, beta0, root0 = call(
        down0_kernel,
        (turned, zlo, zhi, q0b, q0c),
        [(16, 48, LANES), (16, 24, LANES), (16, 24, LANES)] + [(20, 144, LANES)] * 3,
        [(planes, depth + 16, LANES)] * 2
        + [(planes, depth, LANES)]
        + [(depth, LANES)] * 2
        + [(16, depth // 2, LANES)] * 2
        + [(LANES, LANES)],
    )
    ylo, yhi = swap(ysend_hi, ysend_lo, "gy")

    q1b = pair_lanes(Y1, 4, (0, 1, 2, 3), 4, 0, 0.5)
    q1c = pair_lanes(Y1, 4, (0, 3), 4, 16, 0.125)
    block, w1, beta1, root1 = call(
        down1_kernel,
        (own1, ylo, yhi, q1b, q1c),
        [(24, LANES), (16, 96, LANES), (16, 96, LANES), (16, 80, LANES)],
        [(LANES, LANES)] * 3 + [(64, LANES)] * 2,
    )
    spread = jnp.broadcast_to(block[None], (gx * gy, 24, LANES))
    got = lax.all_to_all(spread, ("gx", "gy"), 0, 0, tiled=True)

    x2, x3 = 4 * gx, 2 * gx
    b2, c2, zsend_lo, zsend_hi = call(
        functools.partial(plane_kernel, gx, gy),
        (got,),
        [(x2, 32, LANES)] * 2 + [(2, x2, HZ2, LANES)] * 2,
        [(LANES, LANES)] * 2,
    )
    zlo, zhi = swap(zsend_hi, zsend_lo, "gz")

    q2b = pair_lanes(4 * gy, 0, (0, 1, 2, 3), 2 * gy, 0, 0.5)
    q2c = pair_lanes(4 * gy, 0, (0, 1, 2, 3), 2 * gy, 64, 0.125)
    own3, zsend_up, zsend_down, w2, beta2, root2 = call(
        functools.partial(down2_kernel, gx, gy),
        (b2, c2, zlo, zhi, q2b, q2c),
        [(x3, 32, LANES)] + [(x3, HZ3, LANES)] * 2 + [(x2 + 2, 80, LANES)] * 2 + [(x2, 64, LANES)],
        [(64, LANES)] * 4 + [(x3, 32, LANES)] * 2,
    )
    zlo, zhi = swap(zsend_up, zsend_down, "gz")

    q3b = pair_lanes(2 * gy, 0, (0, 1, 2, 3), gy, 0, 0.5)
    q3c = pair_lanes(2 * gy, 0, (0, 1, 2, 3), gy, 64, 0.125)
    u4 = repeat_lanes(gy, 0, 2 * gy, 0)
    u3 = repeat_lanes(2 * gy, 0, 4 * gy, 0)
    (e2,) = call(
        functools.partial(coarse_kernel, gx, gy),
        (own3, zlo, zhi, w2, beta2, root2, q3b, q3c, u4, u3),
        [(x2 + 4, 40, LANES)],
        [(x3 + 2, 80, LANES)] * 3
        + [(x3, 64, LANES)]
        + [(gx + 2, 48, LANES)] * 3
        + [(gx, 32, LANES)]
        + [(64, LANES)] * 4
        + [(gx, 32, LANES)] * 2
        + [(x2 + 2, 80, LANES)] * 2,
    )

    width = 4 * gy
    source_lane = lax.broadcasted_iota(jnp.int32, (LANES, LANES), 0)
    target_lane = lax.broadcasted_iota(jnp.int32, (LANES, LANES), 1)
    wanted_y = 4 * lax.axis_index("gy") - 2 + (target_lane % Y1) // 2
    wanted = (target_lane // Y1) * width + wanted_y
    valid = (wanted_y >= 0) & (wanted_y < width) & (target_lane < 4 * Y1)
    u2 = ((source_lane == wanted) & valid).astype(F32)
    u1 = repeat_lanes(Y1, 4, Y0, HY0)
    place = lax.axis_index("gx").astype(jnp.int32).reshape(1)
    (correction,) = call(
        up_kernel,
        (place, e2, w1, beta1, root1, w0, beta0, root0, u2, u1),
        [(4, 16, 16, LANES)],
        [(16, 96, LANES)] * 2 + [(20, 160, LANES)] * 2 + [(80, LANES), (144, LANES)],
        smem=1,
    )
    return correction


def solution(mesh):
    return jax.shard_map(
        shards,
        mesh=mesh,
        in_specs=(P(None, "gx", "gy", "gz"), P("gx", "gy", "gz"), P(), P("gx", "gy", "gz")),
        out_specs=P(None, "gx", "gy", "gz"),
        check_vma=False,
    )
```

```python
import functools

import jax
import jax.numpy as jnp
import numpy as np
from jax import lax
from jax.experimental import pallas as pl
from jax.experimental.pallas import tpu as pltpu
from jax.sharding import PartitionSpec as P

F32 = jnp.float32
COARSE_ITERS = 8
TAU = 0.8 / 6.0
LANES = 128
HX0, HY0, HZ0 = 3, 3, 16
Y0 = 16 + 2 * HY0
Y1 = 16
HZ2 = 10
HZ3 = 20
OFF2, OFF3 = 4, 2


def halves(a):
    high = a.astype(jnp.bfloat16)
    return [high, (a - high.astype(F32)).astype(jnp.bfloat16)]


def mm(pairs):
    left, right = [], []
    for a, m in pairs:
        left += halves(a)
        right += [m, m]
    return jnp.dot(jnp.concatenate(left, axis=1), jnp.concatenate(right, axis=0), preferred_element_type=F32)


def lane_of(n):
    return lax.broadcasted_iota(jnp.int32, (n, LANES), 1)


def lane_roll(x, shift):
    return pltpu.roll(x, shift % LANES, 1) if shift % LANES else x


def around(ref, x, row, n):
    mid = ref[x, pl.ds(row, n), :]
    total = ref[x - 1, pl.ds(row, n), :] + ref[x + 1, pl.ds(row, n), :]
    total = total + (ref[x, pl.ds(row - 1, n), :] + ref[x, pl.ds(row + 1, n), :])
    return mid, total + (lane_roll(mid, 1) + lane_roll(mid, -1))


def around_whole(ref, x, row, n, width):
    mid = ref[x, pl.ds(row, n), :]
    total = ref[x - 1, pl.ds(row, n), :] + ref[x + 1, pl.ds(row, n), :]
    total = total + (ref[x, pl.ds(row - 1, n), :] + ref[x, pl.ds(row + 1, n), :])
    place = lane_of(n) & (width - 1)
    total = total + jnp.where(place == 0, 0.0, lane_roll(mid, 1))
    return mid, total + jnp.where(place == width - 1, 0.0, lane_roll(mid, -1))


def chunks(n, size):
    return [(r, min(size, n - r)) for r in range(0, n, size)]


def roots_of(c):
    live = c > 0.0
    inv = lax.rsqrt(jnp.where(live, c, 1.0))
    return jnp.where(live, c * inv, 0.0), jnp.where(live, inv, 0.0)


def inverse(root):
    live = root > 0.0
    return jnp.where(live, 1.0 / jnp.where(live, root, 1.0), 0.0)


def jacobi(live, mid, beta, total):
    return jnp.where(live, 0.2 * mid + beta + TAU * total, 0.0)


def pair_lanes(width, start, fields, out_width, out_start, scale):
    m = np.zeros((LANES, LANES), jnp.bfloat16)
    for k, f in enumerate(fields):
        for j in range(out_width):
            for i in range(2):
                m[f * width + start + 2 * j + i, out_start + k * out_width + j] = scale
    return m


def repeat_lanes(width, shift, out_width, out_shift):
    m = np.zeros((LANES, LANES), jnp.bfloat16)
    for f in range(4):
        for j in range(out_width):
            i = shift + (j - out_shift) // 2
            if 0 <= i < width:
                m[f * width + i, f * out_width + j] = 1.0
    return m


def residual(w, beta, root, x, row, n, mid_total):
    mid, total = mid_total
    root_x = root[x, pl.ds(row - 8, n), :]
    return root_x * ((1.0 / TAU) * beta[x, pl.ds(row, n), :] - 6.0 * mid + total), root_x * root_x


def loop(begin, end, body, unroll=1):
    def step(i, carry):
        body(i)
        return carry

    lax.fori_loop(begin, end, step, 0, unroll=unroll)


def fold_rows(ref, k, n):
    return ref[k, pl.ds(0, n, stride=2), :] + ref[k, pl.ds(1, n, stride=2), :]


def unfold_rows(ref, k, n, value):
    ref[k, pl.ds(0, n, stride=2), :] = value
    ref[k, pl.ds(1, n, stride=2), :] = value


def prepare_kernel(table, ids, spread, source, roughness, visc, low, high):
    blocks = jnp.concatenate([ids[0], ids[1]], axis=0)
    found = jnp.zeros(blocks.shape, F32)
    for k in range(table.shape[0]):
        found = found + jnp.where(blocks == k, table[k], 0.0)
    along_z = jnp.dot(found, spread[...], precision=lax.Precision.HIGHEST, preferred_element_type=F32)
    for x in range(16):
        for j in range(2):
            row = 2 * (x // 8) + j
            visc[x, pl.ds(8 * j, 8), :] = roughness[x, pl.ds(8 * j, 8), :] * along_z[row : row + 1]
    for x in range(HX0):
        for f in range(4):
            low[f, x] = source[f, x]
            high[f, x] = source[f, 16 - HX0 + x]
        low[4, x] = visc[x]
        high[4, x] = visc[16 - HX0 + x]


def edge_kernel(xlo, source, visc, xhi, ylo, yhi):
    def put(x, f, plane):
        ylo[x, pl.ds(f * HY0, HY0), :] = plane[0:HY0]
        yhi[x, pl.ds(f * HY0, HY0), :] = plane[16 - HY0 : 16]

    for x in range(HX0):
        for f in range(5):
            put(x, f, xlo[f, x])
            put(x + HX0 + 16, f, xhi[f, x])

    def own(x):
        for f in range(4):
            put(x + HX0, f, source[f, x])
        put(x + HX0, 4, visc[x])

    loop(0, 16, own, 16)


def turn_kernel(xlo, source, visc, xhi, ylo, yhi, turned, zlo, zhi, stage):
    stage[...] = jnp.zeros_like(stage)

    def turn(x, slot, planes):
        for f in range(5):
            stage[slot, pl.ds(f * Y0 + HY0, 16), :] = planes[f]
            stage[slot, pl.ds(f * Y0, HY0), :] = ylo[x, pl.ds(f * HY0, HY0), :]
            stage[slot, pl.ds(f * Y0 + HY0 + 16, HY0), :] = yhi[x, pl.ds(f * HY0, HY0), :]
        t = stage[slot].T
        turned[x] = t
        zlo[x] = t[0:HZ0]
        zhi[x] = t[128 - HZ0 : 128]

    for x in range(HX0):
        turn(x, 0, [xlo[f, x] for f in range(5)])
        turn(x + HX0 + 16, 1, [xhi[f, x] for f in range(5)])

    def own(k):
        for slot in range(4):
            x = 4 * k + slot
            turn(x + HX0, slot, [source[f, x] for f in range(4)] + [visc[x]])

    loop(0, 4, own, 2)


def down0_kernel(turned, zlo, zhi, qb, qc, out, ylo, yhi, w, beta, root, rsum, csum, rz, cz, stage):
    planes = 16 + 2 * HX0
    depth = 128 + 2 * HZ0
    half = depth // 2

    def prepare(x, t, row, n):
        lane = lane_of(n)
        v = lane_roll(jnp.where(lane < 4 * Y0, 0.0, t), -4 * Y0)
        v = v + lane_roll(v, Y0)
        v = v + lane_roll(v, 2 * Y0)
        root_v, inv_v = roots_of(v)
        pressure = lane >= 3 * Y0
        root[x, pl.ds(row, n), :] = jnp.where(pressure, inv_v, root_v)
        beta[x, pl.ds(8 + row, n), :] = TAU * t * jnp.where(pressure, root_v, inv_v)

    def setup(x):
        for ref in (beta, w):
            ref[x, pl.ds(0, 8), :] = jnp.zeros((8, LANES), F32)
            ref[x, pl.ds(8 + depth, 8), :] = jnp.zeros((8, LANES), F32)
        prepare(x, zlo[x], 0, HZ0)
        for r, n in chunks(128, 32):
            prepare(x, turned[x, pl.ds(r, n), :], HZ0 + r, n)
        prepare(x, zhi[x], HZ0 + 128, HZ0)

    loop(0, planes, setup, 2)

    def smooth(x):
        for r, n in chunks(depth, 32):
            mid, total = around(beta, x, 8 + r, n)
            w[x, pl.ds(8 + r, n), :] = jnp.where(root[x, pl.ds(r, n), :] > 0.0, 1.2 * mid + TAU * total, 0.0)

    loop(1, planes - 1, smooth, 10)

    def restrict(k):
        for r, n in chunks(depth, 32):
            x = HX0 + 2 * k
            res_a, coef_a = residual(w, beta, root, x, 8 + r, n, around(w, x, 8 + r, n))
            res_b, coef_b = residual(w, beta, root, x + 1, 8 + r, n, around(w, x + 1, 8 + r, n))
            rsum[k, pl.ds(r, n), :] = res_a + res_b
            csum[k, pl.ds(r, n), :] = coef_a + coef_b

    loop(0, 8, restrict, 4)

    def fold(k):
        rz[pl.ds(k * half, half), :] = fold_rows(rsum, k, half)
        cz[pl.ds(k * half, half), :] = fold_rows(csum, k, half)

    for k in range(8):
        fold(k)
    stage[...] = jnp.zeros_like(stage)
    for k in range(0, 8, 2):
        both = mm(((rz[pl.ds(k * half, 2 * half), :], qb[...]), (cz[pl.ds(k * half, 2 * half), :], qc[...])))
        for i in range(2):
            stage[k + i, pl.ds(0, half), :] = both[i * half : (i + 1) * half]
    for k in range(8):
        t = stage[k].T
        out[k] = t[0:48]
        for a in range(6):
            ylo[k, pl.ds(a * 4, 4), :] = t[a * 8 : a * 8 + 4]
            yhi[k, pl.ds(a * 4, 4), :] = t[a * 8 + 4 : a * 8 + 8]


def join_kernel(own, ylo, yhi, low, high):
    for ref, first in ((low, 0), (high, 4)):
        for x in range(4):
            ref[x, pl.ds(0, 48), :] = own[first + x]
            ref[x, pl.ds(48, 24), :] = ylo[first + x]
            ref[x, pl.ds(72, 24), :] = yhi[first + x]


def down1_kernel(own, ylo, yhi, xlo, xhi, qb, qc, block, w, beta, root, stage, rsum, csum, rz, cz):
    stage[...] = jnp.zeros_like(stage)

    def prepare(x, slot, mine, lo, hi):
        for a in range(6):
            stage[slot, pl.ds(a * Y1 + 4, 8), :] = mine(a * 8, 8)
            stage[slot, pl.ds(a * Y1, 4), :] = lo(a * 4, 4)
            stage[slot, pl.ds(a * Y1 + 12, 4), :] = hi(a * 4, 4)
        t = stage[slot].T[0:80]
        lane = lane_of(80)
        c = jnp.where(lane < Y1, lane_roll(t, 64), jnp.where(lane < 2 * Y1, lane_roll(t, 80), lane_roll(t, 96)))
        root_x, inv_x = roots_of(jnp.where(lane < 4 * Y1, c, 0.0))
        root[x] = root_x
        beta[x, pl.ds(8, 80), :] = TAU * t * inv_x
        for ref in (beta, w):
            ref[x, pl.ds(0, 8), :] = jnp.zeros((8, LANES), F32)
            ref[x, pl.ds(88, 8), :] = jnp.zeros((8, LANES), F32)

    for x in range(4):
        for slot, side in ((0, xlo), (1, xhi)):
            prepare(
                x + 12 * slot,
                2 * (x % 2) + slot,
                lambda r, n: side[x, pl.ds(r, n), :],
                lambda r, n: side[x, pl.ds(48 + r, n), :],
                lambda r, n: side[x, pl.ds(72 + r, n), :],
            )
    for x in range(8):
        prepare(
            x + 4,
            x % 4,
            lambda r, n: own[x, pl.ds(r, n), :],
            lambda r, n: ylo[x, pl.ds(r, n), :],
            lambda r, n: yhi[x, pl.ds(r, n), :],
        )

    def smooth(x):
        for r, n in chunks(80, 40):
            mid, total = around(beta, x, 8 + r, n)
            w[x, pl.ds(8 + r, n), :] = jnp.where(root[x, pl.ds(r, n), :] > 0.0, 1.2 * mid + TAU * total, 0.0)

    loop(1, 15, smooth, 14)
    for k in range(4):
        for r, n in chunks(64, 32):
            x = 4 + 2 * k
            res_a, coef_a = residual(w, beta, root, x, 16 + r, n, around(w, x, 16 + r, n))
            res_b, coef_b = residual(w, beta, root, x + 1, 16 + r, n, around(w, x + 1, 16 + r, n))
            rsum[k, pl.ds(r, n), :] = res_a + res_b
            csum[k, pl.ds(r, n), :] = coef_a + coef_b
    for k in range(4):
        rz[pl.ds(k * 32, 32), :] = fold_rows(rsum, k, 32)
        cz[pl.ds(k * 32, 32), :] = fold_rows(csum, k, 32)
    t = mm(((rz[...], qb[...]), (cz[...], qc[...]))).T[0:24]

    def copy(i):
        block[i] = t

    loop(0, block.shape[0], copy, 8 if block.shape[0] % 8 == 0 else 1)


def plane_kernel(gx, gy, got, b, c, zlo, zhi, stage_b, stage_c):
    width = 4 * gy
    stage_b[...] = jnp.zeros_like(stage_b)
    stage_c[...] = jnp.zeros_like(stage_c)

    def one(i, slot):
        for j in range(gy):
            for a in range(4):
                stage_b[slot, pl.ds(a * width + 4 * j, 4), :] = got[i * gy + j, pl.ds(4 * a, 4), :]
            for a in range(2):
                stage_c[slot, pl.ds(a * width + 4 * j, 4), :] = got[i * gy + j, pl.ds(16 + 4 * a, 4), :]
        tb = stage_b[slot].T
        tc = stage_c[slot].T
        for x in range(4):
            at = 4 * i + x
            b[at] = tb[x * 32 : (x + 1) * 32]
            c[at] = tc[x * 32 : (x + 1) * 32]
            for ref, first in ((zlo, x * 32), (zhi, (x + 1) * 32 - HZ2)):
                ref[at, pl.ds(0, HZ2), :] = tb[first : first + HZ2]
                ref[at, pl.ds(HZ2, 5), :] = jnp.where(
                    lane_of(5) < 64, tc[first : first + 5], lane_roll(tc[first + 5 : first + 10], 64)
                )
                ref[at, pl.ds(HZ2 + 5, 1), :] = jnp.zeros((1, LANES), F32)

    def body(k):
        one(2 * k, 0)
        one(2 * k + 1, 1)

    loop(0, gx // 2, body)


def down2_kernel(gx, gy, b, c, zlo, zhi, qb, qc, out, zup, zdown, w, beta, root, rsum, csum, rz, cz):
    size_x, width = 4 * gx, 4 * gy

    def prepare(x, row, t, tc):
        n = t.shape[0]
        lane = lane_of(n)
        c_all = jnp.where(lane < width, tc, jnp.where(lane < 2 * width, lane_roll(tc, width), lane_roll(tc, 2 * width)))
        root_x, inv_x = roots_of(jnp.where(lane < 4 * width, c_all, 0.0))
        root[x + OFF2, pl.ds(row, n), :] = root_x
        beta[x + OFF2, pl.ds(8 + row, n), :] = TAU * t * inv_x

    for x in list(range(OFF2)) + list(range(OFF2 + size_x, 2 * OFF2 + size_x)):
        for ref in (beta, w, root):
            ref[x] = jnp.zeros(ref.shape[1:], F32)

    def setup(x):
        for ref in (beta, w):
            ref[x + OFF2, pl.ds(0, 16), :] = jnp.zeros((16, LANES), F32)
            ref[x + OFF2, pl.ds(64, 16), :] = jnp.zeros((16, LANES), F32)
        root[x + OFF2, pl.ds(0, 8), :] = jnp.zeros((8, LANES), F32)
        root[x + OFF2, pl.ds(56, 8), :] = jnp.zeros((8, LANES), F32)
        prepare(x, 16, b[x], c[x])
        for ref, row in ((zlo, 16 - HZ2), (zhi, 48)):
            packed = ref[x, pl.ds(HZ2, 5), :]
            prepare(x, row, ref[x, pl.ds(0, 5), :], jnp.where(lane_of(5) < 64, packed, 0.0))
            prepare(x, row + 5, ref[x, pl.ds(5, 5), :], jnp.where(lane_of(5) < 64, lane_roll(packed, 64), 0.0))

    loop(0, size_x, setup, 8)

    def smooth(x):
        for r, n in chunks(64, 32):
            mid, total = around_whole(beta, x, 8 + r, n, width)
            w[x, pl.ds(8 + r, n), :] = jnp.where(root[x, pl.ds(r, n), :] > 0.0, 1.2 * mid + TAU * total, 0.0)

    loop(OFF2, size_x + OFF2, smooth, 8)
    restrict_whole(size_x, OFF2, width, w, beta, root, rsum, csum, rz, cz)
    for k in range(0, size_x // 2, 4):
        rows = pl.ds(k * 32, 128)
        t = mm(((rz[rows, :], qb[...]), (cz[rows, :], qc[...])))
        for i in range(4):
            out[k + i] = t[i * 32 : (i + 1) * 32]
            zup[k + i] = t[i * 32 + 24 - HZ3 : i * 32 + 24]
            zdown[k + i] = t[i * 32 + 8 : i * 32 + 8 + HZ3]


def restrict_whole(size_x, off, width, w, beta, root, rsum, csum, rz, cz):
    def body(k):
        for r, n in chunks(64, 32):
            x = 2 * k + off
            res_a, coef_a = residual(w, beta, root, x, 8 + r, n, around_whole(w, x, 8 + r, n, width))
            res_b, coef_b = residual(w, beta, root, x + 1, 8 + r, n, around_whole(w, x + 1, 8 + r, n, width))
            rsum[k, pl.ds(r, n), :] = res_a + res_b
            csum[k, pl.ds(r, n), :] = coef_a + coef_b

    loop(0, size_x // 2, body, 4 if size_x % 8 == 0 else 2)
    for k in range(size_x // 2):
        rz[pl.ds(k * 32, 32), :] = fold_rows(rsum, k, 32)
        cz[pl.ds(k * 32, 32), :] = fold_rows(csum, k, 32)


def relax_whole(first, planes, begin, depth, width, src, dst, beta, root, unroll, shift=0):
    def body(x):
        for r, n in chunks(depth, 32):
            r = r + begin
            mid, total = around_whole(src, x, 8 + r, n, width)
            live = root[x + shift, pl.ds(r, n), :] > 0.0
            dst[x, pl.ds(8 + r, n), :] = jacobi(live, mid, beta[x + shift, pl.ds(8 + r, n), :], total)

    loop(first, first + planes, body, unroll)


def coarse_kernel(gx, gy, place, own, zlo, zhi, w2, beta2, root2, q3b, q3c, u4, u3, e2, beta3, w3, v3, root3, beta4, w4, v4, root4, rsum, csum, rz, cz, v2, w2b, fine3, fine2):
    size_x, width = 2 * gx, 2 * gy
    for ref in (beta3, w3, v3, root3, beta4, w4, v4):
        ref[...] = jnp.zeros_like(ref)

    def prepare(x, row, t):
        n = t.shape[0]
        root_x, inv_x = roots_of(jnp.where(lane_of(n) < 4 * width, lane_roll(t, 64), 0.0))
        root3[x + OFF3, pl.ds(row, n), :] = root_x
        beta3[x + OFF3, pl.ds(8 + row, n), :] = TAU * t * inv_x

    def setup(x):
        prepare(x, 24 - HZ3, zlo[x])
        prepare(x, 24, own[x, pl.ds(8, 16), :])
        prepare(x, 40, zhi[x])

    loop(0, size_x, setup, 4)

    def smooth(x):
        for r, n in chunks(64, 32):
            mid, total = around_whole(beta3, x, 8 + r, n, width)
            w3[x, pl.ds(8 + r, n), :] = jnp.where(root3[x, pl.ds(r, n), :] > 0.0, 1.2 * mid + TAU * total, 0.0)

    loop(OFF3, size_x + OFF3, smooth, 4)
    restrict_whole(size_x, OFF3, width, w3, beta3, root3, rsum, csum, rz, cz)
    t = mm(((rz[...], q3b[...]), (cz[...], q3c[...])))
    for x in range(gx):
        t_x = t[x * 32 : (x + 1) * 32]
        root_x, inv_x = roots_of(jnp.where(lane_of(32) < 4 * gy, lane_roll(t_x, 64), 0.0))
        root4[x + 1] = root_x
        beta4[x + 1, pl.ds(8, 32), :] = TAU * t_x * inv_x
        w4[x + 1, pl.ds(8, 32), :] = TAU * t_x * inv_x
    here, there = w4, v4
    for step in range(COARSE_ITERS - 1):
        relax_whole(1, gx, 0, 32, gy, here, there, beta4, root4, gx)
        here, there = there, here

    e4 = [here[x + 1, pl.ds(16, 16), :] * inverse(root4[x + 1, pl.ds(8, 16), :]) for x in range(gx)]
    e4 = mm(((jnp.concatenate(e4, axis=0), u4[...]),))
    for x in range(gx):
        unfold_rows(fine3, x, 16, e4[x * 16 : (x + 1) * 16])
        for i in range(2):
            at = 2 * x + i + OFF3
            w3[at, pl.ds(24, 32), :] = w3[at, pl.ds(24, 32), :] + root3[at, pl.ds(16, 32), :] * fine3[x]
    relax_whole(OFF3, size_x, 16, 32, width, w3, v3, beta3, root3, 4)
    relax_whole(OFF3, size_x, 16, 32, width, v3, w3, beta3, root3, 4)

    first3 = 2 * place[0] - 2 + OFF3
    first2 = 4 * place[0] - 4 + OFF2
    e3 = [w3[first3 + k, pl.ds(28, 24), :] * inverse(root3[first3 + k, pl.ds(20, 24), :]) for k in range(6)]
    e3 = mm(((jnp.concatenate(e3, axis=0), u3[...]),))
    for k in range(6):
        unfold_rows(fine2, k, 24, e3[k * 24 : (k + 1) * 24])
    for p in range(12):
        add = root2[first2 + p, pl.ds(8, 48), :] * fine2[p // 2]
        w2b[p, pl.ds(16, 48), :] = w2[first2 + p, pl.ds(16, 48), :] + add
        for ref in (w2b, v2):
            ref[p, pl.ds(8, 8), :] = jnp.zeros((8, LANES), F32)
            ref[p, pl.ds(64, 8), :] = jnp.zeros((8, LANES), F32)
    relax_whole(1, 10, 8, 48, 2 * width, w2b, v2, beta2, root2, 10, first2)
    relax_whole(2, 8, 8, 48, 2 * width, v2, w2b, beta2, root2, 8, first2)
    for k in range(8):
        e2[k] = w2b[k + 2, pl.ds(20, 40), :] * inverse(root2[first2 + k + 2, pl.ds(12, 40), :])


def up_kernel(gy, place, e2, w1, beta1, root1, w0, beta0, root0, u1, out, w1b, v1, w0b, v0, fine1, fine0, turned):
    width = 4 * gy
    source_lane = lax.broadcasted_iota(jnp.int32, (LANES, LANES), 0)
    target_lane = lane_of(LANES)
    wanted_y = 4 * place[0] - 2 + ((target_lane & (Y1 - 1)) >> 1)
    wanted = (target_lane >> 4) * width + wanted_y
    valid = (source_lane == wanted) & (wanted_y >= 0) & (wanted_y < width) & (target_lane < 4 * Y1)
    u2 = jnp.where(valid, 1.0, 0.0).astype(jnp.bfloat16)
    for ref in (w1b, v1):
        for row in (0, 88):
            ref[:, pl.ds(row, 8), :] = jnp.zeros((16, 8, LANES), F32)
    for ref in (w0b, v0):
        for row in (0, 152):
            ref[:, pl.ds(row, 8), :] = jnp.zeros((20, 8, LANES), F32)
    for k in range(0, 8, 4):
        e = mm(((jnp.concatenate([e2[k + i] for i in range(4)], axis=0), u2),))
        for i in range(4):
            unfold_rows(fine1, k + i, 40, e[i * 40 : (i + 1) * 40])
    for x in range(1, 15):
        w1b[x, pl.ds(8, 80), :] = w1[x, pl.ds(8, 80), :] + root1[x] * fine1[x // 2]

    def relax1(src, dst, begin, end):
        def body(x):
            for r, n in chunks(80, 40):
                mid, total = around(src, x, 8 + r, n)
                live = root1[x, pl.ds(r, n), :] > 0.0
                dst[x, pl.ds(8 + r, n), :] = jacobi(live, mid, beta1[x, pl.ds(8 + r, n), :], total)

        loop(begin, end, body, end - begin)

    relax1(w1b, v1, 2, 14)
    relax1(v1, w1b, 3, 13)

    for k in range(0, 10, 2):
        e = [w1b[x, pl.ds(12, 72), :] * inverse(root1[x, pl.ds(4, 72), :]) for x in (k + 3, k + 4)]
        e = mm(((jnp.concatenate(e, axis=0), u1[...]),))
        for i in range(2):
            unfold_rows(fine0, k + i, 72, e[i * 72 : (i + 1) * 72])

    def up0(k):
        for i in range(2):
            x = 2 * k + i
            for r, n in chunks(144, 48):
                add = root0[x + 1, pl.ds(8 + r, n), :] * fine0[k, pl.ds(r, n), :]
                w0b[x, pl.ds(8 + r, n), :] = w0[x + 1, pl.ds(16 + r, n), :] + add

    loop(0, 10, up0, 10)

    def first0(x):
        for r, n in chunks(144, 24):
            mid, total = around(w0b, x, 8 + r, n)
            live = root0[x + 1, pl.ds(8 + r, n), :] > 0.0
            v0[x, pl.ds(8 + r, n), :] = jacobi(live, mid, beta0[x + 1, pl.ds(16 + r, n), :], total)

    loop(1, 19, first0, 9)

    def last0(j):
        for slot in range(4):
            k = 4 * j + slot
            x = k + 2
            for r, n in chunks(128, 32):
                mid, total = around(v0, x, 16 + r, n)
                root_x = root0[x + 1, pl.ds(16 + r, n), :]
                new = jacobi(root_x > 0.0, mid, beta0[x + 1, pl.ds(24 + r, n), :], total)
                turned[slot, pl.ds(r, n), :] = new * inverse(root_x)
        for slot in range(4):
            t = turned[slot].T
            for f in range(4):
                out[f, 4 * j + slot] = t[f * Y0 + HY0 : f * Y0 + HY0 + 16]

    loop(0, 4, last0)


def call(kernel, args, outs, scratch, smem=0):
    vmem = pl.BlockSpec(memory_space=pltpu.VMEM)
    scalar = pl.BlockSpec(memory_space=pltpu.SMEM)
    return pl.pallas_call(
        kernel,
        out_shape=[jax.ShapeDtypeStruct(s, F32) for s in outs],
        in_specs=[scalar] * smem + [vmem] * (len(args) - smem),
        out_specs=[vmem] * len(outs),
        scratch_shapes=[pltpu.VMEM(s, F32) for s in scratch],
        compiler_params=pltpu.CompilerParams(vmem_limit_bytes=16 * 1024 * 1024),
    )(*args)


def swap(to_up, to_down, axis):
    n = lax.axis_size(axis)
    from_below = lax.ppermute(to_up, axis, [(i, i + 1) for i in range(n - 1)])
    from_above = lax.ppermute(to_down, axis, [(i + 1, i) for i in range(n - 1)])
    return from_below, from_above


def whole_plane(block):
    return lax.all_to_all(block, ("gx", "gy"), 0, 0, tiled=True)


def position(axis):
    return lax.axis_index(axis).astype(jnp.int32)


def shards(gx, gy, source, material_ids, material_table, roughness):
    spread = np.repeat(np.eye(16, dtype=np.float32), 8, axis=1)
    visc, low, high = call(
        prepare_kernel,
        (material_table, material_ids, spread, source, roughness),
        [(16, 16, LANES)] + [(5, HX0, 16, LANES)] * 2,
        [],
        smem=1,
    )
    xlo, xhi = swap(high, low, "gx")
    planes = 16 + 2 * HX0
    ysend_lo, ysend_hi = call(edge_kernel, (xlo, source, visc, xhi), [(planes, 15, LANES)] * 2, [])
    ylo, yhi = swap(ysend_hi, ysend_lo, "gy")
    turned, zsend_lo, zsend_hi = call(
        turn_kernel,
        (xlo, source, visc, xhi, ylo, yhi),
        [(planes, 128, LANES)] + [(planes, HZ0, LANES)] * 2,
        [(4, LANES, LANES)],
    )
    zlo, zhi = swap(zsend_hi, zsend_lo, "gz")

    q0b = pair_lanes(Y0, HY0, (0, 1, 2, 3), 8, 0, 0.5)
    q0c = pair_lanes(Y0, HY0, (0, 3), 8, 32, 0.125)
    depth = 128 + 2 * HZ0
    own1, ysend_lo, ysend_hi, w0, beta0, root0 = call(
        down0_kernel,
        (turned, zlo, zhi, q0b, q0c),
        [(8, 48, LANES)] + [(8, 24, LANES)] * 2 + [(planes, depth + 16, LANES)] * 2 + [(planes, depth, LANES)],
        [(8, depth, LANES)] * 2 + [(4 * depth, LANES)] * 2 + [(8, LANES, LANES)],
    )
    ylo, yhi = swap(ysend_hi, ysend_lo, "gy")
    low, high = call(join_kernel, (own1, ylo, yhi), [(4, 96, LANES)] * 2, [])
    xlo, xhi = swap(high, low, "gx")

    q1b = pair_lanes(Y1, 4, (0, 1, 2, 3), 4, 0, 0.5)
    q1c = pair_lanes(Y1, 4, (0, 3), 4, 16, 0.125)
    block, w1, beta1, root1 = call(
        down1_kernel,
        (own1, ylo, yhi, xlo, xhi, q1b, q1c),
        [(gx * gy, 24, LANES), (16, 96, LANES), (16, 96, LANES), (16, 80, LANES)],
        [(4, LANES, LANES)] + [(4, 64, LANES)] * 2 + [(LANES, LANES)] * 2,
    )
    got = whole_plane(block)

    x2, x3 = 4 * gx, 2 * gx
    b2, c2, zsend_lo, zsend_hi = call(
        functools.partial(plane_kernel, gx, gy),
        (got,),
        [(x2, 32, LANES)] * 2 + [(x2, 16, LANES)] * 2,
        [(2, LANES, LANES)] * 2,
    )
    zlo, zhi = swap(zsend_hi, zsend_lo, "gz")

    q2b = pair_lanes(4 * gy, 0, (0, 1, 2, 3), 2 * gy, 0, 0.5)
    q2c = pair_lanes(4 * gy, 0, (0, 1, 2, 3), 2 * gy, 64, 0.125)
    own3, zsend_up, zsend_down, w2, beta2, root2 = call(
        functools.partial(down2_kernel, gx, gy),
        (b2, c2, zlo, zhi, q2b, q2c),
        [(x3, 32, LANES)] + [(x3, HZ3, LANES)] * 2 + [(x2 + 2 * OFF2, 80, LANES)] * 2 + [(x2 + 2 * OFF2, 64, LANES)],
        [(x3, 64, LANES)] * 2 + [(x3 * 32, LANES)] * 2,
    )
    zlo, zhi = swap(zsend_up, zsend_down, "gz")

    q3b = pair_lanes(2 * gy, 0, (0, 1, 2, 3), gy, 0, 0.5)
    q3c = pair_lanes(2 * gy, 0, (0, 1, 2, 3), gy, 64, 0.125)
    u4 = repeat_lanes(gy, 0, 2 * gy, 0)
    u3 = repeat_lanes(2 * gy, 0, 4 * gy, 0)
    (e2,) = call(
        functools.partial(coarse_kernel, gx, gy),
        (position("gx").reshape(1), own3, zlo, zhi, w2, beta2, root2, q3b, q3c, u4, u3),
        [(8, 40, LANES)],
        [(x3 + 2 * OFF3, 80, LANES)] * 3
        + [(x3 + 2 * OFF3, 64, LANES)]
        + [(gx + 2, 48, LANES)] * 3
        + [(gx + 2, 32, LANES)]
        + [(gx, 64, LANES)] * 2
        + [(gx * 32, LANES)] * 2
        + [(12, 80, LANES)] * 2
        + [(gx, 32, LANES), (6, 48, LANES)],
        smem=1,
    )

    u1 = repeat_lanes(Y1, 4, Y0, HY0)
    (correction,) = call(
        functools.partial(up_kernel, gy),
        (position("gy").reshape(1), e2, w1, beta1, root1, w0, beta0, root0, u1),
        [(4, 16, 16, LANES)],
        [(16, 96, LANES)] * 2
        + [(20, 160, LANES)] * 2
        + [(8, 80, LANES), (10, 144, LANES), (4, LANES, LANES)],
        smem=1,
    )
    return correction


def solution(mesh):
    return jax.shard_map(
        functools.partial(shards, mesh.shape["gx"], mesh.shape["gy"]),
        mesh=mesh,
        in_specs=(P(None, "gx", "gy", "gz"), P("gx", "gy", "gz"), P(), P("gx", "gy", "gz")),
        out_specs=P(None, "gx", "gy", "gz"),
        check_vma=False,
    )
```

```python
import functools
import math

import jax
import jax.numpy as jnp
from jax import lax
from jax.experimental import pallas as pl
from jax.experimental.pallas import tpu as pltpu
from jax.sharding import PartitionSpec as P

F32 = jnp.float32
COARSE_ITERS = 8
TAU = 0.8 / 6.0
LANES = 128
HX0, HY0, HZ0 = 3, 3, 16
Y0 = 16 + 2 * HY0
Y1 = 16
HZ2 = 10
HZ3 = 20
OFF2, OFF3 = 4, 2


def halves(a):
    high = a.astype(jnp.bfloat16)
    return [high, (a - high.astype(F32)).astype(jnp.bfloat16)]


def mm(pairs):
    left, right = [], []
    for a, m in pairs:
        left += halves(a)
        right += [m, m]
    return jnp.dot(jnp.concatenate(left, axis=1), jnp.concatenate(right, axis=0), preferred_element_type=F32)


def lane_of(n):
    return lax.broadcasted_iota(jnp.int32, (n, LANES), 1)


def lane_roll(x, shift):
    return pltpu.roll(x, shift % LANES, 1) if shift % LANES else x


def around(ref, x, row, n):
    mid = ref[x, pl.ds(row, n), :]
    total = ref[x - 1, pl.ds(row, n), :] + ref[x + 1, pl.ds(row, n), :]
    total = total + (ref[x, pl.ds(row - 1, n), :] + ref[x, pl.ds(row + 1, n), :])
    return mid, total + (lane_roll(mid, 1) + lane_roll(mid, -1))


def around_whole(ref, x, row, n, width):
    mid = ref[x, pl.ds(row, n), :]
    total = ref[x - 1, pl.ds(row, n), :] + ref[x + 1, pl.ds(row, n), :]
    total = total + (ref[x, pl.ds(row - 1, n), :] + ref[x, pl.ds(row + 1, n), :])
    place = lane_of(n) & (width - 1)
    total = total + jnp.where(place == 0, 0.0, lane_roll(mid, 1))
    return mid, total + jnp.where(place == width - 1, 0.0, lane_roll(mid, -1))


def chunks(n, size):
    return [(r, min(size, n - r)) for r in range(0, n, size)]


def roots_of(c):
    live = c > 0.0
    inv = lax.rsqrt(jnp.where(live, c, 1.0))
    return jnp.where(live, c * inv, 0.0), jnp.where(live, inv, 0.0)


def inverse(root):
    live = root > 0.0
    return jnp.where(live, 1.0 / jnp.where(live, root, 1.0), 0.0)


def jacobi(live, mid, beta, total):
    return jnp.where(live, 0.2 * mid + beta + TAU * total, 0.0)


def bits(mask):
    return jnp.where(mask, 1.0, 0.0)


def pair_lanes(width, start, out_width, out_start, scale, fields=4, step=1):
    source = lax.broadcasted_iota(jnp.int32, (LANES, LANES), 0)
    out = lane_of(LANES) - out_start
    shift = out_width.bit_length() - 1
    first = (out >> shift) * (step * width) + start + 2 * (out & (out_width - 1))
    hit = ((source == first) | (source == first + 1)) & (out >= 0) & (out < fields * out_width)
    return (scale * bits(hit)).astype(jnp.bfloat16)


def repeat_lanes(width, out_width):
    source = lax.broadcasted_iota(jnp.int32, (LANES, LANES), 0)
    out = lane_of(LANES)
    return bits((source == out >> 1) & (out < 4 * out_width)).astype(jnp.bfloat16)


def repeat_to_level0():
    source = lax.broadcasted_iota(jnp.int32, (LANES, LANES), 0)
    out = lane_of(LANES)
    field = bits(out >= Y0) + bits(out >= 2 * Y0) + bits(out >= 3 * Y0)
    field = field.astype(jnp.int32)
    wanted = field * Y1 + 4 + ((out - field * Y0 - HY0) >> 1)
    return bits((source == wanted) & (out < 4 * Y0)).astype(jnp.bfloat16)


def residual(w, beta, root, x, row, n, mid_total):
    mid, total = mid_total
    root_x = root[x, pl.ds(row - 8, n), :]
    return root_x * ((1.0 / TAU) * beta[x, pl.ds(row, n), :] - 6.0 * mid + total), root_x * root_x


def loop(begin, end, body, unroll=1):
    def step(i, carry):
        body(i)
        return carry

    lax.fori_loop(begin, end, step, 0, unroll=unroll)


def fold_rows(ref, k, n):
    return ref[k, pl.ds(0, n, stride=2), :] + ref[k, pl.ds(1, n, stride=2), :]


def unfold_rows(ref, k, n, value):
    ref[k, pl.ds(0, n, stride=2), :] = value
    ref[k, pl.ds(1, n, stride=2), :] = value


def prepare_kernel(table_any, ids_any, source_any, roughness_any, full, low, high, table, ids, roughness, sems):
    copies = [
        pltpu.make_async_copy(table_any, table, sems.at[0]),
        pltpu.make_async_copy(ids_any, ids, sems.at[1]),
        pltpu.make_async_copy(roughness_any, roughness, sems.at[2]),
        pltpu.make_async_copy(source_any, full.at[pl.ds(0, 4)], sems.at[3]),
    ]
    for copy in copies:
        copy.start()
    for copy in copies[:3]:
        copy.wait()
    block = lane_of(8) >> 3
    for i in range(2):
        for j in range(2):
            along_z = jnp.zeros((8, LANES), F32)
            for k in range(16):
                along_z = jnp.where(block == k, table[ids[i, j, k]], along_z)
            for x in range(8 * i, 8 * i + 8):
                full[4, x, pl.ds(8 * j, 8), :] = roughness[x, pl.ds(8 * j, 8), :] * along_z
    copies[3].wait()
    for x in range(HX0):
        for f in range(5):
            low[f, x] = full[f, x]
            high[f, x] = full[f, 16 - HX0 + x]


def edge_kernel(xlo, full, xhi, ylo, yhi):
    def put(x, f, plane):
        ylo[x, pl.ds(f * HY0, HY0), :] = plane[0:HY0]
        yhi[x, pl.ds(f * HY0, HY0), :] = plane[16 - HY0 : 16]

    for x in range(HX0):
        for f in range(5):
            put(x, f, xlo[f, x])
            put(x + HX0 + 16, f, xhi[f, x])

    def own(x):
        for f in range(5):
            put(x + HX0, f, full[f, x])

    loop(0, 16, own, 16)


def turn_kernel(xlo, full, xhi, ylo, yhi, turned, zlo, zhi, stage):
    stage[...] = jnp.zeros_like(stage)

    def turn(x, slot, planes):
        for f in range(5):
            stage[slot, pl.ds(f * Y0 + HY0, 16), :] = planes[f]
            stage[slot, pl.ds(f * Y0, HY0), :] = ylo[x, pl.ds(f * HY0, HY0), :]
            stage[slot, pl.ds(f * Y0 + HY0 + 16, HY0), :] = yhi[x, pl.ds(f * HY0, HY0), :]
        t = stage[slot].T
        turned[x] = t
        zlo[x] = t[0:HZ0]
        zhi[x] = t[128 - HZ0 : 128]

    for x in range(HX0):
        turn(x, 0, [xlo[f, x] for f in range(5)])
        turn(x + HX0 + 16, 1, [xhi[f, x] for f in range(5)])

    def own(k):
        for slot in range(4):
            x = 4 * k + slot
            turn(x + HX0, slot, [full[f, x] for f in range(5)])

    loop(0, 4, own, 2)


def down0_kernel(turned, zlo, zhi, out, ylo, yhi, w, beta, root, rsum, csum, rz, cz, stage):
    planes = 16 + 2 * HX0
    depth = 128 + 2 * HZ0
    half = depth // 2
    qb = pair_lanes(Y0, HY0, 8, 0, 0.5)
    qc = pair_lanes(Y0, HY0, 8, 32, 0.125, 2, 3)

    def prepare(x, t, row, n):
        lane = lane_of(n)
        v = lane_roll(jnp.where(lane < 4 * Y0, 0.0, t), -4 * Y0)
        v = v + lane_roll(v, Y0)
        v = v + lane_roll(v, 2 * Y0)
        root_v, inv_v = roots_of(v)
        pressure = lane >= 3 * Y0
        root[x, pl.ds(row, n), :] = jnp.where(pressure, inv_v, root_v)
        beta[x, pl.ds(8 + row, n), :] = TAU * t * jnp.where(pressure, root_v, inv_v)

    def setup(x):
        for ref in (beta, w):
            ref[x, pl.ds(0, 8), :] = jnp.zeros((8, LANES), F32)
            ref[x, pl.ds(8 + depth, 8), :] = jnp.zeros((8, LANES), F32)
        prepare(x, zlo[x], 0, HZ0)
        for r, n in chunks(128, 32):
            prepare(x, turned[x, pl.ds(r, n), :], HZ0 + r, n)
        prepare(x, zhi[x], HZ0 + 128, HZ0)

    loop(0, planes, setup, 2)

    def smooth(x):
        for r, n in chunks(depth, 32):
            mid, total = around(beta, x, 8 + r, n)
            w[x, pl.ds(8 + r, n), :] = jnp.where(root[x, pl.ds(r, n), :] > 0.0, 1.2 * mid + TAU * total, 0.0)

    loop(1, planes - 1, smooth, 10)

    def restrict(k):
        for r, n in chunks(depth, 32):
            x = HX0 + 2 * k
            res_a, coef_a = residual(w, beta, root, x, 8 + r, n, around(w, x, 8 + r, n))
            res_b, coef_b = residual(w, beta, root, x + 1, 8 + r, n, around(w, x + 1, 8 + r, n))
            rsum[k, pl.ds(r, n), :] = res_a + res_b
            csum[k, pl.ds(r, n), :] = coef_a + coef_b

    loop(0, 8, restrict, 4)

    def fold(k):
        rz[pl.ds(k * half, half), :] = fold_rows(rsum, k, half)
        cz[pl.ds(k * half, half), :] = fold_rows(csum, k, half)

    for k in range(8):
        fold(k)
    stage[...] = jnp.zeros_like(stage)
    for k in range(0, 8, 2):
        both = mm(((rz[pl.ds(k * half, 2 * half), :], qb), (cz[pl.ds(k * half, 2 * half), :], qc)))
        for i in range(2):
            stage[k + i, pl.ds(0, half), :] = both[i * half : (i + 1) * half]
    for k in range(8):
        t = stage[k].T
        out[k] = t[0:48]
        for a in range(6):
            ylo[k, pl.ds(a * 4, 4), :] = t[a * 8 : a * 8 + 4]
            yhi[k, pl.ds(a * 4, 4), :] = t[a * 8 + 4 : a * 8 + 8]


def join_kernel(own, ylo, yhi, low, high):
    for ref, first in ((low, 0), (high, 4)):
        for x in range(4):
            ref[x, pl.ds(0, 48), :] = own[first + x]
            ref[x, pl.ds(48, 24), :] = ylo[first + x]
            ref[x, pl.ds(72, 24), :] = yhi[first + x]


def down1_kernel(own, ylo, yhi, xlo, xhi, block, w, beta, root, stage, rsum, csum, rz, cz):
    stage[...] = jnp.zeros_like(stage)

    def prepare(x, slot, mine, lo, hi):
        for a in range(6):
            stage[slot, pl.ds(a * Y1 + 4, 8), :] = mine(a * 8, 8)
            stage[slot, pl.ds(a * Y1, 4), :] = lo(a * 4, 4)
            stage[slot, pl.ds(a * Y1 + 12, 4), :] = hi(a * 4, 4)
        t = stage[slot].T[0:80]
        lane = lane_of(80)
        c = jnp.where(lane < Y1, lane_roll(t, 64), jnp.where(lane < 2 * Y1, lane_roll(t, 80), lane_roll(t, 96)))
        root_x, inv_x = roots_of(jnp.where(lane < 4 * Y1, c, 0.0))
        root[x] = root_x
        beta[x, pl.ds(8, 80), :] = TAU * t * inv_x
        for ref in (beta, w):
            ref[x, pl.ds(0, 8), :] = jnp.zeros((8, LANES), F32)
            ref[x, pl.ds(88, 8), :] = jnp.zeros((8, LANES), F32)

    for x in range(4):
        for slot, side in ((0, xlo), (1, xhi)):
            prepare(
                x + 12 * slot,
                2 * (x % 2) + slot,
                lambda r, n: side[x, pl.ds(r, n), :],
                lambda r, n: side[x, pl.ds(48 + r, n), :],
                lambda r, n: side[x, pl.ds(72 + r, n), :],
            )
    for x in range(8):
        prepare(
            x + 4,
            x % 4,
            lambda r, n: own[x, pl.ds(r, n), :],
            lambda r, n: ylo[x, pl.ds(r, n), :],
            lambda r, n: yhi[x, pl.ds(r, n), :],
        )

    def smooth(x):
        for r, n in chunks(80, 40):
            mid, total = around(beta, x, 8 + r, n)
            w[x, pl.ds(8 + r, n), :] = jnp.where(root[x, pl.ds(r, n), :] > 0.0, 1.2 * mid + TAU * total, 0.0)

    loop(1, 15, smooth, 14)
    for k in range(4):
        for r, n in chunks(64, 32):
            x = 4 + 2 * k
            res_a, coef_a = residual(w, beta, root, x, 16 + r, n, around(w, x, 16 + r, n))
            res_b, coef_b = residual(w, beta, root, x + 1, 16 + r, n, around(w, x + 1, 16 + r, n))
            rsum[k, pl.ds(r, n), :] = res_a + res_b
            csum[k, pl.ds(r, n), :] = coef_a + coef_b
    for k in range(4):
        rz[pl.ds(k * 32, 32), :] = fold_rows(rsum, k, 32)
        cz[pl.ds(k * 32, 32), :] = fold_rows(csum, k, 32)
    qb = pair_lanes(Y1, 4, 4, 0, 0.5)
    qc = pair_lanes(Y1, 4, 4, 16, 0.125, 2, 3)
    t = mm(((rz[...], qb), (cz[...], qc))).T[0:24]

    def copy(i):
        block[i] = t

    loop(0, block.shape[0], copy, 8 if block.shape[0] % 8 == 0 else 1)


def plane_kernel(gx, gy, got, b, c, zlo, zhi, stage_b, stage_c):
    width = 4 * gy
    stage_b[...] = jnp.zeros_like(stage_b)
    stage_c[...] = jnp.zeros_like(stage_c)

    def one(i, slot):
        for j in range(gy):
            for a in range(4):
                stage_b[slot, pl.ds(a * width + 4 * j, 4), :] = got[i * gy + j, pl.ds(4 * a, 4), :]
            for a in range(2):
                stage_c[slot, pl.ds(a * width + 4 * j, 4), :] = got[i * gy + j, pl.ds(16 + 4 * a, 4), :]
        tb = stage_b[slot].T
        tc = stage_c[slot].T
        for x in range(4):
            at = 4 * i + x
            b[at] = tb[x * 32 : (x + 1) * 32]
            c[at] = tc[x * 32 : (x + 1) * 32]
            for ref, first in ((zlo, x * 32), (zhi, (x + 1) * 32 - HZ2)):
                ref[at, pl.ds(0, HZ2), :] = tb[first : first + HZ2]
                ref[at, pl.ds(HZ2, 5), :] = jnp.where(
                    lane_of(5) < 64, tc[first : first + 5], lane_roll(tc[first + 5 : first + 10], 64)
                )
                ref[at, pl.ds(HZ2 + 5, 1), :] = jnp.zeros((1, LANES), F32)

    def body(k):
        one(2 * k, 0)
        one(2 * k + 1, 1)

    loop(0, gx // 2, body)


def down2_kernel(gx, gy, place, b, c, zlo, zhi, out, zup, zdown, w_kept, beta_kept, root_kept, w, beta, root, rsum, csum, rz, cz):
    size_x, width = 4 * gx, 4 * gy

    def prepare(x, row, t, tc):
        n = t.shape[0]
        lane = lane_of(n)
        c_all = jnp.where(lane < width, tc, jnp.where(lane < 2 * width, lane_roll(tc, width), lane_roll(tc, 2 * width)))
        root_x, inv_x = roots_of(jnp.where(lane < 4 * width, c_all, 0.0))
        root[x + OFF2, pl.ds(row, n), :] = root_x
        beta[x + OFF2, pl.ds(8 + row, n), :] = TAU * t * inv_x

    for x in list(range(OFF2)) + list(range(OFF2 + size_x, 2 * OFF2 + size_x)):
        for ref in (beta, w, root):
            ref[x] = jnp.zeros(ref.shape[1:], F32)

    def setup(x):
        for ref in (beta, w):
            ref[x + OFF2, pl.ds(0, 16), :] = jnp.zeros((16, LANES), F32)
            ref[x + OFF2, pl.ds(64, 16), :] = jnp.zeros((16, LANES), F32)
        root[x + OFF2, pl.ds(0, 8), :] = jnp.zeros((8, LANES), F32)
        root[x + OFF2, pl.ds(56, 8), :] = jnp.zeros((8, LANES), F32)
        prepare(x, 16, b[x], c[x])
        for ref, row in ((zlo, 16 - HZ2), (zhi, 48)):
            packed = ref[x, pl.ds(HZ2, 5), :]
            prepare(x, row, ref[x, pl.ds(0, 5), :], jnp.where(lane_of(5) < 64, packed, 0.0))
            prepare(x, row + 5, ref[x, pl.ds(5, 5), :], jnp.where(lane_of(5) < 64, lane_roll(packed, 64), 0.0))

    loop(0, size_x, setup, 8)

    def smooth(x):
        for r, n in chunks(64, 32):
            mid, total = around_whole(beta, x, 8 + r, n, width)
            w[x, pl.ds(8 + r, n), :] = jnp.where(root[x, pl.ds(r, n), :] > 0.0, 1.2 * mid + TAU * total, 0.0)

    loop(OFF2, size_x + OFF2, smooth, 8)
    restrict_whole(size_x, OFF2, width, w, beta, root, rsum, csum, rz, cz)
    qb = pair_lanes(width, 0, width // 2, 0, 0.5)
    qc = pair_lanes(width, 0, width // 2, 64, 0.125)
    first = 4 * place[0] - 4 + OFF2
    for p in range(12):
        w_kept[p] = w[first + p, pl.ds(16, 48), :]
        beta_kept[p] = beta[first + p, pl.ds(16, 48), :]
        root_kept[p] = root[first + p, pl.ds(8, 48), :]
    for k in range(0, size_x // 2, 4):
        rows = pl.ds(k * 32, 128)
        t = mm(((rz[rows, :], qb), (cz[rows, :], qc)))
        for i in range(4):
            out[k + i] = t[i * 32 : (i + 1) * 32]
            zup[k + i] = t[i * 32 + 24 - HZ3 : i * 32 + 24]
            zdown[k + i] = t[i * 32 + 8 : i * 32 + 8 + HZ3]


def restrict_whole(size_x, off, width, w, beta, root, rsum, csum, rz, cz):
    def body(k):
        for r, n in chunks(64, 32):
            x = 2 * k + off
            res_a, coef_a = residual(w, beta, root, x, 8 + r, n, around_whole(w, x, 8 + r, n, width))
            res_b, coef_b = residual(w, beta, root, x + 1, 8 + r, n, around_whole(w, x + 1, 8 + r, n, width))
            rsum[k, pl.ds(r, n), :] = res_a + res_b
            csum[k, pl.ds(r, n), :] = coef_a + coef_b

    loop(0, size_x // 2, body, 4 if size_x % 8 == 0 else 2)
    for k in range(size_x // 2):
        rz[pl.ds(k * 32, 32), :] = fold_rows(rsum, k, 32)
        cz[pl.ds(k * 32, 32), :] = fold_rows(csum, k, 32)


def relax_whole(first, planes, begin, depth, width, src, dst, beta, root, unroll):
    def body(x):
        for r, n in chunks(depth, 32):
            r = r + begin
            mid, total = around_whole(src, x, 8 + r, n, width)
            live = root[x, pl.ds(r, n), :] > 0.0
            dst[x, pl.ds(8 + r, n), :] = jacobi(live, mid, beta[x, pl.ds(8 + r, n), :], total)

    loop(first, first + planes, body, unroll)


def relax_kept(first, planes, width, src, dst, beta, root):
    def body(x):
        for r, n in chunks(48, 24):
            mid, total = around_whole(src, x, 8 + r, n, width)
            dst[x, pl.ds(8 + r, n), :] = jacobi(root[x, pl.ds(r, n), :] > 0.0, mid, beta[x, pl.ds(r, n), :], total)

    loop(first, first + planes, body, planes)


def coarse_kernel(gx, gy, place, own, zlo, zhi, w2, beta2, root2, e2, beta3, w3, v3, root3, beta4, w4, v4, root4, rsum, csum, rz, cz, v2, w2b, fine3, fine2):
    size_x, width = 2 * gx, 2 * gy
    for ref in (beta3, w3, v3, root3, beta4, w4, v4):
        ref[...] = jnp.zeros_like(ref)

    def prepare(x, row, t):
        n = t.shape[0]
        root_x, inv_x = roots_of(jnp.where(lane_of(n) < 4 * width, lane_roll(t, 64), 0.0))
        root3[x + OFF3, pl.ds(row, n), :] = root_x
        beta3[x + OFF3, pl.ds(8 + row, n), :] = TAU * t * inv_x

    def setup(x):
        prepare(x, 24 - HZ3, zlo[x])
        prepare(x, 24, own[x, pl.ds(8, 16), :])
        prepare(x, 40, zhi[x])

    loop(0, size_x, setup, 4)

    def smooth(x):
        for r, n in chunks(64, 32):
            mid, total = around_whole(beta3, x, 8 + r, n, width)
            w3[x, pl.ds(8 + r, n), :] = jnp.where(root3[x, pl.ds(r, n), :] > 0.0, 1.2 * mid + TAU * total, 0.0)

    loop(OFF3, size_x + OFF3, smooth, 4)
    restrict_whole(size_x, OFF3, width, w3, beta3, root3, rsum, csum, rz, cz)
    t = mm(((rz[...], pair_lanes(width, 0, gy, 0, 0.5)), (cz[...], pair_lanes(width, 0, gy, 64, 0.125))))
    for x in range(gx):
        t_x = t[x * 32 : (x + 1) * 32]
        root_x, inv_x = roots_of(jnp.where(lane_of(32) < 4 * gy, lane_roll(t_x, 64), 0.0))
        root4[x + 1] = root_x
        beta4[x + 1, pl.ds(8, 32), :] = TAU * t_x * inv_x
        w4[x + 1, pl.ds(8, 32), :] = TAU * t_x * inv_x
    here, there = w4, v4
    for step in range(COARSE_ITERS - 1):
        relax_whole(1, gx, 0, 32, gy, here, there, beta4, root4, gx)
        here, there = there, here

    e4 = [here[x + 1, pl.ds(16, 16), :] * inverse(root4[x + 1, pl.ds(8, 16), :]) for x in range(gx)]
    e4 = mm(((jnp.concatenate(e4, axis=0), repeat_lanes(gy, width)),))
    for x in range(gx):
        unfold_rows(fine3, x, 16, e4[x * 16 : (x + 1) * 16])
        for i in range(2):
            at = 2 * x + i + OFF3
            w3[at, pl.ds(24, 32), :] = w3[at, pl.ds(24, 32), :] + root3[at, pl.ds(16, 32), :] * fine3[x]
    relax_whole(OFF3, size_x, 16, 32, width, w3, v3, beta3, root3, 4)
    relax_whole(OFF3, size_x, 16, 32, width, v3, w3, beta3, root3, 4)

    first3 = 2 * place[0] - 2 + OFF3
    e3 = [w3[first3 + k, pl.ds(28, 24), :] * inverse(root3[first3 + k, pl.ds(20, 24), :]) for k in range(6)]
    e3 = mm(((jnp.concatenate(e3, axis=0), repeat_lanes(width, 2 * width)),))
    for k in range(6):
        unfold_rows(fine2, k, 24, e3[k * 24 : (k + 1) * 24])
    for p in range(12):
        w2b[p, pl.ds(8, 48), :] = w2[p] + root2[p] * fine2[p // 2]
        for ref in (w2b, v2):
            ref[p, pl.ds(0, 8), :] = jnp.zeros((8, LANES), F32)
            ref[p, pl.ds(56, 8), :] = jnp.zeros((8, LANES), F32)
    relax_kept(1, 10, 2 * width, w2b, v2, beta2, root2)
    relax_kept(2, 8, 2 * width, v2, w2b, beta2, root2)
    for k in range(8):
        e2[k] = w2b[k + 2, pl.ds(12, 40), :] * inverse(root2[k + 2, pl.ds(4, 40), :])


def up_kernel(gy, place, e2, w1, beta1, root1, w0, beta0, root0, out, w1b, v1, w0b, v0, fine1, fine0, turned):
    width = 4 * gy
    source_lane = lax.broadcasted_iota(jnp.int32, (LANES, LANES), 0)
    target_lane = lane_of(LANES)
    wanted_y = 4 * place[0] - 2 + ((target_lane & (Y1 - 1)) >> 1)
    wanted = (target_lane >> 4) * width + wanted_y
    valid = (source_lane == wanted) & (wanted_y >= 0) & (wanted_y < width) & (target_lane < 4 * Y1)
    u2 = jnp.where(valid, 1.0, 0.0).astype(jnp.bfloat16)
    for ref in (w1b, v1):
        for row in (0, 88):
            ref[:, pl.ds(row, 8), :] = jnp.zeros((16, 8, LANES), F32)
    for ref in (w0b, v0):
        for row in (0, 152):
            ref[:, pl.ds(row, 8), :] = jnp.zeros((20, 8, LANES), F32)
    for k in range(0, 8, 4):
        e = mm(((jnp.concatenate([e2[k + i] for i in range(4)], axis=0), u2),))
        for i in range(4):
            unfold_rows(fine1, k + i, 40, e[i * 40 : (i + 1) * 40])
    for x in range(1, 15):
        w1b[x, pl.ds(8, 80), :] = w1[x, pl.ds(8, 80), :] + root1[x] * fine1[x // 2]

    def relax1(src, dst, begin, end):
        def body(x):
            for r, n in chunks(80, 40):
                mid, total = around(src, x, 8 + r, n)
                live = root1[x, pl.ds(r, n), :] > 0.0
                dst[x, pl.ds(8 + r, n), :] = jacobi(live, mid, beta1[x, pl.ds(8 + r, n), :], total)

        loop(begin, end, body, end - begin)

    relax1(w1b, v1, 2, 14)
    relax1(v1, w1b, 3, 13)

    u1 = repeat_to_level0()
    for k in range(0, 10, 2):
        e = [w1b[x, pl.ds(12, 72), :] * inverse(root1[x, pl.ds(4, 72), :]) for x in (k + 3, k + 4)]
        e = mm(((jnp.concatenate(e, axis=0), u1),))
        for i in range(2):
            unfold_rows(fine0, k + i, 72, e[i * 72 : (i + 1) * 72])

    def up0(k):
        for i in range(2):
            x = 2 * k + i
            for r, n in chunks(144, 48):
                add = root0[x + 1, pl.ds(8 + r, n), :] * fine0[k, pl.ds(r, n), :]
                w0b[x, pl.ds(8 + r, n), :] = w0[x + 1, pl.ds(16 + r, n), :] + add

    loop(0, 10, up0, 10)

    def first0(x):
        for r, n in chunks(144, 24):
            mid, total = around(w0b, x, 8 + r, n)
            live = root0[x + 1, pl.ds(8 + r, n), :] > 0.0
            v0[x, pl.ds(8 + r, n), :] = jacobi(live, mid, beta0[x + 1, pl.ds(16 + r, n), :], total)

    loop(1, 19, first0, 9)

    def last0(j):
        for slot in range(4):
            k = 4 * j + slot
            x = k + 2
            for r, n in chunks(128, 32):
                mid, total = around(v0, x, 16 + r, n)
                root_x = root0[x + 1, pl.ds(16 + r, n), :]
                new = jacobi(root_x > 0.0, mid, beta0[x + 1, pl.ds(24 + r, n), :], total)
                turned[slot, pl.ds(r, n), :] = new * inverse(root_x)
        for slot in range(4):
            t = turned[slot].T
            for f in range(4):
                out[f, 4 * j + slot] = t[f * Y0 + HY0 : f * Y0 + HY0 + 16]

    loop(0, 4, last0)


def call(kernel, args, outs, scratch, smem=0):
    vmem = pl.BlockSpec(memory_space=pltpu.VMEM)
    scalar = pl.BlockSpec(memory_space=pltpu.SMEM)
    sizes = [a.shape for a in args] + outs + scratch
    held = sum(4 * math.prod(s[:-2]) * -(-s[-2] // 8) * 8 * LANES for s in sizes if len(s) > 1)
    return pl.pallas_call(
        kernel,
        out_shape=[jax.ShapeDtypeStruct(s, F32) for s in outs],
        in_specs=[scalar] * smem + [vmem] * (len(args) - smem),
        out_specs=[vmem] * len(outs),
        scratch_shapes=[pltpu.VMEM(s, F32) for s in scratch],
        compiler_params=pltpu.CompilerParams(vmem_limit_bytes=held + 2 * 1024 * 1024),
    )(*args)


def swap(to_up, to_down, axis):
    n = lax.axis_size(axis)
    from_below = lax.ppermute(to_up, axis, [(i, i + 1) for i in range(n - 1)])
    from_above = lax.ppermute(to_down, axis, [(i + 1, i) for i in range(n - 1)])
    return from_below, from_above


def whole_plane(block):
    return lax.all_to_all(block, ("gx", "gy"), 0, 0, tiled=True)


def position(axis):
    return lax.axis_index(axis).astype(jnp.int32)


def shards(gx, gy, source, material_ids, material_table, roughness):
    anywhere = pl.BlockSpec(memory_space=pltpu.HBM)
    full, low, high = pl.pallas_call(
        prepare_kernel,
        out_shape=[jax.ShapeDtypeStruct((5, n, 16, LANES), F32) for n in (16, HX0, HX0)],
        in_specs=[anywhere] * 4,
        out_specs=[pl.BlockSpec(memory_space=pltpu.VMEM)] * 3,
        scratch_shapes=[
            pltpu.SMEM(material_table.shape, F32),
            pltpu.SMEM(material_ids.shape, jnp.int32),
            pltpu.VMEM(roughness.shape, F32),
            pltpu.SemaphoreType.DMA((4,)),
        ],
        compiler_params=pltpu.CompilerParams(vmem_limit_bytes=4 * 1024 * 1024),
    )(material_table, material_ids, source, roughness)
    xlo, xhi = swap(high, low, "gx")
    planes = 16 + 2 * HX0
    ysend_lo, ysend_hi = call(edge_kernel, (xlo, full, xhi), [(planes, 15, LANES)] * 2, [])
    ylo, yhi = swap(ysend_hi, ysend_lo, "gy")
    turned, zsend_lo, zsend_hi = call(
        turn_kernel,
        (xlo, full, xhi, ylo, yhi),
        [(planes, 128, LANES)] + [(planes, HZ0, LANES)] * 2,
        [(4, LANES, LANES)],
    )
    zlo, zhi = swap(zsend_hi, zsend_lo, "gz")

    depth = 128 + 2 * HZ0
    own1, ysend_lo, ysend_hi, w0, beta0, root0 = call(
        down0_kernel,
        (turned, zlo, zhi),
        [(8, 48, LANES)] + [(8, 24, LANES)] * 2 + [(planes, depth + 16, LANES)] * 2 + [(planes, depth, LANES)],
        [(8, depth, LANES)] * 2 + [(4 * depth, LANES)] * 2 + [(8, LANES, LANES)],
    )
    ylo, yhi = swap(ysend_hi, ysend_lo, "gy")
    low, high = call(join_kernel, (own1, ylo, yhi), [(4, 96, LANES)] * 2, [])
    xlo, xhi = swap(high, low, "gx")

    block, w1, beta1, root1 = call(
        down1_kernel,
        (own1, ylo, yhi, xlo, xhi),
        [(gx * gy, 24, LANES), (16, 96, LANES), (16, 96, LANES), (16, 80, LANES)],
        [(4, LANES, LANES)] + [(4, 64, LANES)] * 2 + [(LANES, LANES)] * 2,
    )
    got = whole_plane(block)

    x2, x3 = 4 * gx, 2 * gx
    b2, c2, zsend_lo, zsend_hi = call(
        functools.partial(plane_kernel, gx, gy),
        (got,),
        [(x2, 32, LANES)] * 2 + [(x2, 16, LANES)] * 2,
        [(2, LANES, LANES)] * 2,
    )
    zlo, zhi = swap(zsend_hi, zsend_lo, "gz")

    own3, zsend_up, zsend_down, w2, beta2, root2 = call(
        functools.partial(down2_kernel, gx, gy),
        (position("gx").reshape(1), b2, c2, zlo, zhi),
        [(x3, 32, LANES)] + [(x3, HZ3, LANES)] * 2 + [(12, 48, LANES)] * 3,
        [(x2 + 2 * OFF2, 80, LANES)] * 2
        + [(x2 + 2 * OFF2, 64, LANES)]
        + [(x3, 64, LANES)] * 2
        + [(x3 * 32, LANES)] * 2,
        smem=1,
    )
    zlo, zhi = swap(zsend_up, zsend_down, "gz")

    (e2,) = call(
        functools.partial(coarse_kernel, gx, gy),
        (position("gx").reshape(1), own3, zlo, zhi, w2, beta2, root2),
        [(8, 40, LANES)],
        [(x3 + 2 * OFF3, 80, LANES)] * 3
        + [(x3 + 2 * OFF3, 64, LANES)]
        + [(gx + 2, 48, LANES)] * 3
        + [(gx + 2, 32, LANES)]
        + [(gx, 64, LANES)] * 2
        + [(gx * 32, LANES)] * 2
        + [(12, 64, LANES)] * 2
        + [(gx, 32, LANES), (6, 48, LANES)],
        smem=1,
    )

    (correction,) = call(
        functools.partial(up_kernel, gy),
        (position("gy").reshape(1), e2, w1, beta1, root1, w0, beta0, root0),
        [(4, 16, 16, LANES)],
        [(16, 96, LANES)] * 2
        + [(20, 160, LANES)] * 2
        + [(8, 80, LANES), (10, 144, LANES), (4, LANES, LANES)],
        smem=1,
    )
    return correction


def solution(mesh):
    return jax.shard_map(
        functools.partial(shards, mesh.shape["gx"], mesh.shape["gy"]),
        mesh=mesh,
        in_specs=(P(None, "gx", "gy", "gz"), P("gx", "gy", "gz"), P(), P("gx", "gy", "gz")),
        out_specs=P(None, "gx", "gy", "gz"),
        check_vma=False,
    )
```

```python
import functools
import math

import jax
import jax.numpy as jnp
from jax import lax
from jax.experimental import pallas as pl
from jax.experimental.pallas import tpu as pltpu
from jax.sharding import PartitionSpec as P

F32 = jnp.float32
COARSE_ITERS = 8
TAU = 0.8 / 6.0
LANES = 128
HX0, HY0, HZ0 = 3, 3, 16
Y0 = 16 + 2 * HY0
Y1 = 16
HZ2 = 10
HZ3 = 20
OFF2, OFF3 = 4, 2


def halves(a):
    high = a.astype(jnp.bfloat16)
    return [high, (a - high.astype(F32)).astype(jnp.bfloat16)]


def mm(pairs):
    left, right = [], []
    for a, m in pairs:
        left += halves(a)
        right += [m, m]
    return jnp.dot(jnp.concatenate(left, axis=1), jnp.concatenate(right, axis=0), preferred_element_type=F32)


def lane_of(n):
    return lax.broadcasted_iota(jnp.int32, (n, LANES), 1)


def lane_roll(x, shift):
    return pltpu.roll(x, shift % LANES, 1) if shift % LANES else x


def around(ref, x, row, n):
    mid = ref[x, pl.ds(row, n), :]
    total = ref[x - 1, pl.ds(row, n), :] + ref[x + 1, pl.ds(row, n), :]
    total = total + (ref[x, pl.ds(row - 1, n), :] + ref[x, pl.ds(row + 1, n), :])
    return mid, total + (lane_roll(mid, 1) + lane_roll(mid, -1))


def around_whole(ref, x, row, n, width):
    mid = ref[x, pl.ds(row, n), :]
    total = ref[x - 1, pl.ds(row, n), :] + ref[x + 1, pl.ds(row, n), :]
    total = total + (ref[x, pl.ds(row - 1, n), :] + ref[x, pl.ds(row + 1, n), :])
    place = lane_of(n) & (width - 1)
    total = total + jnp.where(place == 0, 0.0, lane_roll(mid, 1))
    return mid, total + jnp.where(place == width - 1, 0.0, lane_roll(mid, -1))


def chunks(n, size):
    return [(r, min(size, n - r)) for r in range(0, n, size)]


def roots_of(c):
    live = c > 0.0
    inv = lax.rsqrt(jnp.where(live, c, 1.0))
    return jnp.where(live, c * inv, 0.0), jnp.where(live, inv, 0.0)


def inverse(root):
    live = root > 0.0
    return jnp.where(live, 1.0 / jnp.where(live, root, 1.0), 0.0)


def jacobi(live, mid, beta, total):
    return jnp.where(live, 0.2 * mid + beta + TAU * total, 0.0)


def bits(mask):
    return jnp.where(mask, 1.0, 0.0)


def pair_lanes(width, start, out_width, out_start, scale, fields=4, step=1):
    source = lax.broadcasted_iota(jnp.int32, (LANES, LANES), 0)
    out = lane_of(LANES) - out_start
    shift = out_width.bit_length() - 1
    first = (out >> shift) * (step * width) + start + 2 * (out & (out_width - 1))
    hit = ((source == first) | (source == first + 1)) & (out >= 0) & (out < fields * out_width)
    return (scale * bits(hit)).astype(jnp.bfloat16)


def repeat_lanes(width, out_width):
    source = lax.broadcasted_iota(jnp.int32, (LANES, LANES), 0)
    out = lane_of(LANES)
    return bits((source == out >> 1) & (out < 4 * out_width)).astype(jnp.bfloat16)


def repeat_to_level0():
    source = lax.broadcasted_iota(jnp.int32, (LANES, LANES), 0)
    out = lane_of(LANES)
    field = bits(out >= Y0) + bits(out >= 2 * Y0) + bits(out >= 3 * Y0)
    field = field.astype(jnp.int32)
    wanted = field * Y1 + 4 + ((out - field * Y0 - HY0) >> 1)
    return bits((source == wanted) & (out < 4 * Y0)).astype(jnp.bfloat16)


def residual(w, beta, root, x, row, n, mid_total):
    mid, total = mid_total
    root_x = root[x, pl.ds(row - 8, n), :]
    return root_x * ((1.0 / TAU) * beta[x, pl.ds(row, n), :] - 6.0 * mid + total), root_x * root_x


def loop(begin, end, body, unroll=1):
    def step(i, carry):
        body(i)
        return carry

    lax.fori_loop(begin, end, step, 0, unroll=unroll)


def fold_rows(ref, k, n):
    return ref[k, pl.ds(0, n, stride=2), :] + ref[k, pl.ds(1, n, stride=2), :]


def unfold_rows(ref, k, n, value):
    ref[k, pl.ds(0, n, stride=2), :] = value
    ref[k, pl.ds(1, n, stride=2), :] = value


def prepare_kernel(table_any, ids_any, source_any, roughness_any, full, low, high, table, ids, roughness, sems):
    copies = [
        pltpu.make_async_copy(table_any, table, sems.at[0]),
        pltpu.make_async_copy(ids_any, ids, sems.at[1]),
        pltpu.make_async_copy(roughness_any, roughness, sems.at[2]),
        pltpu.make_async_copy(source_any, full.at[pl.ds(0, 4)], sems.at[3]),
    ]
    for copy in copies:
        copy.start()
    for copy in copies[:3]:
        copy.wait()
    block = lane_of(8) >> 3
    for i in range(2):
        for j in range(2):
            along_z = jnp.zeros((8, LANES), F32)
            for k in range(16):
                along_z = jnp.where(block == k, table[ids[i, j, k]], along_z)
            for x in range(8 * i, 8 * i + 8):
                full[4, x, pl.ds(8 * j, 8), :] = roughness[x, pl.ds(8 * j, 8), :] * along_z
    copies[3].wait()
    for x in range(HX0):
        for f in range(5):
            low[f, x] = full[f, x]
            high[f, x] = full[f, 16 - HX0 + x]


def edge_kernel(xlo, full, xhi, ylo, yhi):
    def put(x, f, plane):
        ylo[x, pl.ds(f * HY0, HY0), :] = plane[0:HY0]
        yhi[x, pl.ds(f * HY0, HY0), :] = plane[16 - HY0 : 16]

    for x in range(HX0):
        for f in range(5):
            put(x, f, xlo[f, x])
            put(x + HX0 + 16, f, xhi[f, x])

    def own(x):
        for f in range(5):
            put(x + HX0, f, full[f, x])

    loop(0, 16, own, 16)


def turn_kernel(xlo, full, xhi, ylo, yhi, turned, zlo, zhi, stage):
    stage[...] = jnp.zeros_like(stage)

    def turn(x, slot, planes):
        for f in range(5):
            stage[slot, pl.ds(f * Y0 + HY0, 16), :] = planes[f]
            stage[slot, pl.ds(f * Y0, HY0), :] = ylo[x, pl.ds(f * HY0, HY0), :]
            stage[slot, pl.ds(f * Y0 + HY0 + 16, HY0), :] = yhi[x, pl.ds(f * HY0, HY0), :]
        t = stage[slot].T
        turned[x] = t
        zlo[x] = t[0:HZ0]
        zhi[x] = t[128 - HZ0 : 128]

    for x in range(HX0):
        turn(x, 0, [xlo[f, x] for f in range(5)])
        turn(x + HX0 + 16, 1, [xhi[f, x] for f in range(5)])

    def own(k):
        for slot in range(4):
            x = 4 * k + slot
            turn(x + HX0, slot, [full[f, x] for f in range(5)])

    loop(0, 4, own, 2)


def down0_kernel(turned, zlo, zhi, out, ylo, yhi, w, beta, root, rsum, csum, rz, cz, stage):
    planes = 16 + 2 * HX0
    depth = 128 + 2 * HZ0
    half = depth // 2
    qb = pair_lanes(Y0, HY0, 8, 0, 0.5)
    qc = pair_lanes(Y0, HY0, 8, 32, 0.125, 2, 3)

    def prepare(x, t, row, n):
        lane = lane_of(n)
        v = lane_roll(jnp.where(lane < 4 * Y0, 0.0, t), -4 * Y0)
        v = v + lane_roll(v, Y0)
        v = v + lane_roll(v, 2 * Y0)
        root_v, inv_v = roots_of(v)
        pressure = lane >= 3 * Y0
        root[x, pl.ds(row, n), :] = jnp.where(pressure, inv_v, root_v)
        beta[x, pl.ds(8 + row, n), :] = TAU * t * jnp.where(pressure, root_v, inv_v)

    def setup(x):
        for ref in (beta, w):
            ref[x, pl.ds(0, 8), :] = jnp.zeros((8, LANES), F32)
            ref[x, pl.ds(8 + depth, 8), :] = jnp.zeros((8, LANES), F32)
        prepare(x, zlo[x], 0, HZ0)
        for r, n in chunks(128, 32):
            prepare(x, turned[x, pl.ds(r, n), :], HZ0 + r, n)
        prepare(x, zhi[x], HZ0 + 128, HZ0)

    loop(0, planes, setup, 2)

    def smooth(x):
        for r, n in chunks(depth, 32):
            mid, total = around(beta, x, 8 + r, n)
            w[x, pl.ds(8 + r, n), :] = jnp.where(root[x, pl.ds(r, n), :] > 0.0, 1.2 * mid + TAU * total, 0.0)

    loop(1, planes - 1, smooth, 10)

    def restrict(k):
        for r, n in chunks(depth, 32):
            x = HX0 + 2 * k
            res_a, coef_a = residual(w, beta, root, x, 8 + r, n, around(w, x, 8 + r, n))
            res_b, coef_b = residual(w, beta, root, x + 1, 8 + r, n, around(w, x + 1, 8 + r, n))
            rsum[k, pl.ds(r, n), :] = res_a + res_b
            csum[k, pl.ds(r, n), :] = coef_a + coef_b

    loop(0, 8, restrict, 4)

    def fold(k):
        rz[pl.ds(k * half, half), :] = fold_rows(rsum, k, half)
        cz[pl.ds(k * half, half), :] = fold_rows(csum, k, half)

    for k in range(8):
        fold(k)
    stage[...] = jnp.zeros_like(stage)
    for k in range(0, 8, 2):
        both = mm(((rz[pl.ds(k * half, 2 * half), :], qb), (cz[pl.ds(k * half, 2 * half), :], qc)))
        for i in range(2):
            stage[k + i, pl.ds(0, half), :] = both[i * half : (i + 1) * half]
    for k in range(8):
        t = stage[k].T
        out[k] = t[0:48]
        for a in range(6):
            ylo[k, pl.ds(a * 4, 4), :] = t[a * 8 : a * 8 + 4]
            yhi[k, pl.ds(a * 4, 4), :] = t[a * 8 + 4 : a * 8 + 8]


def join_kernel(own, ylo, yhi, low, high):
    for ref, first in ((low, 0), (high, 4)):
        for x in range(4):
            ref[x, pl.ds(0, 48), :] = own[first + x]
            ref[x, pl.ds(48, 24), :] = ylo[first + x]
            ref[x, pl.ds(72, 24), :] = yhi[first + x]


def down1_kernel(own, ylo, yhi, xlo, xhi, block, w, beta, root, stage, rsum, csum, rz, cz):
    stage[...] = jnp.zeros_like(stage)

    def prepare(x, slot, mine, lo, hi):
        for a in range(6):
            stage[slot, pl.ds(a * Y1 + 4, 8), :] = mine(a * 8, 8)
            stage[slot, pl.ds(a * Y1, 4), :] = lo(a * 4, 4)
            stage[slot, pl.ds(a * Y1 + 12, 4), :] = hi(a * 4, 4)
        t = stage[slot].T[0:80]
        lane = lane_of(80)
        c = jnp.where(lane < Y1, lane_roll(t, 64), jnp.where(lane < 2 * Y1, lane_roll(t, 80), lane_roll(t, 96)))
        root_x, inv_x = roots_of(jnp.where(lane < 4 * Y1, c, 0.0))
        root[x] = root_x
        beta[x, pl.ds(8, 80), :] = TAU * t * inv_x
        for ref in (beta, w):
            ref[x, pl.ds(0, 8), :] = jnp.zeros((8, LANES), F32)
            ref[x, pl.ds(88, 8), :] = jnp.zeros((8, LANES), F32)

    for x in range(4):
        for slot, side in ((0, xlo), (1, xhi)):
            prepare(
                x + 12 * slot,
                2 * (x % 2) + slot,
                lambda r, n: side[x, pl.ds(r, n), :],
                lambda r, n: side[x, pl.ds(48 + r, n), :],
                lambda r, n: side[x, pl.ds(72 + r, n), :],
            )
    for x in range(8):
        prepare(
            x + 4,
            x % 4,
            lambda r, n: own[x, pl.ds(r, n), :],
            lambda r, n: ylo[x, pl.ds(r, n), :],
            lambda r, n: yhi[x, pl.ds(r, n), :],
        )

    def smooth(x):
        for r, n in chunks(80, 40):
            mid, total = around(beta, x, 8 + r, n)
            w[x, pl.ds(8 + r, n), :] = jnp.where(root[x, pl.ds(r, n), :] > 0.0, 1.2 * mid + TAU * total, 0.0)

    loop(1, 15, smooth, 14)
    for k in range(4):
        for r, n in chunks(64, 32):
            x = 4 + 2 * k
            res_a, coef_a = residual(w, beta, root, x, 16 + r, n, around(w, x, 16 + r, n))
            res_b, coef_b = residual(w, beta, root, x + 1, 16 + r, n, around(w, x + 1, 16 + r, n))
            rsum[k, pl.ds(r, n), :] = res_a + res_b
            csum[k, pl.ds(r, n), :] = coef_a + coef_b
    for k in range(4):
        rz[pl.ds(k * 32, 32), :] = fold_rows(rsum, k, 32)
        cz[pl.ds(k * 32, 32), :] = fold_rows(csum, k, 32)
    qb = pair_lanes(Y1, 4, 4, 0, 0.5)
    qc = pair_lanes(Y1, 4, 4, 16, 0.125, 2, 3)
    t = mm(((rz[...], qb), (cz[...], qc))).T[0:24]

    def copy(i):
        block[i] = t

    loop(0, block.shape[0], copy, 8 if block.shape[0] % 8 == 0 else 1)


def plane_kernel(gx, gy, got, b, c, zlo, zhi, stage_b, stage_c):
    width = 4 * gy
    stage_b[...] = jnp.zeros_like(stage_b)
    stage_c[...] = jnp.zeros_like(stage_c)

    def one(i, slot):
        for j in range(gy):
            for a in range(4):
                stage_b[slot, pl.ds(a * width + 4 * j, 4), :] = got[i * gy + j, pl.ds(4 * a, 4), :]
            for a in range(2):
                stage_c[slot, pl.ds(a * width + 4 * j, 4), :] = got[i * gy + j, pl.ds(16 + 4 * a, 4), :]
        tb = stage_b[slot].T
        tc = stage_c[slot].T
        for x in range(4):
            at = 4 * i + x
            b[at] = tb[x * 32 : (x + 1) * 32]
            c[at] = tc[x * 32 : (x + 1) * 32]
            for ref, first in ((zlo, x * 32), (zhi, (x + 1) * 32 - HZ2)):
                ref[at, pl.ds(0, HZ2), :] = tb[first : first + HZ2]
                ref[at, pl.ds(HZ2, 5), :] = jnp.where(
                    lane_of(5) < 64, tc[first : first + 5], lane_roll(tc[first + 5 : first + 10], 64)
                )
                ref[at, pl.ds(HZ2 + 5, 1), :] = jnp.zeros((1, LANES), F32)

    def body(k):
        one(2 * k, 0)
        one(2 * k + 1, 1)

    loop(0, gx // 2, body)


def down2_kernel(gx, gy, b, c, zlo, zhi, out, zup, zdown, w_kept, beta_kept, root_kept, w, beta, root, rsum, csum, rz, cz):
    size_x, width = 4 * gx, 4 * gy

    def prepare(x, row, t, tc):
        n = t.shape[0]
        lane = lane_of(n)
        c_all = jnp.where(lane < width, tc, jnp.where(lane < 2 * width, lane_roll(tc, width), lane_roll(tc, 2 * width)))
        root_x, inv_x = roots_of(jnp.where(lane < 4 * width, c_all, 0.0))
        root[x + OFF2, pl.ds(row, n), :] = root_x
        beta[x + OFF2, pl.ds(8 + row, n), :] = TAU * t * inv_x

    for x in list(range(OFF2)) + list(range(OFF2 + size_x, 2 * OFF2 + size_x)):
        for ref in (beta, w, root):
            ref[x] = jnp.zeros(ref.shape[1:], F32)

    def setup(x):
        for ref in (beta, w):
            ref[x + OFF2, pl.ds(0, 16), :] = jnp.zeros((16, LANES), F32)
            ref[x + OFF2, pl.ds(64, 16), :] = jnp.zeros((16, LANES), F32)
        root[x + OFF2, pl.ds(0, 8), :] = jnp.zeros((8, LANES), F32)
        root[x + OFF2, pl.ds(56, 8), :] = jnp.zeros((8, LANES), F32)
        prepare(x, 16, b[x], c[x])
        for ref, row in ((zlo, 16 - HZ2), (zhi, 48)):
            packed = ref[x, pl.ds(HZ2, 5), :]
            prepare(x, row, ref[x, pl.ds(0, 5), :], jnp.where(lane_of(5) < 64, packed, 0.0))
            prepare(x, row + 5, ref[x, pl.ds(5, 5), :], jnp.where(lane_of(5) < 64, lane_roll(packed, 64), 0.0))

    loop(0, size_x, setup, 8)

    def smooth(x):
        for r, n in chunks(64, 32):
            mid, total = around_whole(beta, x, 8 + r, n, width)
            w[x, pl.ds(8 + r, n), :] = jnp.where(root[x, pl.ds(r, n), :] > 0.0, 1.2 * mid + TAU * total, 0.0)

    loop(OFF2, size_x + OFF2, smooth, 8)
    restrict_whole(size_x, OFF2, width, w, beta, root, rsum, csum, rz, cz)
    qb = pair_lanes(width, 0, width // 2, 0, 0.5)
    qc = pair_lanes(width, 0, width // 2, 64, 0.125)
    first = 4 * position("gx") - 4 + OFF2
    for p in range(12):
        w_kept[p] = w[first + p, pl.ds(16, 48), :]
        beta_kept[p] = beta[first + p, pl.ds(16, 48), :]
        root_kept[p] = root[first + p, pl.ds(8, 48), :]
    for k in range(0, size_x // 2, 4):
        rows = pl.ds(k * 32, 128)
        t = mm(((rz[rows, :], qb), (cz[rows, :], qc)))
        for i in range(4):
            out[k + i] = t[i * 32 : (i + 1) * 32]
            zup[k + i] = t[i * 32 + 24 - HZ3 : i * 32 + 24]
            zdown[k + i] = t[i * 32 + 8 : i * 32 + 8 + HZ3]


def restrict_whole(size_x, off, width, w, beta, root, rsum, csum, rz, cz):
    def body(k):
        for r, n in chunks(64, 32):
            x = 2 * k + off
            res_a, coef_a = residual(w, beta, root, x, 8 + r, n, around_whole(w, x, 8 + r, n, width))
            res_b, coef_b = residual(w, beta, root, x + 1, 8 + r, n, around_whole(w, x + 1, 8 + r, n, width))
            rsum[k, pl.ds(r, n), :] = res_a + res_b
            csum[k, pl.ds(r, n), :] = coef_a + coef_b

    loop(0, size_x // 2, body, 4 if size_x % 8 == 0 else 2)
    for k in range(size_x // 2):
        rz[pl.ds(k * 32, 32), :] = fold_rows(rsum, k, 32)
        cz[pl.ds(k * 32, 32), :] = fold_rows(csum, k, 32)


def relax_whole(first, planes, begin, depth, width, src, dst, beta, root, unroll):
    def body(x):
        for r, n in chunks(depth, 32):
            r = r + begin
            mid, total = around_whole(src, x, 8 + r, n, width)
            live = root[x, pl.ds(r, n), :] > 0.0
            dst[x, pl.ds(8 + r, n), :] = jacobi(live, mid, beta[x, pl.ds(8 + r, n), :], total)

    loop(first, first + planes, body, unroll)


def relax_kept(first, planes, width, src, dst, beta, root):
    def body(x):
        for r, n in chunks(48, 24):
            mid, total = around_whole(src, x, 8 + r, n, width)
            dst[x, pl.ds(8 + r, n), :] = jacobi(root[x, pl.ds(r, n), :] > 0.0, mid, beta[x, pl.ds(r, n), :], total)

    loop(first, first + planes, body, planes)


def coarse_kernel(gx, gy, own, zlo, zhi, w2, beta2, root2, e2, beta3, w3, v3, root3, beta4, w4, v4, root4, rsum, csum, rz, cz, v2, w2b, fine3, fine2):
    size_x, width = 2 * gx, 2 * gy
    for ref in (beta3, w3, v3, root3, beta4, w4, v4):
        ref[...] = jnp.zeros_like(ref)

    def prepare(x, row, t):
        n = t.shape[0]
        root_x, inv_x = roots_of(jnp.where(lane_of(n) < 4 * width, lane_roll(t, 64), 0.0))
        root3[x + OFF3, pl.ds(row, n), :] = root_x
        beta3[x + OFF3, pl.ds(8 + row, n), :] = TAU * t * inv_x

    def setup(x):
        prepare(x, 24 - HZ3, zlo[x])
        prepare(x, 24, own[x, pl.ds(8, 16), :])
        prepare(x, 40, zhi[x])

    loop(0, size_x, setup, 4)

    def smooth(x):
        for r, n in chunks(64, 32):
            mid, total = around_whole(beta3, x, 8 + r, n, width)
            w3[x, pl.ds(8 + r, n), :] = jnp.where(root3[x, pl.ds(r, n), :] > 0.0, 1.2 * mid + TAU * total, 0.0)

    loop(OFF3, size_x + OFF3, smooth, 4)
    restrict_whole(size_x, OFF3, width, w3, beta3, root3, rsum, csum, rz, cz)
    t = mm(((rz[...], pair_lanes(width, 0, gy, 0, 0.5)), (cz[...], pair_lanes(width, 0, gy, 64, 0.125))))
    for x in range(gx):
        t_x = t[x * 32 : (x + 1) * 32]
        root_x, inv_x = roots_of(jnp.where(lane_of(32) < 4 * gy, lane_roll(t_x, 64), 0.0))
        root4[x + 1] = root_x
        beta4[x + 1, pl.ds(8, 32), :] = TAU * t_x * inv_x
        w4[x + 1, pl.ds(8, 32), :] = TAU * t_x * inv_x
    here, there = w4, v4
    for step in range(COARSE_ITERS - 1):
        relax_whole(1, gx, 0, 32, gy, here, there, beta4, root4, gx)
        here, there = there, here

    e4 = [here[x + 1, pl.ds(16, 16), :] * inverse(root4[x + 1, pl.ds(8, 16), :]) for x in range(gx)]
    e4 = mm(((jnp.concatenate(e4, axis=0), repeat_lanes(gy, width)),))
    for x in range(gx):
        unfold_rows(fine3, x, 16, e4[x * 16 : (x + 1) * 16])
        for i in range(2):
            at = 2 * x + i + OFF3
            w3[at, pl.ds(24, 32), :] = w3[at, pl.ds(24, 32), :] + root3[at, pl.ds(16, 32), :] * fine3[x]
    relax_whole(OFF3, size_x, 16, 32, width, w3, v3, beta3, root3, 4)
    relax_whole(OFF3, size_x, 16, 32, width, v3, w3, beta3, root3, 4)

    first3 = 2 * position("gx") - 2 + OFF3
    e3 = [w3[first3 + k, pl.ds(28, 24), :] * inverse(root3[first3 + k, pl.ds(20, 24), :]) for k in range(6)]
    e3 = mm(((jnp.concatenate(e3, axis=0), repeat_lanes(width, 2 * width)),))
    for k in range(6):
        unfold_rows(fine2, k, 24, e3[k * 24 : (k + 1) * 24])
    for p in range(12):
        w2b[p, pl.ds(8, 48), :] = w2[p] + root2[p] * fine2[p // 2]
        for ref in (w2b, v2):
            ref[p, pl.ds(0, 8), :] = jnp.zeros((8, LANES), F32)
            ref[p, pl.ds(56, 8), :] = jnp.zeros((8, LANES), F32)
    relax_kept(1, 10, 2 * width, w2b, v2, beta2, root2)
    relax_kept(2, 8, 2 * width, v2, w2b, beta2, root2)
    for k in range(8):
        e2[k] = w2b[k + 2, pl.ds(12, 40), :] * inverse(root2[k + 2, pl.ds(4, 40), :])


def up_kernel(gy, e2, w1, beta1, root1, w0, beta0, root0, out, w1b, v1, w0b, v0, fine1, fine0, turned):
    width = 4 * gy
    source_lane = lax.broadcasted_iota(jnp.int32, (LANES, LANES), 0)
    target_lane = lane_of(LANES)
    wanted_y = 4 * position("gy") - 2 + ((target_lane & (Y1 - 1)) >> 1)
    wanted = (target_lane >> 4) * width + wanted_y
    valid = (source_lane == wanted) & (wanted_y >= 0) & (wanted_y < width) & (target_lane < 4 * Y1)
    u2 = jnp.where(valid, 1.0, 0.0).astype(jnp.bfloat16)
    for ref in (w1b, v1):
        for row in (0, 88):
            ref[:, pl.ds(row, 8), :] = jnp.zeros((16, 8, LANES), F32)
    for ref in (w0b, v0):
        for row in (0, 152):
            ref[:, pl.ds(row, 8), :] = jnp.zeros((20, 8, LANES), F32)
    for k in range(0, 8, 4):
        e = mm(((jnp.concatenate([e2[k + i] for i in range(4)], axis=0), u2),))
        for i in range(4):
            unfold_rows(fine1, k + i, 40, e[i * 40 : (i + 1) * 40])
    for x in range(1, 15):
        w1b[x, pl.ds(8, 80), :] = w1[x, pl.ds(8, 80), :] + root1[x] * fine1[x // 2]

    def relax1(src, dst, begin, end):
        def body(x):
            for r, n in chunks(80, 40):
                mid, total = around(src, x, 8 + r, n)
                live = root1[x, pl.ds(r, n), :] > 0.0
                dst[x, pl.ds(8 + r, n), :] = jacobi(live, mid, beta1[x, pl.ds(8 + r, n), :], total)

        loop(begin, end, body, end - begin)

    relax1(w1b, v1, 2, 14)
    relax1(v1, w1b, 3, 13)

    u1 = repeat_to_level0()
    for k in range(0, 10, 2):
        e = [w1b[x, pl.ds(12, 72), :] * inverse(root1[x, pl.ds(4, 72), :]) for x in (k + 3, k + 4)]
        e = mm(((jnp.concatenate(e, axis=0), u1),))
        for i in range(2):
            unfold_rows(fine0, k + i, 72, e[i * 72 : (i + 1) * 72])

    def up0(k):
        for i in range(2):
            x = 2 * k + i
            for r, n in chunks(144, 48):
                add = root0[x + 1, pl.ds(8 + r, n), :] * fine0[k, pl.ds(r, n), :]
                w0b[x, pl.ds(8 + r, n), :] = w0[x + 1, pl.ds(16 + r, n), :] + add

    loop(0, 10, up0, 10)

    def first0(x):
        for r, n in chunks(144, 24):
            mid, total = around(w0b, x, 8 + r, n)
            live = root0[x + 1, pl.ds(8 + r, n), :] > 0.0
            v0[x, pl.ds(8 + r, n), :] = jacobi(live, mid, beta0[x + 1, pl.ds(16 + r, n), :], total)

    loop(1, 19, first0, 9)

    def last0(j):
        for slot in range(4):
            k = 4 * j + slot
            x = k + 2
            for r, n in chunks(128, 32):
                mid, total = around(v0, x, 16 + r, n)
                root_x = root0[x + 1, pl.ds(16 + r, n), :]
                new = jacobi(root_x > 0.0, mid, beta0[x + 1, pl.ds(24 + r, n), :], total)
                turned[slot, pl.ds(r, n), :] = new * inverse(root_x)
        for slot in range(4):
            t = turned[slot].T
            for f in range(4):
                out[f, 4 * j + slot] = t[f * Y0 + HY0 : f * Y0 + HY0 + 16]

    loop(0, 4, last0)


def call(kernel, args, outs, scratch):
    vmem = pl.BlockSpec(memory_space=pltpu.VMEM)
    sizes = [a.shape for a in args] + outs + scratch
    held = sum(4 * math.prod(s[:-2]) * -(-s[-2] // 8) * 8 * LANES for s in sizes if len(s) > 1)
    return pl.pallas_call(
        kernel,
        out_shape=[jax.ShapeDtypeStruct(s, F32) for s in outs],
        in_specs=[vmem] * len(args),
        out_specs=[vmem] * len(outs),
        scratch_shapes=[pltpu.VMEM(s, F32) for s in scratch],
        compiler_params=pltpu.CompilerParams(vmem_limit_bytes=held + 2 * 1024 * 1024),
    )(*args)


def swap(to_up, to_down, axis):
    n = lax.axis_size(axis)
    from_below = lax.ppermute(to_up, axis, [(i, i + 1) for i in range(n - 1)])
    from_above = lax.ppermute(to_down, axis, [(i + 1, i) for i in range(n - 1)])
    return from_below, from_above


def whole_plane(block):
    return lax.all_to_all(block, ("gx", "gy"), 0, 0, tiled=True)


def position(axis):
    return lax.axis_index(axis).astype(jnp.int32)


def shards(gx, gy, source, material_ids, material_table, roughness):
    anywhere = pl.BlockSpec(memory_space=pltpu.HBM)
    full, low, high = pl.pallas_call(
        prepare_kernel,
        out_shape=[jax.ShapeDtypeStruct((5, n, 16, LANES), F32) for n in (16, HX0, HX0)],
        in_specs=[anywhere] * 4,
        out_specs=[pl.BlockSpec(memory_space=pltpu.VMEM)] * 3,
        scratch_shapes=[
            pltpu.SMEM(material_table.shape, F32),
            pltpu.SMEM(material_ids.shape, jnp.int32),
            pltpu.VMEM(roughness.shape, F32),
            pltpu.SemaphoreType.DMA((4,)),
        ],
        compiler_params=pltpu.CompilerParams(vmem_limit_bytes=4 * 1024 * 1024),
    )(material_table, material_ids, source, roughness)
    xlo, xhi = swap(high, low, "gx")
    planes = 16 + 2 * HX0
    ysend_lo, ysend_hi = call(edge_kernel, (xlo, full, xhi), [(planes, 15, LANES)] * 2, [])
    ylo, yhi = swap(ysend_hi, ysend_lo, "gy")
    turned, zsend_lo, zsend_hi = call(
        turn_kernel,
        (xlo, full, xhi, ylo, yhi),
        [(planes, 128, LANES)] + [(planes, HZ0, LANES)] * 2,
        [(4, LANES, LANES)],
    )
    zlo, zhi = swap(zsend_hi, zsend_lo, "gz")

    depth = 128 + 2 * HZ0
    own1, ysend_lo, ysend_hi, w0, beta0, root0 = call(
        down0_kernel,
        (turned, zlo, zhi),
        [(8, 48, LANES)] + [(8, 24, LANES)] * 2 + [(planes, depth + 16, LANES)] * 2 + [(planes, depth, LANES)],
        [(8, depth, LANES)] * 2 + [(4 * depth, LANES)] * 2 + [(8, LANES, LANES)],
    )
    ylo, yhi = swap(ysend_hi, ysend_lo, "gy")
    low, high = call(join_kernel, (own1, ylo, yhi), [(4, 96, LANES)] * 2, [])
    xlo, xhi = swap(high, low, "gx")

    block, w1, beta1, root1 = call(
        down1_kernel,
        (own1, ylo, yhi, xlo, xhi),
        [(gx * gy, 24, LANES), (16, 96, LANES), (16, 96, LANES), (16, 80, LANES)],
        [(4, LANES, LANES)] + [(4, 64, LANES)] * 2 + [(LANES, LANES)] * 2,
    )
    got = whole_plane(block)

    x2, x3 = 4 * gx, 2 * gx
    b2, c2, zsend_lo, zsend_hi = call(
        functools.partial(plane_kernel, gx, gy),
        (got,),
        [(x2, 32, LANES)] * 2 + [(x2, 16, LANES)] * 2,
        [(2, LANES, LANES)] * 2,
    )
    zlo, zhi = swap(zsend_hi, zsend_lo, "gz")

    own3, zsend_up, zsend_down, w2, beta2, root2 = call(
        functools.partial(down2_kernel, gx, gy),
        (b2, c2, zlo, zhi),
        [(x3, 32, LANES)] + [(x3, HZ3, LANES)] * 2 + [(12, 48, LANES)] * 3,
        [(x2 + 2 * OFF2, 80, LANES)] * 2
        + [(x2 + 2 * OFF2, 64, LANES)]
        + [(x3, 64, LANES)] * 2
        + [(x3 * 32, LANES)] * 2,
    )
    zlo, zhi = swap(zsend_up, zsend_down, "gz")

    (e2,) = call(
        functools.partial(coarse_kernel, gx, gy),
        (own3, zlo, zhi, w2, beta2, root2),
        [(8, 40, LANES)],
        [(x3 + 2 * OFF3, 80, LANES)] * 3
        + [(x3 + 2 * OFF3, 64, LANES)]
        + [(gx + 2, 48, LANES)] * 3
        + [(gx + 2, 32, LANES)]
        + [(gx, 64, LANES)] * 2
        + [(gx * 32, LANES)] * 2
        + [(12, 64, LANES)] * 2
        + [(gx, 32, LANES), (6, 48, LANES)],
    )

    (correction,) = call(
        functools.partial(up_kernel, gy),
        (e2, w1, beta1, root1, w0, beta0, root0),
        [(4, 16, 16, LANES)],
        [(16, 96, LANES)] * 2
        + [(20, 160, LANES)] * 2
        + [(8, 80, LANES), (10, 144, LANES), (4, LANES, LANES)],
    )
    return correction


def solution(mesh):
    return jax.shard_map(
        functools.partial(shards, mesh.shape["gx"], mesh.shape["gy"]),
        mesh=mesh,
        in_specs=(P(None, "gx", "gy", "gz"), P("gx", "gy", "gz"), P(), P("gx", "gy", "gz")),
        out_specs=P(None, "gx", "gy", "gz"),
        check_vma=False,
    )
```

```python
import functools
import math

import jax
import jax.numpy as jnp
from jax import lax
from jax.experimental import pallas as pl
from jax.experimental.pallas import tpu as pltpu
from jax.sharding import PartitionSpec as P

F32 = jnp.float32
COARSE_ITERS = 8
TAU = 0.8 / 6.0
LANES = 128
HX0, HY0, HZ0 = 3, 3, 16
Y0 = 16 + 2 * HY0
H1, H2 = 6, 5
Y1, Y2 = 8 + 2 * H1, 4 + 2 * H2
OFF3 = 2


def halves(a):
    high = a.astype(jnp.bfloat16)
    return [high, (a - high.astype(F32)).astype(jnp.bfloat16)]


def mm(pairs):
    left, right = [], []
    for a, m in pairs:
        left += halves(a)
        right += [m, m]
    return jnp.dot(jnp.concatenate(left, axis=1), jnp.concatenate(right, axis=0), preferred_element_type=F32)


def lane_of(n):
    return lax.broadcasted_iota(jnp.int32, (n, LANES), 1)


def lane_roll(x, shift):
    return pltpu.roll(x, shift % LANES, 1) if shift % LANES else x


def around(ref, x, row, n):
    mid = ref[x, pl.ds(row, n), :]
    total = ref[x - 1, pl.ds(row, n), :] + ref[x + 1, pl.ds(row, n), :]
    total = total + (ref[x, pl.ds(row - 1, n), :] + ref[x, pl.ds(row + 1, n), :])
    return mid, total + (lane_roll(mid, 1) + lane_roll(mid, -1))


def around_whole(ref, x, row, n, width):
    mid = ref[x, pl.ds(row, n), :]
    total = ref[x - 1, pl.ds(row, n), :] + ref[x + 1, pl.ds(row, n), :]
    total = total + (ref[x, pl.ds(row - 1, n), :] + ref[x, pl.ds(row + 1, n), :])
    place = lane_of(n) & (width - 1)
    total = total + jnp.where(place == 0, 0.0, lane_roll(mid, 1))
    return mid, total + jnp.where(place == width - 1, 0.0, lane_roll(mid, -1))


def chunks(n, size):
    return [(r, min(size, n - r)) for r in range(0, n, size)]


def roots_of(c):
    live = c > 0.0
    inv = lax.rsqrt(jnp.where(live, c, 1.0))
    return jnp.where(live, c * inv, 0.0), jnp.where(live, inv, 0.0)


def inverse(root):
    live = root > 0.0
    return jnp.where(live, 1.0 / jnp.where(live, root, 1.0), 0.0)


def jacobi(live, mid, beta, total):
    return jnp.where(live, 0.2 * mid + beta + TAU * total, 0.0)


def bits(mask):
    return jnp.where(mask, 1.0, 0.0)


def pair_lanes(width, start, out_width, out_start, scale, fields=4, step=1):
    source = lax.broadcasted_iota(jnp.int32, (LANES, LANES), 0)
    out = lane_of(LANES) - out_start
    shift = out_width.bit_length() - 1
    first = (out >> shift) * (step * width) + start + 2 * (out & (out_width - 1))
    hit = ((source == first) | (source == first + 1)) & (out >= 0) & (out < fields * out_width)
    return (scale * bits(hit)).astype(jnp.bfloat16)


def repeat_lanes(width, out_width):
    source = lax.broadcasted_iota(jnp.int32, (LANES, LANES), 0)
    out = lane_of(LANES)
    return bits((source == out >> 1) & (out < 4 * out_width)).astype(jnp.bfloat16)


def repeat_local(width, shift, out_width, out_start, fields=4):
    source = lax.broadcasted_iota(jnp.int32, (LANES, LANES), 0)
    out = lane_of(LANES)
    field = bits(out >= out_width) + bits(out >= 2 * out_width) + bits(out >= 3 * out_width)
    field = field.astype(jnp.int32)
    row = shift + ((out - field * out_width - out_start) >> 1)
    hit = (source == field * width + row) & (row >= 0) & (row < width) & (out < fields * out_width)
    return bits(hit).astype(jnp.bfloat16)


def four_fields(t, width):
    lane = lane_of(t.shape[0])
    c = jnp.where(lane < 2 * width, lane_roll(t, -3 * width), lane_roll(t, -2 * width))
    c = jnp.where(lane < width, lane_roll(t, -4 * width), c)
    return jnp.where(lane < 4 * width, c, 0.0)


def residual(w, beta, root, x, row, n, mid_total):
    mid, total = mid_total
    root_x = root[x, pl.ds(row - 8, n), :]
    return root_x * ((1.0 / TAU) * beta[x, pl.ds(row, n), :] - 6.0 * mid + total), root_x * root_x


def thirds(ref):
    n = ref.shape[0] // 3
    return [ref.at[pl.ds(i * n, n)] for i in range(3)]


def loop(begin, end, body, unroll=1):
    def step(i, carry):
        body(i)
        return carry

    lax.fori_loop(begin, end, step, 0, unroll=unroll)


def fold_rows(ref, k, n):
    return ref[k, pl.ds(0, n, stride=2), :] + ref[k, pl.ds(1, n, stride=2), :]


def unfold_rows(ref, k, n, value):
    ref[k, pl.ds(0, n, stride=2), :] = value
    ref[k, pl.ds(1, n, stride=2), :] = value


def prepare_kernel(table_any, ids_any, source_any, roughness_any, full, low, high, table, ids, roughness, sems):
    copies = [
        pltpu.make_async_copy(table_any, table, sems.at[0]),
        pltpu.make_async_copy(ids_any, ids, sems.at[1]),
        pltpu.make_async_copy(roughness_any, roughness, sems.at[2]),
        pltpu.make_async_copy(source_any, full.at[pl.ds(0, 4)], sems.at[3]),
    ]
    for copy in copies:
        copy.start()
    for copy in copies[:3]:
        copy.wait()
    block = lane_of(8) >> 3
    for i in range(2):
        for j in range(2):
            along_z = jnp.zeros((8, LANES), F32)
            for k in range(16):
                along_z = jnp.where(block == k, table[ids[i, j, k]], along_z)
            for x in range(8 * i, 8 * i + 8):
                full[4, x, pl.ds(8 * j, 8), :] = roughness[x, pl.ds(8 * j, 8), :] * along_z
    copies[3].wait()
    for x in range(HX0):
        for f in range(5):
            low[f, x] = full[f, x]
            high[f, x] = full[f, 16 - HX0 + x]


def edge_kernel(xlo, full, xhi, ylo, yhi):
    def put(x, f, plane):
        ylo[x, pl.ds(f * HY0, HY0), :] = plane[0:HY0]
        yhi[x, pl.ds(f * HY0, HY0), :] = plane[16 - HY0 : 16]

    for x in range(HX0):
        for f in range(5):
            put(x, f, xlo[f, x])
            put(x + HX0 + 16, f, xhi[f, x])

    def own(x):
        for f in range(5):
            put(x + HX0, f, full[f, x])

    loop(0, 16, own, 16)


def turn_kernel(xlo, full, xhi, ylo, yhi, turned, zlo, zhi, stage):
    stage[...] = jnp.zeros_like(stage)

    def turn(x, slot, planes):
        for f in range(5):
            stage[slot, pl.ds(f * Y0 + HY0, 16), :] = planes[f]
            stage[slot, pl.ds(f * Y0, HY0), :] = ylo[x, pl.ds(f * HY0, HY0), :]
            stage[slot, pl.ds(f * Y0 + HY0 + 16, HY0), :] = yhi[x, pl.ds(f * HY0, HY0), :]
        t = stage[slot].T
        turned[x] = t
        zlo[x] = t[0:HZ0]
        zhi[x] = t[128 - HZ0 : 128]

    for x in range(HX0):
        turn(x, 0, [xlo[f, x] for f in range(5)])
        turn(x + HX0 + 16, 1, [xhi[f, x] for f in range(5)])

    def own(k):
        for slot in range(4):
            x = 4 * k + slot
            turn(x + HX0, slot, [full[f, x] for f in range(5)])

    loop(0, 4, own, 2)


def down0_kernel(turned, zlo, zhi, out, ylo, yhi, kept, rsum, csum, rz, cz, stage):
    planes = 16 + 2 * HX0
    depth = 128 + 2 * HZ0
    half = depth // 2
    w, beta, root = thirds(kept)
    qb = pair_lanes(Y0, HY0, 8, 0, 0.5)
    qc = pair_lanes(Y0, HY0, 8, 32, 0.125, 2, 3)

    def prepare(x, t, row, n):
        lane = lane_of(n)
        v = lane_roll(jnp.where(lane < 4 * Y0, 0.0, t), -4 * Y0)
        v = v + lane_roll(v, Y0)
        v = v + lane_roll(v, 2 * Y0)
        root_v, inv_v = roots_of(v)
        pressure = lane >= 3 * Y0
        root[x, pl.ds(row, n), :] = jnp.where(pressure, inv_v, root_v)
        beta[x, pl.ds(8 + row, n), :] = TAU * t * jnp.where(pressure, root_v, inv_v)

    def setup(x):
        for ref in (beta, w):
            ref[x, pl.ds(0, 8), :] = jnp.zeros((8, LANES), F32)
            ref[x, pl.ds(8 + depth, 8), :] = jnp.zeros((8, LANES), F32)
        prepare(x, zlo[x], 0, HZ0)
        for r, n in chunks(128, 32):
            prepare(x, turned[x, pl.ds(r, n), :], HZ0 + r, n)
        prepare(x, zhi[x], HZ0 + 128, HZ0)

    loop(0, planes, setup, 2)

    def smooth(x):
        for r, n in chunks(depth, 32):
            mid, total = around(beta, x, 8 + r, n)
            w[x, pl.ds(8 + r, n), :] = jnp.where(root[x, pl.ds(r, n), :] > 0.0, 1.2 * mid + TAU * total, 0.0)

    loop(1, planes - 1, smooth, 10)

    def restrict(k):
        for r, n in chunks(depth, 32):
            x = HX0 + 2 * k
            res_a, coef_a = residual(w, beta, root, x, 8 + r, n, around(w, x, 8 + r, n))
            res_b, coef_b = residual(w, beta, root, x + 1, 8 + r, n, around(w, x + 1, 8 + r, n))
            rsum[k, pl.ds(r, n), :] = res_a + res_b
            csum[k, pl.ds(r, n), :] = coef_a + coef_b

    loop(0, 8, restrict, 4)

    def fold(k):
        rz[pl.ds(k * half, half), :] = fold_rows(rsum, k, half)
        cz[pl.ds(k * half, half), :] = fold_rows(csum, k, half)

    for k in range(8):
        fold(k)
    stage[...] = jnp.zeros_like(stage)
    for k in range(0, 8, 2):
        both = mm(((rz[pl.ds(k * half, 2 * half), :], qb), (cz[pl.ds(k * half, 2 * half), :], qc)))
        for i in range(2):
            stage[k + i, pl.ds(0, half), :] = both[i * half : (i + 1) * half]
    for k in range(8):
        t = stage[k].T
        out[k] = t[0:48]
        for a in range(6):
            ylo[k, pl.ds(a * H1, H1), :] = t[a * 8 : a * 8 + H1]
            yhi[k, pl.ds(a * H1, H1), :] = t[a * 8 + 8 - H1 : a * 8 + 8]


def join1_kernel(own, ylo, yhi, turned, low, high, stage):
    stage[...] = jnp.zeros_like(stage)
    for x in range(8):
        slot = x % 4
        for a in range(6):
            stage[slot, pl.ds(a * Y1 + H1, 8), :] = own[x, pl.ds(a * 8, 8), :]
            stage[slot, pl.ds(a * Y1, H1), :] = ylo[x, pl.ds(a * H1, H1), :]
            stage[slot, pl.ds(a * Y1 + H1 + 8, H1), :] = yhi[x, pl.ds(a * H1, H1), :]
        t = stage[slot].T[0:80]
        turned[x] = t
        if x < H1:
            low[x] = t
        if x >= 8 - H1:
            high[x - 8 + H1] = t


def down1_kernel(own, xlo, xhi, block, turned2, ylo2, yhi2, kept, rsum, csum, rz, cz, beta2, root2, w2, stage):
    w, beta, root = thirds(kept)

    def prepare(x, t):
        root_x, inv_x = roots_of(four_fields(t, Y1))
        root[x, pl.ds(0, 80), :] = root_x
        beta[x, pl.ds(8, 80), :] = TAU * t * inv_x
        for ref in (beta, w):
            ref[x, pl.ds(0, 8), :] = jnp.zeros((8, LANES), F32)
            ref[x, pl.ds(88, 8), :] = jnp.zeros((8, LANES), F32)

    for x in range(H1):
        prepare(x, xlo[x])
        prepare(x + H1 + 8, xhi[x])
    for x in range(8):
        prepare(x + H1, own[x])

    def smooth(x):
        for r, n in chunks(80, 40):
            mid, total = around(beta, x, 8 + r, n)
            w[x, pl.ds(8 + r, n), :] = jnp.where(root[x, pl.ds(r, n), :] > 0.0, 1.2 * mid + TAU * total, 0.0)

    loop(1, 19, smooth, 9)

    def restrict(k):
        for r, n in chunks(80, 40):
            x = 2 + 2 * k
            res_a, coef_a = residual(w, beta, root, x, 8 + r, n, around(w, x, 8 + r, n))
            res_b, coef_b = residual(w, beta, root, x + 1, 8 + r, n, around(w, x + 1, 8 + r, n))
            rsum[k, pl.ds(r, n), :] = res_a + res_b
            csum[k, pl.ds(r, n), :] = coef_a + coef_b

    loop(0, 8, restrict, 4)
    for k in range(8):
        rz[pl.ds(k * 40, 40), :] = fold_rows(rsum, k, 40)
        cz[pl.ds(k * 40, 40), :] = fold_rows(csum, k, 40)

    t2 = mm(((rz[...], pair_lanes(Y1, 2, 8, 0, 0.5)), (cz[...], pair_lanes(Y1, 2, 8, 32, 0.125, 2, 3))))
    stage[...] = jnp.zeros_like(stage)
    for x in range(8):
        t = t2[x * 40 : (x + 1) * 40]
        root_x, inv_x = roots_of(four_fields(t, 8))
        root2[x] = root_x
        beta2[x, pl.ds(8, 40), :] = TAU * t * inv_x
        for ref in (beta2, w2):
            ref[x, pl.ds(0, 8), :] = jnp.zeros((8, LANES), F32)
            ref[x, pl.ds(48, 8), :] = jnp.zeros((8, LANES), F32)
        if 1 <= x < 7:
            stage[x % 4, pl.ds(0, 40), :] = t
            flat = stage[x % 4].T
            for a in range(6):
                turned2[x - 1, pl.ds(a * 4, 4), :] = flat[a * 8 + 2 : a * 8 + 6]
                yhi2[x - 1, pl.ds(a * H2, H2), :] = flat[a * 8 + 1 : a * 8 + 1 + H2]
                ylo2[x - 1, pl.ds(a * H2, H2), :] = flat[a * 8 + 2 : a * 8 + 2 + H2]
    for x in range(1, 7):
        mid, total = around(beta2, x, 8, 40)
        w2[x, pl.ds(8, 40), :] = jnp.where(root2[x] > 0.0, 1.2 * mid + TAU * total, 0.0)
    for k in range(2):
        x = 2 + 2 * k
        res, coef = jnp.zeros((32, LANES), F32), jnp.zeros((32, LANES), F32)
        for i in range(2):
            res_i, coef_i = residual(w2, beta2, root2, x + i, 12, 32, around(w2, x + i, 12, 32))
            res, coef = res + res_i, coef + coef_i
        rsum[k, pl.ds(0, 32), :] = res
        csum[k, pl.ds(0, 32), :] = coef
    rows = [jnp.concatenate([fold_rows(ref, k, 16) for k in range(2)], axis=0) for ref in (rsum, csum)]
    t3 = mm(((rows[0], pair_lanes(8, 2, 2, 0, 0.5)), (rows[1], pair_lanes(8, 2, 2, 8, 0.125, 2, 3))))

    stage[0, pl.ds(0, 32), :] = t3
    stage[0, pl.ds(32, 96), :] = jnp.zeros((96, LANES), F32)
    flat = stage[0].T[0:16]
    lane = lane_of(1)
    turns = [lane_roll(flat, 32 * g) for g in range(4)]
    packed = []
    for r in range(3):
        row = turns[0][4 * r : 4 * r + 1]
        for g in range(1, 4):
            row = jnp.where((lane >= 32 * g) & (lane < 32 * g + 32), turns[g][4 * r + g : 4 * r + g + 1], row)
        packed.append(row)
    for i in range(block.shape[0] // 24):
        block[pl.ds(24 * i, 24), :] = jnp.concatenate(packed * 8, axis=0)
    for i in range(block.shape[0] // 24 * 8, block.shape[0] // 3):
        block[pl.ds(3 * i, 3), :] = jnp.concatenate(packed, axis=0)


def join2_kernel(own, ylo, yhi, turned, low, high, stage):
    stage[...] = jnp.zeros_like(stage)
    for x in range(6):
        slot = x % 4
        for a in range(6):
            stage[slot, pl.ds(a * Y2 + H2, 4), :] = own[x, pl.ds(a * 4, 4), :]
            stage[slot, pl.ds(a * Y2, H2), :] = ylo[x, pl.ds(a * H2, H2), :]
            stage[slot, pl.ds(a * Y2 + H2 + 4, H2), :] = yhi[x, pl.ds(a * H2, H2), :]
        t = stage[slot].T[4:36]
        if 1 <= x < 5:
            turned[x - 1] = t
        if x < 5:
            high[x] = t
        if x >= 1:
            low[x - 1] = t


def join3_kernel(own, xlo, xhi, whole, zlo, zhi):
    for x in range(4 + 2 * H2):
        t = xlo[x] if x < H2 else own[x - H2] if x < H2 + 4 else xhi[x - H2 - 4]
        whole[x] = t
        zlo[x] = t[0:8]
        zhi[x] = t[24:32]


def plane_kernel(gx, gy, got, own, lo4, hi4, turns, stage):
    width = 2 * gy
    stage[...] = jnp.zeros_like(stage)
    for s in range(4):
        turns[s] = lane_roll(got[...], 32 * s)
    lane = lane_of(gy)
    for h in range(-(-gx // 4)):
        for i in range(12):
            r, g = i // 4, i % 4
            row = jnp.zeros((gy, LANES), F32)
            for q in range(min(4, gx - 4 * h)):
                part = turns[(q - g) % 4, pl.ds((4 * h + q) * gy * 3 + r, gy, stride=3), :]
                row = jnp.where((lane >= 32 * q) & (lane < 32 * q + 32), part, row)
            stage[h, pl.ds((i // 2) * width + i % 2, gy, stride=2), :] = row
        t = stage[h].T
        for q in range(min(4, gx - 4 * h)):
            for x in range(2):
                at = 2 * (4 * h + q) + x
                rows = t[32 * q + 16 * x : 32 * q + 16 * x + 16]
                own[at] = rows
                lo4[at] = rows[0:4]
                hi4[at] = rows[12:16]


def restrict_whole(size_x, off, width, w, beta, root, rsum, csum, rz, cz):
    def body(k):
        for r, n in chunks(64, 32):
            x = 2 * k + off
            res_a, coef_a = residual(w, beta, root, x, 8 + r, n, around_whole(w, x, 8 + r, n, width))
            res_b, coef_b = residual(w, beta, root, x + 1, 8 + r, n, around_whole(w, x + 1, 8 + r, n, width))
            rsum[k, pl.ds(r, n), :] = res_a + res_b
            csum[k, pl.ds(r, n), :] = coef_a + coef_b

    loop(0, size_x // 2, body, 4 if size_x % 8 == 0 else 2)
    for k in range(size_x // 2):
        rz[pl.ds(k * 32, 32), :] = fold_rows(rsum, k, 32)
        cz[pl.ds(k * 32, 32), :] = fold_rows(csum, k, 32)


def relax_whole(first, planes, begin, depth, width, src, dst, beta, root, unroll):
    def body(x):
        for r, n in chunks(depth, 32):
            r = r + begin
            mid, total = around_whole(src, x, 8 + r, n, width)
            live = root[x, pl.ds(r, n), :] > 0.0
            dst[x, pl.ds(8 + r, n), :] = jacobi(live, mid, beta[x, pl.ds(8 + r, n), :], total)

    loop(first, first + planes, body, unroll)


def coarse_kernel(gx, gy, own, below, above, below2, above2, e3, beta3, w3, v3, root3, beta4, w4, v4, root4, rsum, csum, rz, cz, fine3):
    size_x, width = 2 * gx, 2 * gy
    for ref in (beta3, w3, v3, root3, beta4, w4, v4):
        ref[...] = jnp.zeros_like(ref)

    def prepare(x, row, t):
        n = t.shape[0]
        root_x, inv_x = roots_of(four_fields(t, width))
        root3[x + OFF3, pl.ds(row, n), :] = root_x
        beta3[x + OFF3, pl.ds(8 + row, n), :] = TAU * t * inv_x

    def setup(x):
        prepare(x, 4, below2[x])
        prepare(x, 8, below[x])
        prepare(x, 24, own[x])
        prepare(x, 40, above[x])
        prepare(x, 56, above2[x])

    loop(0, size_x, setup, 4)

    def smooth(x):
        for r, n in chunks(64, 32):
            mid, total = around_whole(beta3, x, 8 + r, n, width)
            w3[x, pl.ds(8 + r, n), :] = jnp.where(root3[x, pl.ds(r, n), :] > 0.0, 1.2 * mid + TAU * total, 0.0)

    loop(OFF3, size_x + OFF3, smooth, 4)
    restrict_whole(size_x, OFF3, width, w3, beta3, root3, rsum, csum, rz, cz)
    t = mm(((rz[...], pair_lanes(width, 0, gy, 0, 0.5)), (cz[...], pair_lanes(width, 0, gy, 64, 0.125))))
    for x in range(gx):
        t_x = t[x * 32 : (x + 1) * 32]
        root_x, inv_x = roots_of(jnp.where(lane_of(32) < 4 * gy, lane_roll(t_x, 64), 0.0))
        root4[x + 1] = root_x
        beta4[x + 1, pl.ds(8, 32), :] = TAU * t_x * inv_x
        w4[x + 1, pl.ds(8, 32), :] = TAU * t_x * inv_x
    here, there = w4, v4
    for step in range(COARSE_ITERS - 1):
        relax_whole(1, gx, 0, 32, gy, here, there, beta4, root4, gx)
        here, there = there, here

    e4 = [here[x + 1, pl.ds(16, 16), :] * inverse(root4[x + 1, pl.ds(8, 16), :]) for x in range(gx)]
    e4 = mm(((jnp.concatenate(e4, axis=0), repeat_lanes(gy, width)),))
    for x in range(gx):
        unfold_rows(fine3, x, 16, e4[x * 16 : (x + 1) * 16])
        for i in range(2):
            at = 2 * x + i + OFF3
            w3[at, pl.ds(24, 32), :] = w3[at, pl.ds(24, 32), :] + root3[at, pl.ds(16, 32), :] * fine3[x]
    relax_whole(OFF3, size_x, 16, 32, width, w3, v3, beta3, root3, 4)
    relax_whole(OFF3, size_x, 16, 32, width, v3, w3, beta3, root3, 4)

    first3 = 2 * position("gx") - 2 + OFF3
    for k in range(6):
        e3[k] = w3[first3 + k, pl.ds(28, 24), :] * inverse(root3[first3 + k, pl.ds(20, 24), :])


def up_kernel(gy, e3, b2, zlo2, zhi2, kept1, kept0, out, beta2, root2, w2, v2, fine2, w1b, v1, w0b, v0, fine1, fine0, turned):
    w1, beta1, root1 = thirds(kept1)
    w0, beta0, root0 = thirds(kept0)
    for ref in (w2, v2):
        ref[...] = jnp.zeros_like(ref)

    def prepare(x, row, t):
        n = t.shape[0]
        root_x, inv_x = roots_of(four_fields(t, Y2))
        root2[x, pl.ds(row, n), :] = root_x
        beta2[x, pl.ds(8 + row, n), :] = TAU * t * inv_x

    def setup(x):
        beta2[x, pl.ds(0, 8), :] = jnp.zeros((8, LANES), F32)
        beta2[x, pl.ds(56, 8), :] = jnp.zeros((8, LANES), F32)
        prepare(x, 0, zlo2[x])
        prepare(x, 8, b2[x])
        prepare(x, 40, zhi2[x])

    loop(0, 4 + 2 * H2, setup, 7)

    repeat = repeat_local(2 * gy, 2 * position("gy") - 2, Y2, 1)
    e = mm(((jnp.concatenate([e3[k] for k in range(6)], axis=0), repeat),))
    for k in range(6):
        unfold_rows(fine2, k, 24, e[k * 24 : (k + 1) * 24])
    for x in range(1, 13):
        mid, total = around(beta2, x, 8, 48)
        root_x = root2[x]
        add = root_x * fine2[(x - 1) // 2]
        w2[x, pl.ds(8, 48), :] = jnp.where(root_x > 0.0, 1.2 * mid + TAU * total + add, 0.0)
    for src, dst, begin, end in ((w2, v2, 2, 12), (v2, w2, 3, 11)):
        for x in range(begin, end):
            mid, total = around(src, x, 8, 48)
            dst[x, pl.ds(8, 48), :] = jacobi(root2[x] > 0.0, mid, beta2[x, pl.ds(8, 48), :], total)

    u2 = repeat_local(Y2, 2, Y1, 0)
    for ref in (w1b, v1):
        for row in (0, 88):
            ref[:, pl.ds(row, 8), :] = jnp.zeros((20, 8, LANES), F32)
    for ref in (w0b, v0):
        for row in (0, 152):
            ref[:, pl.ds(row, 8), :] = jnp.zeros((20, 8, LANES), F32)
    for k in range(0, 8, 4):
        e2 = [w2[x, pl.ds(12, 40), :] * inverse(root2[x, pl.ds(4, 40), :]) for x in range(k + 3, k + 7)]
        e = mm(((jnp.concatenate(e2, axis=0), u2),))
        for i in range(4):
            unfold_rows(fine1, k + i, 40, e[i * 40 : (i + 1) * 40])
    for x in range(3, 17):
        w1b[x, pl.ds(8, 80), :] = w1[x, pl.ds(8, 80), :] + root1[x, pl.ds(0, 80), :] * fine1[x // 2 - 1]

    def relax1(src, dst, begin, end):
        def body(x):
            for r, n in chunks(80, 40):
                mid, total = around(src, x, 8 + r, n)
                live = root1[x, pl.ds(r, n), :] > 0.0
                dst[x, pl.ds(8 + r, n), :] = jacobi(live, mid, beta1[x, pl.ds(8 + r, n), :], total)

        loop(begin, end, body, end - begin)

    relax1(w1b, v1, 4, 16)
    relax1(v1, w1b, 5, 15)

    u1 = repeat_local(Y1, H1, Y0, HY0)
    for k in range(0, 10, 2):
        e = [w1b[x, pl.ds(12, 72), :] * inverse(root1[x, pl.ds(4, 72), :]) for x in (k + 5, k + 6)]
        e = mm(((jnp.concatenate(e, axis=0), u1),))
        for i in range(2):
            unfold_rows(fine0, k + i, 72, e[i * 72 : (i + 1) * 72])

    def up0(k):
        for i in range(2):
            x = 2 * k + i
            for r, n in chunks(144, 48):
                add = root0[x + 1, pl.ds(8 + r, n), :] * fine0[k, pl.ds(r, n), :]
                w0b[x, pl.ds(8 + r, n), :] = w0[x + 1, pl.ds(16 + r, n), :] + add

    loop(0, 10, up0, 10)

    def first0(x):
        for r, n in chunks(144, 24):
            mid, total = around(w0b, x, 8 + r, n)
            live = root0[x + 1, pl.ds(8 + r, n), :] > 0.0
            v0[x, pl.ds(8 + r, n), :] = jacobi(live, mid, beta0[x + 1, pl.ds(16 + r, n), :], total)

    loop(1, 19, first0, 9)

    def last0(j):
        for slot in range(4):
            k = 4 * j + slot
            x = k + 2
            for r, n in chunks(128, 32):
                mid, total = around(v0, x, 16 + r, n)
                root_x = root0[x + 1, pl.ds(16 + r, n), :]
                new = jacobi(root_x > 0.0, mid, beta0[x + 1, pl.ds(24 + r, n), :], total)
                turned[slot, pl.ds(r, n), :] = new * inverse(root_x)
        for slot in range(4):
            t = turned[slot].T
            for f in range(4):
                out[f, 4 * j + slot] = t[f * Y0 + HY0 : f * Y0 + HY0 + 16]

    loop(0, 4, last0)


def call(kernel, args, outs, scratch):
    vmem = pl.BlockSpec(memory_space=pltpu.VMEM)
    sizes = [a.shape for a in args] + outs + scratch
    held = sum(4 * math.prod(s[:-2]) * -(-s[-2] // 8) * 8 * LANES for s in sizes if len(s) > 1)
    return pl.pallas_call(
        kernel,
        out_shape=[jax.ShapeDtypeStruct(s, F32) for s in outs],
        in_specs=[vmem] * len(args),
        out_specs=[vmem] * len(outs),
        scratch_shapes=[pltpu.VMEM(s, F32) for s in scratch],
        compiler_params=pltpu.CompilerParams(vmem_limit_bytes=held + 2 * 1024 * 1024),
    )(*args)


def swap(to_up, to_down, axis, far=1):
    n = lax.axis_size(axis)
    from_below = lax.ppermute(to_up, axis, [(i, i + far) for i in range(n - far)])
    from_above = lax.ppermute(to_down, axis, [(i + far, i) for i in range(n - far)])
    return from_below, from_above


def whole_plane(block):
    return lax.all_to_all(block, ("gx", "gy"), 0, 0, tiled=True)


def position(axis):
    return lax.axis_index(axis).astype(jnp.int32)


def shards(gx, gy, source, material_ids, material_table, roughness):
    anywhere = pl.BlockSpec(memory_space=pltpu.HBM)
    full, low, high = pl.pallas_call(
        prepare_kernel,
        out_shape=[jax.ShapeDtypeStruct((5, n, 16, LANES), F32) for n in (16, HX0, HX0)],
        in_specs=[anywhere] * 4,
        out_specs=[pl.BlockSpec(memory_space=pltpu.VMEM)] * 3,
        scratch_shapes=[
            pltpu.SMEM(material_table.shape, F32),
            pltpu.SMEM(material_ids.shape, jnp.int32),
            pltpu.VMEM(roughness.shape, F32),
            pltpu.SemaphoreType.DMA((4,)),
        ],
        compiler_params=pltpu.CompilerParams(vmem_limit_bytes=4 * 1024 * 1024),
    )(material_table, material_ids, source, roughness)
    xlo, xhi = swap(high, low, "gx")
    planes = 16 + 2 * HX0
    ysend_lo, ysend_hi = call(edge_kernel, (xlo, full, xhi), [(planes, 15, LANES)] * 2, [])
    ylo, yhi = swap(ysend_hi, ysend_lo, "gy")
    turned, zsend_lo, zsend_hi = call(
        turn_kernel,
        (xlo, full, xhi, ylo, yhi),
        [(planes, 128, LANES)] + [(planes, HZ0, LANES)] * 2,
        [(4, LANES, LANES)],
    )
    zlo, zhi = swap(zsend_hi, zsend_lo, "gz")

    depth = 128 + 2 * HZ0
    own1, ysend_lo, ysend_hi, kept0 = call(
        down0_kernel,
        (turned, zlo, zhi),
        [(8, 48, LANES)] + [(8, 6 * H1, LANES)] * 2 + [(3 * planes, depth + 16, LANES)],
        [(8, depth, LANES)] * 2 + [(4 * depth, LANES)] * 2 + [(8, LANES, LANES)],
    )
    ylo, yhi = swap(ysend_hi, ysend_lo, "gy")
    turned1, low, high = call(
        join1_kernel, (own1, ylo, yhi), [(8, 80, LANES)] + [(H1, 80, LANES)] * 2, [(4, LANES, LANES)]
    )
    xlo, xhi = swap(high, low, "gx")

    x1, x2, x3 = 8 + 2 * H1, 4 + 2 * H2, 2 * gx
    block, turned2, ysend_lo, ysend_hi, kept1 = call(
        down1_kernel,
        (turned1, xlo, xhi),
        [(3 * gx * gy, LANES), (6, 24, LANES)] + [(6, 6 * H2, LANES)] * 2 + [(3 * x1, 96, LANES)],
        [(8, 80, LANES)] * 2
        + [(320, LANES)] * 2
        + [(8, 56, LANES), (8, 40, LANES), (8, 56, LANES), (4, LANES, LANES)],
    )
    ylo, yhi = swap(ysend_hi, ysend_lo, "gy")
    got = whole_plane(block)
    turned2, low, high = call(
        join2_kernel, (turned2, ylo, yhi), [(4, 32, LANES)] + [(H2, 32, LANES)] * 2, [(4, LANES, LANES)]
    )
    xlo, xhi = swap(high, low, "gx")
    own3, lo4, hi4 = call(
        functools.partial(plane_kernel, gx, gy),
        (got,),
        [(x3, 16, LANES)] + [(x3, 4, LANES)] * 2,
        [(4, 3 * gx * gy, LANES), (2, LANES, LANES)],
    )
    below, above = swap(own3, own3, "gz")
    below2, above2 = swap(hi4, lo4, "gz", 2)
    b2, zsend_lo, zsend_hi = call(join3_kernel, (turned2, xlo, xhi), [(x2, 32, LANES)] + [(x2, 8, LANES)] * 2, [])
    zlo2, zhi2 = swap(zsend_hi, zsend_lo, "gz")
    (e3,) = call(
        functools.partial(coarse_kernel, gx, gy),
        (own3, below, above, below2, above2),
        [(6, 24, LANES)],
        [(x3 + 2 * OFF3, 80, LANES)] * 3
        + [(x3 + 2 * OFF3, 64, LANES)]
        + [(gx + 2, 48, LANES)] * 3
        + [(gx + 2, 32, LANES)]
        + [(gx, 64, LANES)] * 2
        + [(gx * 32, LANES)] * 2
        + [(gx, 32, LANES)],
    )

    (correction,) = call(
        functools.partial(up_kernel, gy),
        (e3, b2, zlo2, zhi2, kept1, kept0),
        [(4, 16, 16, LANES)],
        [(x2, 64, LANES), (x2, 48, LANES), (x2, 64, LANES), (x2, 64, LANES), (6, 48, LANES)]
        + [(x1, 96, LANES)] * 2
        + [(20, 160, LANES)] * 2
        + [(8, 80, LANES), (10, 144, LANES), (4, LANES, LANES)],
    )
    return correction


def solution(mesh):
    return jax.shard_map(
        functools.partial(shards, mesh.shape["gx"], mesh.shape["gy"]),
        mesh=mesh,
        in_specs=(P(None, "gx", "gy", "gz"), P("gx", "gy", "gz"), P(), P("gx", "gy", "gz")),
        out_specs=P(None, "gx", "gy", "gz"),
        check_vma=False,
    )
```

```python
import functools
import math

import jax
import jax.numpy as jnp
from jax import lax
from jax.experimental import pallas as pl
from jax.experimental.pallas import tpu as pltpu
from jax.sharding import PartitionSpec as P

F32 = jnp.float32
COARSE_ITERS = 8
TAU = 0.8 / 6.0
LANES = 128
HX0, HY0, HZ0 = 3, 3, 16
Y0 = 16 + 2 * HY0
H1, H2 = 6, 5
Y1, Y2 = 8 + 2 * H1, 4 + 2 * H2
OFF3 = 2


def halves(a):
    high = a.astype(jnp.bfloat16)
    return [high, (a - high.astype(F32)).astype(jnp.bfloat16)]


def mm(pairs):
    left, right = [], []
    for a, m in pairs:
        left += halves(a)
        right += [m, m]
    return jnp.dot(jnp.concatenate(left, axis=1), jnp.concatenate(right, axis=0), preferred_element_type=F32)


def lane_of(n):
    return lax.broadcasted_iota(jnp.int32, (n, LANES), 1)


def lane_roll(x, shift):
    return pltpu.roll(x, shift % LANES, 1) if shift % LANES else x


def around(ref, x, row, n):
    mid = ref[x, pl.ds(row, n), :]
    total = ref[x - 1, pl.ds(row, n), :] + ref[x + 1, pl.ds(row, n), :]
    total = total + (ref[x, pl.ds(row - 1, n), :] + ref[x, pl.ds(row + 1, n), :])
    return mid, total + (lane_roll(mid, 1) + lane_roll(mid, -1))


def around_whole(ref, x, row, n, width):
    mid = ref[x, pl.ds(row, n), :]
    total = ref[x - 1, pl.ds(row, n), :] + ref[x + 1, pl.ds(row, n), :]
    total = total + (ref[x, pl.ds(row - 1, n), :] + ref[x, pl.ds(row + 1, n), :])
    place = lane_of(n) & (width - 1)
    total = total + jnp.where(place == 0, 0.0, lane_roll(mid, 1))
    return mid, total + jnp.where(place == width - 1, 0.0, lane_roll(mid, -1))


def chunks(n, size):
    return [(r, min(size, n - r)) for r in range(0, n, size)]


def roots_of(c):
    live = c > 0.0
    inv = lax.rsqrt(jnp.where(live, c, 1.0))
    return jnp.where(live, c * inv, 0.0), jnp.where(live, inv, 0.0)


def inverse(root):
    live = root > 0.0
    return jnp.where(live, 1.0 / jnp.where(live, root, 1.0), 0.0)


def jacobi(live, mid, beta, total):
    return jnp.where(live, 0.2 * mid + beta + TAU * total, 0.0)


def bits(mask):
    return jnp.where(mask, 1.0, 0.0)


def pair_lanes(width, start, out_width, out_start, scale, fields=4, step=1):
    source = lax.broadcasted_iota(jnp.int32, (LANES, LANES), 0)
    out = lane_of(LANES) - out_start
    shift = out_width.bit_length() - 1
    first = (out >> shift) * (step * width) + start + 2 * (out & (out_width - 1))
    hit = ((source == first) | (source == first + 1)) & (out >= 0) & (out < fields * out_width)
    return (scale * bits(hit)).astype(jnp.bfloat16)


def repeat_lanes(width, out_width):
    source = lax.broadcasted_iota(jnp.int32, (LANES, LANES), 0)
    out = lane_of(LANES)
    return bits((source == out >> 1) & (out < 4 * out_width)).astype(jnp.bfloat16)


def repeat_local(width, shift, out_width, out_start, fields=4):
    source = lax.broadcasted_iota(jnp.int32, (LANES, LANES), 0)
    out = lane_of(LANES)
    field = bits(out >= out_width) + bits(out >= 2 * out_width) + bits(out >= 3 * out_width)
    field = field.astype(jnp.int32)
    row = shift + ((out - field * out_width - out_start) >> 1)
    hit = (source == field * width + row) & (row >= 0) & (row < width) & (out < fields * out_width)
    return bits(hit).astype(jnp.bfloat16)


def four_fields(t, width):
    lane = lane_of(t.shape[0])
    c = jnp.where(lane < 2 * width, lane_roll(t, -3 * width), lane_roll(t, -2 * width))
    c = jnp.where(lane < width, lane_roll(t, -4 * width), c)
    return jnp.where(lane < 4 * width, c, 0.0)


def residual(w, beta, root, x, row, n, mid_total):
    mid, total = mid_total
    root_x = root[x, pl.ds(row - 8, n), :]
    return root_x * ((1.0 / TAU) * beta[x, pl.ds(row, n), :] - 6.0 * mid + total), root_x * root_x


def thirds(ref):
    n = ref.shape[0] // 3
    return [ref.at[pl.ds(i * n, n)] for i in range(3)]


def loop(begin, end, body, unroll=1):
    def step(i, carry):
        body(i)
        return carry

    lax.fori_loop(begin, end, step, 0, unroll=unroll)


def fold_rows(ref, k, n):
    return ref[k, pl.ds(0, n, stride=2), :] + ref[k, pl.ds(1, n, stride=2), :]


def unfold_rows(ref, k, n, value):
    ref[k, pl.ds(0, n, stride=2), :] = value
    ref[k, pl.ds(1, n, stride=2), :] = value


def prepare_kernel(table_any, ids_any, source_any, roughness_any, full, low, high, table, ids, roughness, sems):
    copies = [
        pltpu.make_async_copy(table_any, table, sems.at[0]),
        pltpu.make_async_copy(ids_any, ids, sems.at[1]),
        pltpu.make_async_copy(roughness_any, roughness, sems.at[2]),
        pltpu.make_async_copy(source_any, full.at[pl.ds(0, 4)], sems.at[3]),
    ]
    for copy in copies:
        copy.start()
    for copy in copies[:3]:
        copy.wait()
    block = lane_of(8) >> 3
    for i in range(2):
        for j in range(2):
            along_z = jnp.zeros((8, LANES), F32)
            for k in range(16):
                along_z = jnp.where(block == k, table[ids[i, j, k]], along_z)
            for x in range(8 * i, 8 * i + 8):
                full[4, x, pl.ds(8 * j, 8), :] = roughness[x, pl.ds(8 * j, 8), :] * along_z
    copies[3].wait()
    for x in range(HX0):
        for f in range(5):
            low[f, x] = full[f, x]
            high[f, x] = full[f, 16 - HX0 + x]


def edge_kernel(xlo, full, xhi, ylo, yhi):
    def put(x, f, plane):
        ylo[x, pl.ds(f * HY0, HY0), :] = plane[0:HY0]
        yhi[x, pl.ds(f * HY0, HY0), :] = plane[16 - HY0 : 16]

    for x in range(HX0):
        for f in range(5):
            put(x, f, xlo[f, x])
            put(x + HX0 + 16, f, xhi[f, x])

    def own(x):
        for f in range(5):
            put(x + HX0, f, full[f, x])

    loop(0, 16, own, 16)


def turn_kernel(xlo, full, xhi, ylo, yhi, turned, zlo, zhi, stage):
    stage[...] = jnp.zeros_like(stage)

    def turn(x, slot, planes):
        for f in range(5):
            stage[slot, pl.ds(f * Y0 + HY0, 16), :] = planes[f]
            stage[slot, pl.ds(f * Y0, HY0), :] = ylo[x, pl.ds(f * HY0, HY0), :]
            stage[slot, pl.ds(f * Y0 + HY0 + 16, HY0), :] = yhi[x, pl.ds(f * HY0, HY0), :]
        t = stage[slot].T
        turned[x] = t
        zlo[x] = t[0:HZ0]
        zhi[x] = t[128 - HZ0 : 128]

    for x in range(HX0):
        turn(x, 0, [xlo[f, x] for f in range(5)])
        turn(x + HX0 + 16, 1, [xhi[f, x] for f in range(5)])

    def own(k):
        for slot in range(4):
            x = 4 * k + slot
            turn(x + HX0, slot, [full[f, x] for f in range(5)])

    loop(0, 4, own, 2)


def down0_kernel(turned, zlo, zhi, out, ylo, yhi, kept, rsum, csum, rz, cz, stage):
    planes = 16 + 2 * HX0
    depth = 128 + 2 * HZ0
    half = depth // 2
    w, beta, root = thirds(kept)
    qb = pair_lanes(Y0, HY0, 8, 0, 0.5)
    qc = pair_lanes(Y0, HY0, 8, 32, 0.125, 2, 3)

    def prepare(x, t, row, n):
        lane = lane_of(n)
        v = lane_roll(jnp.where(lane < 4 * Y0, 0.0, t), -4 * Y0)
        v = v + lane_roll(v, Y0)
        v = v + lane_roll(v, 2 * Y0)
        root_v, inv_v = roots_of(v)
        pressure = lane >= 3 * Y0
        root[x, pl.ds(row, n), :] = jnp.where(pressure, inv_v, root_v)
        beta[x, pl.ds(8 + row, n), :] = TAU * t * jnp.where(pressure, root_v, inv_v)

    def setup(x):
        for ref in (beta, w):
            ref[x, pl.ds(0, 8), :] = jnp.zeros((8, LANES), F32)
            ref[x, pl.ds(8 + depth, 8), :] = jnp.zeros((8, LANES), F32)
        prepare(x, zlo[x], 0, HZ0)
        for r, n in chunks(128, 32):
            prepare(x, turned[x, pl.ds(r, n), :], HZ0 + r, n)
        prepare(x, zhi[x], HZ0 + 128, HZ0)

    loop(0, planes, setup, 2)

    def smooth(x):
        for r, n in chunks(depth, 32):
            mid, total = around(beta, x, 8 + r, n)
            w[x, pl.ds(8 + r, n), :] = jnp.where(root[x, pl.ds(r, n), :] > 0.0, 1.2 * mid + TAU * total, 0.0)

    loop(1, planes - 1, smooth, 10)

    def restrict(k):
        for r, n in chunks(depth, 32):
            x = HX0 + 2 * k
            res_a, coef_a = residual(w, beta, root, x, 8 + r, n, around(w, x, 8 + r, n))
            res_b, coef_b = residual(w, beta, root, x + 1, 8 + r, n, around(w, x + 1, 8 + r, n))
            rsum[k, pl.ds(r, n), :] = res_a + res_b
            csum[k, pl.ds(r, n), :] = coef_a + coef_b

    loop(0, 8, restrict, 4)

    def fold(k):
        rz[pl.ds(k * half, half), :] = fold_rows(rsum, k, half)
        cz[pl.ds(k * half, half), :] = fold_rows(csum, k, half)

    for k in range(8):
        fold(k)
    stage[...] = jnp.zeros_like(stage)
    for k in range(0, 8, 2):
        both = mm(((rz[pl.ds(k * half, 2 * half), :], qb), (cz[pl.ds(k * half, 2 * half), :], qc)))
        for i in range(2):
            stage[k + i, pl.ds(0, half), :] = both[i * half : (i + 1) * half]
    for k in range(8):
        t = stage[k].T
        out[k] = t[0:48]
        for a in range(6):
            ylo[k, pl.ds(a * H1, H1), :] = t[a * 8 : a * 8 + H1]
            yhi[k, pl.ds(a * H1, H1), :] = t[a * 8 + 8 - H1 : a * 8 + 8]


def join1_kernel(own, ylo, yhi, turned, low, high, stage):
    stage[...] = jnp.zeros_like(stage)
    for x in range(8):
        slot = x % 4
        for a in range(6):
            stage[slot, pl.ds(a * Y1 + H1, 8), :] = own[x, pl.ds(a * 8, 8), :]
            stage[slot, pl.ds(a * Y1, H1), :] = ylo[x, pl.ds(a * H1, H1), :]
            stage[slot, pl.ds(a * Y1 + H1 + 8, H1), :] = yhi[x, pl.ds(a * H1, H1), :]
        t = stage[slot].T[0:80]
        turned[x] = t
        if x < H1:
            low[x] = t
        if x >= 8 - H1:
            high[x - 8 + H1] = t


def down1_kernel(own, xlo, xhi, raw2, turned2, ylo2, yhi2, kept, rsum, csum, rz, cz, stage):
    w, beta, root = thirds(kept)

    def prepare(x, t):
        root_x, inv_x = roots_of(four_fields(t, Y1))
        root[x, pl.ds(0, 80), :] = root_x
        beta[x, pl.ds(8, 80), :] = TAU * t * inv_x
        for ref in (beta, w):
            ref[x, pl.ds(0, 8), :] = jnp.zeros((8, LANES), F32)
            ref[x, pl.ds(88, 8), :] = jnp.zeros((8, LANES), F32)

    for x in range(H1):
        prepare(x, xlo[x])
        prepare(x + H1 + 8, xhi[x])
    for x in range(8):
        prepare(x + H1, own[x])

    def smooth(x):
        for r, n in chunks(80, 40):
            mid, total = around(beta, x, 8 + r, n)
            w[x, pl.ds(8 + r, n), :] = jnp.where(root[x, pl.ds(r, n), :] > 0.0, 1.2 * mid + TAU * total, 0.0)

    loop(1, 19, smooth, 9)

    def restrict(k):
        for r, n in chunks(80, 40):
            x = 2 + 2 * k
            res_a, coef_a = residual(w, beta, root, x, 8 + r, n, around(w, x, 8 + r, n))
            res_b, coef_b = residual(w, beta, root, x + 1, 8 + r, n, around(w, x + 1, 8 + r, n))
            rsum[k, pl.ds(r, n), :] = res_a + res_b
            csum[k, pl.ds(r, n), :] = coef_a + coef_b

    loop(0, 8, restrict, 4)
    for k in range(8):
        rz[pl.ds(k * 40, 40), :] = fold_rows(rsum, k, 40)
        cz[pl.ds(k * 40, 40), :] = fold_rows(csum, k, 40)

    t2 = mm(((rz[...], pair_lanes(Y1, 2, 8, 0, 0.5)), (cz[...], pair_lanes(Y1, 2, 8, 32, 0.125, 2, 3))))
    stage[...] = jnp.zeros_like(stage)
    for x in range(8):
        t = t2[x * 40 : (x + 1) * 40]
        raw2[x] = t
        if 1 <= x < 7:
            stage[x % 4, pl.ds(0, 40), :] = t
            flat = stage[x % 4].T
            for a in range(6):
                turned2[x - 1, pl.ds(a * 4, 4), :] = flat[a * 8 + 2 : a * 8 + 6]
                yhi2[x - 1, pl.ds(a * H2, H2), :] = flat[a * 8 + 1 : a * 8 + 1 + H2]
                ylo2[x - 1, pl.ds(a * H2, H2), :] = flat[a * 8 + 2 : a * 8 + 2 + H2]


def down2_kernel(raw2, block, rsum, csum, beta2, root2, w2, stage):
    for x in range(8):
        root_x, inv_x = roots_of(four_fields(raw2[x], 8))
        root2[x] = root_x
        beta2[x, pl.ds(8, 40), :] = TAU * raw2[x] * inv_x
        for ref in (beta2, w2):
            ref[x, pl.ds(0, 8), :] = jnp.zeros((8, LANES), F32)
            ref[x, pl.ds(48, 8), :] = jnp.zeros((8, LANES), F32)
    for x in range(1, 7):
        mid, total = around(beta2, x, 8, 40)
        w2[x, pl.ds(8, 40), :] = jnp.where(root2[x] > 0.0, 1.2 * mid + TAU * total, 0.0)
    for k in range(2):
        x = 2 + 2 * k
        res, coef = jnp.zeros((32, LANES), F32), jnp.zeros((32, LANES), F32)
        for i in range(2):
            res_i, coef_i = residual(w2, beta2, root2, x + i, 12, 32, around(w2, x + i, 12, 32))
            res, coef = res + res_i, coef + coef_i
        rsum[k] = res
        csum[k] = coef
    rows = [jnp.concatenate([fold_rows(ref, k, 16) for k in range(2)], axis=0) for ref in (rsum, csum)]
    t3 = mm(((rows[0], pair_lanes(8, 2, 2, 0, 0.5)), (rows[1], pair_lanes(8, 2, 2, 8, 0.125, 2, 3))))

    stage[0, pl.ds(0, 32), :] = t3
    stage[0, pl.ds(32, 96), :] = jnp.zeros((96, LANES), F32)
    flat = stage[0].T[0:16]
    lane = lane_of(1)
    turns = [lane_roll(flat, 32 * g) for g in range(4)]
    packed = []
    for r in range(3):
        row = turns[0][4 * r : 4 * r + 1]
        for g in range(1, 4):
            row = jnp.where((lane >= 32 * g) & (lane < 32 * g + 32), turns[g][4 * r + g : 4 * r + g + 1], row)
        packed.append(row)
    packed = jnp.concatenate(packed, axis=0)
    for i in range(block.shape[0]):
        block[i] = packed


def join2_kernel(own, ylo, yhi, turned, low, high, stage):
    stage[...] = jnp.zeros_like(stage)
    for x in range(6):
        slot = x % 4
        for a in range(6):
            stage[slot, pl.ds(a * Y2 + H2, 4), :] = own[x, pl.ds(a * 4, 4), :]
            stage[slot, pl.ds(a * Y2, H2), :] = ylo[x, pl.ds(a * H2, H2), :]
            stage[slot, pl.ds(a * Y2 + H2 + 4, H2), :] = yhi[x, pl.ds(a * H2, H2), :]
        t = stage[slot].T[4:36]
        if 1 <= x < 5:
            turned[x - 1] = t
        if x < 5:
            high[x] = t
        if x >= 1:
            low[x - 1] = t


def plane_kernel(gx, gy, got, own2, xlo2, xhi2, own, lo4, hi4, b2, up, down, turns, stage):
    width = 2 * gy
    size_x = 2 * gx
    for x in range(4 + 2 * H2):
        t = xlo2[x] if x < H2 else own2[x - H2] if x < H2 + 4 else xhi2[x - H2 - 4]
        b2[x] = t
        up[size_x + x // 2, pl.ds(8 * (x % 2), 8), :] = t[24:32]
        down[size_x + x // 2, pl.ds(8 * (x % 2), 8), :] = t[0:8]
    for i in range(gx * gy):
        turns[0, pl.ds(3 * i, 3), :] = got[i]
    stage[...] = jnp.zeros_like(stage)
    for s in range(1, 4):
        turns[s] = lane_roll(turns[0], 32 * s)
    lane = lane_of(gy)
    for h in range(-(-gx // 4)):
        for i in range(12):
            r, g = i // 4, i % 4
            row = jnp.zeros((gy, LANES), F32)
            for q in range(min(4, gx - 4 * h)):
                part = turns[(q - g) % 4, pl.ds((4 * h + q) * gy * 3 + r, gy, stride=3), :]
                row = jnp.where((lane >= 32 * q) & (lane < 32 * q + 32), part, row)
            stage[h, pl.ds((i // 2) * width + i % 2, gy, stride=2), :] = row
        t = stage[h].T
        for q in range(min(4, gx - 4 * h)):
            for x in range(2):
                at = 2 * (4 * h + q) + x
                rows = t[32 * q + 16 * x : 32 * q + 16 * x + 16]
                own[at] = rows
                up[at] = rows
                down[at] = rows
                lo4[at] = rows[0:4]
                hi4[at] = rows[12:16]


def restrict_whole(size_x, off, width, w, beta, root, rsum, csum, rz, cz):
    def body(k):
        for r, n in chunks(64, 32):
            x = 2 * k + off
            res_a, coef_a = residual(w, beta, root, x, 8 + r, n, around_whole(w, x, 8 + r, n, width))
            res_b, coef_b = residual(w, beta, root, x + 1, 8 + r, n, around_whole(w, x + 1, 8 + r, n, width))
            rsum[k, pl.ds(r, n), :] = res_a + res_b
            csum[k, pl.ds(r, n), :] = coef_a + coef_b

    loop(0, size_x // 2, body, 4 if size_x % 8 == 0 else 2)
    for k in range(size_x // 2):
        rz[pl.ds(k * 32, 32), :] = fold_rows(rsum, k, 32)
        cz[pl.ds(k * 32, 32), :] = fold_rows(csum, k, 32)


def relax_whole(first, planes, begin, depth, width, src, dst, beta, root, unroll):
    def body(x):
        for r, n in chunks(depth, 32):
            r = r + begin
            mid, total = around_whole(src, x, 8 + r, n, width)
            live = root[x, pl.ds(r, n), :] > 0.0
            dst[x, pl.ds(8 + r, n), :] = jacobi(live, mid, beta[x, pl.ds(8 + r, n), :], total)

    loop(first, first + planes, body, unroll)


def coarse_kernel(gx, gy, own, below, above, below2, above2, e3, beta3, w3, v3, root3, beta4, w4, v4, root4, rsum, csum, rz, cz, fine3):
    size_x, width = 2 * gx, 2 * gy
    for ref in (beta3, w3, v3, root3, beta4, w4, v4):
        ref[...] = jnp.zeros_like(ref)

    def prepare(x, row, t):
        n = t.shape[0]
        root_x, inv_x = roots_of(four_fields(t, width))
        root3[x + OFF3, pl.ds(row, n), :] = root_x
        beta3[x + OFF3, pl.ds(8 + row, n), :] = TAU * t * inv_x

    def setup(x):
        prepare(x, 4, below2[x])
        prepare(x, 8, below[x])
        prepare(x, 24, own[x])
        prepare(x, 40, above[x])
        prepare(x, 56, above2[x])

    loop(0, size_x, setup, 4)

    def smooth(x):
        for r, n in chunks(64, 32):
            mid, total = around_whole(beta3, x, 8 + r, n, width)
            w3[x, pl.ds(8 + r, n), :] = jnp.where(root3[x, pl.ds(r, n), :] > 0.0, 1.2 * mid + TAU * total, 0.0)

    loop(OFF3, size_x + OFF3, smooth, 4)
    restrict_whole(size_x, OFF3, width, w3, beta3, root3, rsum, csum, rz, cz)
    t = mm(((rz[...], pair_lanes(width, 0, gy, 0, 0.5)), (cz[...], pair_lanes(width, 0, gy, 64, 0.125))))
    for x in range(gx):
        t_x = t[x * 32 : (x + 1) * 32]
        root_x, inv_x = roots_of(jnp.where(lane_of(32) < 4 * gy, lane_roll(t_x, 64), 0.0))
        root4[x + 1] = root_x
        beta4[x + 1, pl.ds(8, 32), :] = TAU * t_x * inv_x
        w4[x + 1, pl.ds(8, 32), :] = TAU * t_x * inv_x
    here, there = w4, v4
    for step in range(COARSE_ITERS - 1):
        relax_whole(1, gx, 0, 32, gy, here, there, beta4, root4, gx)
        here, there = there, here

    e4 = [here[x + 1, pl.ds(16, 16), :] * inverse(root4[x + 1, pl.ds(8, 16), :]) for x in range(gx)]
    e4 = mm(((jnp.concatenate(e4, axis=0), repeat_lanes(gy, width)),))
    for x in range(gx):
        unfold_rows(fine3, x, 16, e4[x * 16 : (x + 1) * 16])
        for i in range(2):
            at = 2 * x + i + OFF3
            w3[at, pl.ds(24, 32), :] = w3[at, pl.ds(24, 32), :] + root3[at, pl.ds(16, 32), :] * fine3[x]
    relax_whole(OFF3, size_x, 16, 32, width, w3, v3, beta3, root3, 4)
    relax_whole(OFF3, size_x, 16, 32, width, v3, w3, beta3, root3, 4)

    first3 = 2 * position("gx") - 2 + OFF3
    for k in range(6):
        e3[k] = w3[first3 + k, pl.ds(28, 24), :] * inverse(root3[first3 + k, pl.ds(20, 24), :])


def up_kernel(gx, gy, e3, b2, below, above, kept1, kept0, out, beta2, root2, w2, v2, fine2, w1b, v1, w0b, v0, fine1, fine0, turned):
    w1, beta1, root1 = thirds(kept1)
    w0, beta0, root0 = thirds(kept0)
    for ref in (w2, v2):
        ref[...] = jnp.zeros_like(ref)

    def prepare(x, row, t):
        n = t.shape[0]
        root_x, inv_x = roots_of(four_fields(t, Y2))
        root2[x, pl.ds(row, n), :] = root_x
        beta2[x, pl.ds(8 + row, n), :] = TAU * t * inv_x

    def setup(k):
        for i in range(2):
            x = 2 * k + i
            beta2[x, pl.ds(0, 8), :] = jnp.zeros((8, LANES), F32)
            beta2[x, pl.ds(56, 8), :] = jnp.zeros((8, LANES), F32)
            prepare(x, 0, below[2 * gx + k, pl.ds(8 * i, 8), :])
            prepare(x, 8, b2[x])
            prepare(x, 40, above[2 * gx + k, pl.ds(8 * i, 8), :])

    loop(0, 2 + H2, setup, 7)

    repeat = repeat_local(2 * gy, 2 * position("gy") - 2, Y2, 1)
    e = mm(((jnp.concatenate([e3[k] for k in range(6)], axis=0), repeat),))
    for k in range(6):
        unfold_rows(fine2, k, 24, e[k * 24 : (k + 1) * 24])
    for x in range(1, 13):
        mid, total = around(beta2, x, 8, 48)
        root_x = root2[x]
        add = root_x * fine2[(x - 1) // 2]
        w2[x, pl.ds(8, 48), :] = jnp.where(root_x > 0.0, 1.2 * mid + TAU * total + add, 0.0)
    for src, dst, begin, end in ((w2, v2, 2, 12), (v2, w2, 3, 11)):
        for x in range(begin, end):
            mid, total = around(src, x, 8, 48)
            dst[x, pl.ds(8, 48), :] = jacobi(root2[x] > 0.0, mid, beta2[x, pl.ds(8, 48), :], total)

    u2 = repeat_local(Y2, 2, Y1, 0)
    for ref in (w1b, v1):
        for row in (0, 88):
            ref[:, pl.ds(row, 8), :] = jnp.zeros((20, 8, LANES), F32)
    for ref in (w0b, v0):
        for row in (0, 152):
            ref[:, pl.ds(row, 8), :] = jnp.zeros((20, 8, LANES), F32)
    for k in range(0, 8, 4):
        e2 = [w2[x, pl.ds(12, 40), :] * inverse(root2[x, pl.ds(4, 40), :]) for x in range(k + 3, k + 7)]
        e = mm(((jnp.concatenate(e2, axis=0), u2),))
        for i in range(4):
            unfold_rows(fine1, k + i, 40, e[i * 40 : (i + 1) * 40])
    for x in range(3, 17):
        w1b[x, pl.ds(8, 80), :] = w1[x, pl.ds(8, 80), :] + root1[x, pl.ds(0, 80), :] * fine1[x // 2 - 1]

    def relax1(src, dst, begin, end):
        def body(x):
            for r, n in chunks(80, 40):
                mid, total = around(src, x, 8 + r, n)
                live = root1[x, pl.ds(r, n), :] > 0.0
                dst[x, pl.ds(8 + r, n), :] = jacobi(live, mid, beta1[x, pl.ds(8 + r, n), :], total)

        loop(begin, end, body, end - begin)

    relax1(w1b, v1, 4, 16)
    relax1(v1, w1b, 5, 15)

    u1 = repeat_local(Y1, H1, Y0, HY0)
    for k in range(0, 10, 2):
        e = [w1b[x, pl.ds(12, 72), :] * inverse(root1[x, pl.ds(4, 72), :]) for x in (k + 5, k + 6)]
        e = mm(((jnp.concatenate(e, axis=0), u1),))
        for i in range(2):
            unfold_rows(fine0, k + i, 72, e[i * 72 : (i + 1) * 72])

    def up0(k):
        for i in range(2):
            x = 2 * k + i
            for r, n in chunks(144, 48):
                add = root0[x + 1, pl.ds(8 + r, n), :] * fine0[k, pl.ds(r, n), :]
                w0b[x, pl.ds(8 + r, n), :] = w0[x + 1, pl.ds(16 + r, n), :] + add

    loop(0, 10, up0, 10)

    def first0(x):
        for r, n in chunks(144, 24):
            mid, total = around(w0b, x, 8 + r, n)
            live = root0[x + 1, pl.ds(8 + r, n), :] > 0.0
            v0[x, pl.ds(8 + r, n), :] = jacobi(live, mid, beta0[x + 1, pl.ds(16 + r, n), :], total)

    loop(1, 19, first0, 9)

    def last0(j):
        for slot in range(4):
            k = 4 * j + slot
            x = k + 2
            for r, n in chunks(128, 32):
                mid, total = around(v0, x, 16 + r, n)
                root_x = root0[x + 1, pl.ds(16 + r, n), :]
                new = jacobi(root_x > 0.0, mid, beta0[x + 1, pl.ds(24 + r, n), :], total)
                turned[slot, pl.ds(r, n), :] = new * inverse(root_x)
        for slot in range(4):
            t = turned[slot].T
            for f in range(4):
                out[f, 4 * j + slot] = t[f * Y0 + HY0 : f * Y0 + HY0 + 16]

    loop(0, 4, last0)


def call(kernel, args, outs, scratch):
    vmem = pl.BlockSpec(memory_space=pltpu.VMEM)
    sizes = [a.shape for a in args] + outs + scratch
    held = sum(4 * math.prod(s[:-2]) * -(-s[-2] // 8) * 8 * LANES for s in sizes if len(s) > 1)
    return pl.pallas_call(
        kernel,
        out_shape=[jax.ShapeDtypeStruct(s, F32) for s in outs],
        in_specs=[vmem] * len(args),
        out_specs=[vmem] * len(outs),
        scratch_shapes=[pltpu.VMEM(s, F32) for s in scratch],
        compiler_params=pltpu.CompilerParams(vmem_limit_bytes=held + 2 * 1024 * 1024),
    )(*args)


def swap(to_up, to_down, axis, far=1):
    n = lax.axis_size(axis)
    from_below = lax.ppermute(to_up, axis, [(i, i + far) for i in range(n - far)])
    from_above = lax.ppermute(to_down, axis, [(i + far, i) for i in range(n - far)])
    return from_below, from_above


def whole_plane(block):
    return lax.all_to_all(block, ("gx", "gy"), 0, 0, tiled=True)


def position(axis):
    return lax.axis_index(axis).astype(jnp.int32)


def shards(gx, gy, source, material_ids, material_table, roughness):
    anywhere = pl.BlockSpec(memory_space=pltpu.HBM)
    full, low, high = pl.pallas_call(
        prepare_kernel,
        out_shape=[jax.ShapeDtypeStruct((5, n, 16, LANES), F32) for n in (16, HX0, HX0)],
        in_specs=[anywhere] * 4,
        out_specs=[pl.BlockSpec(memory_space=pltpu.VMEM)] * 3,
        scratch_shapes=[
            pltpu.SMEM(material_table.shape, F32),
            pltpu.SMEM(material_ids.shape, jnp.int32),
            pltpu.VMEM(roughness.shape, F32),
            pltpu.SemaphoreType.DMA((4,)),
        ],
        compiler_params=pltpu.CompilerParams(vmem_limit_bytes=4 * 1024 * 1024),
    )(material_table, material_ids, source, roughness)
    xlo, xhi = swap(high, low, "gx")
    planes = 16 + 2 * HX0
    ysend_lo, ysend_hi = call(edge_kernel, (xlo, full, xhi), [(planes, 15, LANES)] * 2, [])
    ylo, yhi = swap(ysend_hi, ysend_lo, "gy")
    turned, zsend_lo, zsend_hi = call(
        turn_kernel,
        (xlo, full, xhi, ylo, yhi),
        [(planes, 128, LANES)] + [(planes, HZ0, LANES)] * 2,
        [(4, LANES, LANES)],
    )
    zlo, zhi = swap(zsend_hi, zsend_lo, "gz")

    depth = 128 + 2 * HZ0
    own1, ysend_lo, ysend_hi, kept0 = call(
        down0_kernel,
        (turned, zlo, zhi),
        [(8, 48, LANES)] + [(8, 6 * H1, LANES)] * 2 + [(3 * planes, depth + 16, LANES)],
        [(8, depth, LANES)] * 2 + [(4 * depth, LANES)] * 2 + [(8, LANES, LANES)],
    )
    ylo, yhi = swap(ysend_hi, ysend_lo, "gy")
    turned1, low, high = call(
        join1_kernel, (own1, ylo, yhi), [(8, 80, LANES)] + [(H1, 80, LANES)] * 2, [(4, LANES, LANES)]
    )
    xlo, xhi = swap(high, low, "gx")

    x1, x2, x3 = 8 + 2 * H1, 4 + 2 * H2, 2 * gx
    raw2, turned2, ysend_lo, ysend_hi, kept1 = call(
        down1_kernel,
        (turned1, xlo, xhi),
        [(8, 40, LANES), (6, 24, LANES)] + [(6, 6 * H2, LANES)] * 2 + [(3 * x1, 96, LANES)],
        [(8, 80, LANES)] * 2
        + [(320, LANES)] * 2
        + [(4, LANES, LANES)],
    )
    ylo, yhi = swap(ysend_hi, ysend_lo, "gy")
    (block,) = call(
        down2_kernel,
        (raw2,),
        [(gx * gy, 3, LANES)],
        [(2, 32, LANES)] * 2 + [(8, 56, LANES), (8, 40, LANES), (8, 56, LANES), (1, LANES, LANES)],
    )
    got = whole_plane(block)
    turned2, low, high = call(
        join2_kernel, (turned2, ylo, yhi), [(4, 32, LANES)] + [(H2, 32, LANES)] * 2, [(4, LANES, LANES)]
    )
    xlo, xhi = swap(high, low, "gx")
    own3, lo4, hi4, b2, to_up, to_down = call(
        functools.partial(plane_kernel, gx, gy),
        (got, turned2, xlo, xhi),
        [(x3, 16, LANES)] + [(x3, 4, LANES)] * 2 + [(x2, 32, LANES)] + [(x3 + x2 // 2, 16, LANES)] * 2,
        [(4, 3 * gx * gy, LANES), (2, LANES, LANES)],
    )
    below, above = swap(to_up, to_down, "gz")
    below2, above2 = swap(hi4, lo4, "gz", 2)
    (e3,) = call(
        functools.partial(coarse_kernel, gx, gy),
        (own3, below, above, below2, above2),
        [(6, 24, LANES)],
        [(x3 + 2 * OFF3, 80, LANES)] * 3
        + [(x3 + 2 * OFF3, 64, LANES)]
        + [(gx + 2, 48, LANES)] * 3
        + [(gx + 2, 32, LANES)]
        + [(gx, 64, LANES)] * 2
        + [(gx * 32, LANES)] * 2
        + [(gx, 32, LANES)],
    )

    (correction,) = call(
        functools.partial(up_kernel, gx, gy),
        (e3, b2, below, above, kept1, kept0),
        [(4, 16, 16, LANES)],
        [(x2, 64, LANES), (x2, 48, LANES), (x2, 64, LANES), (x2, 64, LANES), (6, 48, LANES)]
        + [(x1, 96, LANES)] * 2
        + [(20, 160, LANES)] * 2
        + [(8, 80, LANES), (10, 144, LANES), (4, LANES, LANES)],
    )
    return correction


def solution(mesh):
    return jax.shard_map(
        functools.partial(shards, mesh.shape["gx"], mesh.shape["gy"]),
        mesh=mesh,
        in_specs=(P(None, "gx", "gy", "gz"), P("gx", "gy", "gz"), P(), P("gx", "gy", "gz")),
        out_specs=P(None, "gx", "gy", "gz"),
        check_vma=False,
    )
```

```python
import functools
import math

import jax
import jax.numpy as jnp
from jax import lax
from jax.experimental import pallas as pl
from jax.experimental.pallas import tpu as pltpu
from jax.sharding import PartitionSpec as P

F32 = jnp.float32
COARSE_ITERS = 8
TAU = 0.8 / 6.0
LANES = 128
HX0, HY0, HZ0 = 3, 3, 16
Y0 = 16 + 2 * HY0
H1, H2 = 6, 5
Y1, Y2 = 8 + 2 * H1, 4 + 2 * H2
OFF3 = 2


def halves(a):
    high = a.astype(jnp.bfloat16)
    return [high, (a - high.astype(F32)).astype(jnp.bfloat16)]


def mm(pairs):
    left, right = [], []
    for a, m in pairs:
        left += halves(a)
        right += [m, m]
    return jnp.dot(jnp.concatenate(left, axis=1), jnp.concatenate(right, axis=0), preferred_element_type=F32)


def lane_of(n):
    return lax.broadcasted_iota(jnp.int32, (n, LANES), 1)


def lane_roll(x, shift):
    return pltpu.roll(x, shift % LANES, 1) if shift % LANES else x


def around(ref, x, row, n):
    mid = ref[x, pl.ds(row, n), :]
    total = ref[x - 1, pl.ds(row, n), :] + ref[x + 1, pl.ds(row, n), :]
    total = total + (ref[x, pl.ds(row - 1, n), :] + ref[x, pl.ds(row + 1, n), :])
    return mid, total + (lane_roll(mid, 1) + lane_roll(mid, -1))


def around_whole(ref, x, row, n, width):
    mid = ref[x, pl.ds(row, n), :]
    total = ref[x - 1, pl.ds(row, n), :] + ref[x + 1, pl.ds(row, n), :]
    total = total + (ref[x, pl.ds(row - 1, n), :] + ref[x, pl.ds(row + 1, n), :])
    place = lane_of(n) & (width - 1)
    total = total + jnp.where(place == 0, 0.0, lane_roll(mid, 1))
    return mid, total + jnp.where(place == width - 1, 0.0, lane_roll(mid, -1))


def chunks(n, size):
    return [(r, min(size, n - r)) for r in range(0, n, size)]


def roots_of(c):
    live = c > 0.0
    inv = lax.rsqrt(jnp.where(live, c, 1.0))
    return jnp.where(live, c * inv, 0.0), jnp.where(live, inv, 0.0)


def inverse(root):
    live = root > 0.0
    return jnp.where(live, 1.0 / jnp.where(live, root, 1.0), 0.0)


def jacobi(live, mid, beta, total):
    return jnp.where(live, 0.2 * mid + beta + TAU * total, 0.0)


def bits(mask):
    return jnp.where(mask, 1.0, 0.0)


def pair_lanes(width, start, out_width, out_start, scale, fields=4, step=1):
    source = lax.broadcasted_iota(jnp.int32, (LANES, LANES), 0)
    out = lane_of(LANES) - out_start
    shift = out_width.bit_length() - 1
    first = (out >> shift) * (step * width) + start + 2 * (out & (out_width - 1))
    hit = ((source == first) | (source == first + 1)) & (out >= 0) & (out < fields * out_width)
    return (scale * bits(hit)).astype(jnp.bfloat16)


def repeat_lanes(width, out_width):
    source = lax.broadcasted_iota(jnp.int32, (LANES, LANES), 0)
    out = lane_of(LANES)
    return bits((source == out >> 1) & (out < 4 * out_width)).astype(jnp.bfloat16)


def repeat_local(width, shift, out_width, out_start, fields=4):
    source = lax.broadcasted_iota(jnp.int32, (LANES, LANES), 0)
    out = lane_of(LANES)
    field = bits(out >= out_width) + bits(out >= 2 * out_width) + bits(out >= 3 * out_width)
    field = field.astype(jnp.int32)
    row = shift + ((out - field * out_width - out_start) >> 1)
    hit = (source == field * width + row) & (row >= 0) & (row < width) & (out < fields * out_width)
    return bits(hit).astype(jnp.bfloat16)


def four_fields(t, width):
    lane = lane_of(t.shape[0])
    c = jnp.where(lane < 2 * width, lane_roll(t, -3 * width), lane_roll(t, -2 * width))
    c = jnp.where(lane < width, lane_roll(t, -4 * width), c)
    return jnp.where(lane < 4 * width, c, 0.0)


def residual(w, beta, root, x, row, n, mid_total):
    mid, total = mid_total
    root_x = root[x, pl.ds(row - 8, n), :]
    return root_x * ((1.0 / TAU) * beta[x, pl.ds(row, n), :] - 6.0 * mid + total), root_x * root_x


def thirds(ref):
    n = ref.shape[0] // 3
    return [ref.at[pl.ds(i * n, n)] for i in range(3)]


def loop(begin, end, body, unroll=1):
    def step(i, carry):
        body(i)
        return carry

    lax.fori_loop(begin, end, step, 0, unroll=unroll)


def fold_rows(ref, k, n):
    return ref[k, pl.ds(0, n, stride=2), :] + ref[k, pl.ds(1, n, stride=2), :]


def unfold_rows(ref, k, n, value):
    ref[k, pl.ds(0, n, stride=2), :] = value
    ref[k, pl.ds(1, n, stride=2), :] = value


def prepare_kernel(table_any, ids_any, source_any, roughness_any, full, low, high, table, ids, roughness, sems):
    copies = [
        pltpu.make_async_copy(table_any, table, sems.at[0]),
        pltpu.make_async_copy(ids_any, ids, sems.at[1]),
        pltpu.make_async_copy(roughness_any, roughness, sems.at[2]),
        pltpu.make_async_copy(source_any, full.at[pl.ds(0, 4)], sems.at[3]),
    ]
    for copy in copies:
        copy.start()
    for copy in copies[:3]:
        copy.wait()
    block = lane_of(8) >> 3
    for i in range(2):
        for j in range(2):
            along_z = jnp.zeros((8, LANES), F32)
            for k in range(16):
                along_z = jnp.where(block == k, table[ids[i, j, k]], along_z)
            for x in range(8 * i, 8 * i + 8):
                full[4, x, pl.ds(8 * j, 8), :] = roughness[x, pl.ds(8 * j, 8), :] * along_z
    copies[3].wait()
    for x in range(HX0):
        for f in range(5):
            low[f, x] = full[f, x]
            high[f, x] = full[f, 16 - HX0 + x]


def edge_kernel(xlo, full, xhi, ylo, yhi):
    def put(x, f, plane):
        ylo[x, pl.ds(f * HY0, HY0), :] = plane[0:HY0]
        yhi[x, pl.ds(f * HY0, HY0), :] = plane[16 - HY0 : 16]

    for x in range(HX0):
        for f in range(5):
            put(x, f, xlo[f, x])
            put(x + HX0 + 16, f, xhi[f, x])

    def own(x):
        for f in range(5):
            put(x + HX0, f, full[f, x])

    loop(0, 16, own, 16)


def turn_kernel(xlo, full, xhi, ylo, yhi, turned, zlo, zhi, stage):
    stage[...] = jnp.zeros_like(stage)

    def turn(x, slot, planes):
        for f in range(5):
            stage[slot, pl.ds(f * Y0 + HY0, 16), :] = planes[f]
            stage[slot, pl.ds(f * Y0, HY0), :] = ylo[x, pl.ds(f * HY0, HY0), :]
            stage[slot, pl.ds(f * Y0 + HY0 + 16, HY0), :] = yhi[x, pl.ds(f * HY0, HY0), :]
        t = stage[slot].T
        turned[x] = t
        zlo[x] = t[0:HZ0]
        zhi[x] = t[128 - HZ0 : 128]

    for x in range(HX0):
        turn(x, 0, [xlo[f, x] for f in range(5)])
        turn(x + HX0 + 16, 1, [xhi[f, x] for f in range(5)])

    def own(k):
        for slot in range(4):
            x = 4 * k + slot
            turn(x + HX0, slot, [full[f, x] for f in range(5)])

    loop(0, 4, own, 2)


def down0_kernel(turned, zlo, zhi, out, ylo, yhi, beta, root, w, rsum, csum, rz, cz, stage):
    planes = 16 + 2 * HX0
    depth = 128 + 2 * HZ0
    half = depth // 2
    qb = pair_lanes(Y0, HY0, 8, 0, 0.5)
    qc = pair_lanes(Y0, HY0, 8, 32, 0.125, 2, 3)

    def prepare(x, t, row, n):
        lane = lane_of(n)
        v = lane_roll(jnp.where(lane < 4 * Y0, 0.0, t), -4 * Y0)
        v = v + lane_roll(v, Y0)
        v = v + lane_roll(v, 2 * Y0)
        root_v, inv_v = roots_of(v)
        pressure = lane >= 3 * Y0
        root[x, pl.ds(row, n), :] = jnp.where(pressure, inv_v, root_v)
        beta[x, pl.ds(8 + row, n), :] = TAU * t * jnp.where(pressure, root_v, inv_v)

    def setup(x):
        for ref in (beta, w):
            ref[x, pl.ds(0, 8), :] = jnp.zeros((8, LANES), F32)
            ref[x, pl.ds(8 + depth, 8), :] = jnp.zeros((8, LANES), F32)
        prepare(x, zlo[x], 0, HZ0)
        for r, n in chunks(128, 32):
            prepare(x, turned[x, pl.ds(r, n), :], HZ0 + r, n)
        prepare(x, zhi[x], HZ0 + 128, HZ0)

    loop(0, planes, setup, 2)

    def smooth(x):
        for r, n in chunks(depth, 32):
            mid, total = around(beta, x, 8 + r, n)
            w[x, pl.ds(8 + r, n), :] = jnp.where(root[x, pl.ds(r, n), :] > 0.0, 1.2 * mid + TAU * total, 0.0)

    loop(1, planes - 1, smooth, 10)

    def restrict(k):
        for r, n in chunks(depth, 32):
            x = HX0 + 2 * k
            res_a, coef_a = residual(w, beta, root, x, 8 + r, n, around(w, x, 8 + r, n))
            res_b, coef_b = residual(w, beta, root, x + 1, 8 + r, n, around(w, x + 1, 8 + r, n))
            rsum[k, pl.ds(r, n), :] = res_a + res_b
            csum[k, pl.ds(r, n), :] = coef_a + coef_b

    loop(0, 8, restrict, 4)

    def fold(k):
        rz[pl.ds(k * half, half), :] = fold_rows(rsum, k, half)
        cz[pl.ds(k * half, half), :] = fold_rows(csum, k, half)

    for k in range(8):
        fold(k)
    stage[...] = jnp.zeros_like(stage)
    for k in range(0, 8, 2):
        both = mm(((rz[pl.ds(k * half, 2 * half), :], qb), (cz[pl.ds(k * half, 2 * half), :], qc)))
        for i in range(2):
            stage[k + i, pl.ds(0, half), :] = both[i * half : (i + 1) * half]
    for k in range(8):
        t = stage[k].T
        out[k] = t[0:48]
        for a in range(6):
            ylo[k, pl.ds(a * H1, H1), :] = t[a * 8 : a * 8 + H1]
            yhi[k, pl.ds(a * H1, H1), :] = t[a * 8 + 8 - H1 : a * 8 + 8]


def join1_kernel(own, ylo, yhi, turned, low, high, stage):
    stage[...] = jnp.zeros_like(stage)
    for x in range(8):
        slot = x % 4
        for a in range(6):
            stage[slot, pl.ds(a * Y1 + H1, 8), :] = own[x, pl.ds(a * 8, 8), :]
            stage[slot, pl.ds(a * Y1, H1), :] = ylo[x, pl.ds(a * H1, H1), :]
            stage[slot, pl.ds(a * Y1 + H1 + 8, H1), :] = yhi[x, pl.ds(a * H1, H1), :]
        t = stage[slot].T[0:80]
        turned[x] = t
        if x < H1:
            low[x] = t
        if x >= 8 - H1:
            high[x - 8 + H1] = t


def down1_kernel(own, xlo, xhi, raw2, turned2, ylo2, yhi2, kept, rsum, csum, rz, cz, stage):
    w, beta, root = thirds(kept)

    def prepare(x, t):
        root_x, inv_x = roots_of(four_fields(t, Y1))
        root[x, pl.ds(0, 80), :] = root_x
        beta[x, pl.ds(8, 80), :] = TAU * t * inv_x
        for ref in (beta, w):
            ref[x, pl.ds(0, 8), :] = jnp.zeros((8, LANES), F32)
            ref[x, pl.ds(88, 8), :] = jnp.zeros((8, LANES), F32)

    for x in range(H1):
        prepare(x, xlo[x])
        prepare(x + H1 + 8, xhi[x])
    for x in range(8):
        prepare(x + H1, own[x])

    def smooth(x):
        for r, n in chunks(80, 40):
            mid, total = around(beta, x, 8 + r, n)
            w[x, pl.ds(8 + r, n), :] = jnp.where(root[x, pl.ds(r, n), :] > 0.0, 1.2 * mid + TAU * total, 0.0)

    loop(1, 19, smooth, 9)

    def restrict(k):
        for r, n in chunks(80, 40):
            x = 2 + 2 * k
            res_a, coef_a = residual(w, beta, root, x, 8 + r, n, around(w, x, 8 + r, n))
            res_b, coef_b = residual(w, beta, root, x + 1, 8 + r, n, around(w, x + 1, 8 + r, n))
            rsum[k, pl.ds(r, n), :] = res_a + res_b
            csum[k, pl.ds(r, n), :] = coef_a + coef_b

    loop(0, 8, restrict, 4)
    for k in range(8):
        rz[pl.ds(k * 40, 40), :] = fold_rows(rsum, k, 40)
        cz[pl.ds(k * 40, 40), :] = fold_rows(csum, k, 40)

    t2 = mm(((rz[...], pair_lanes(Y1, 2, 8, 0, 0.5)), (cz[...], pair_lanes(Y1, 2, 8, 32, 0.125, 2, 3))))
    stage[...] = jnp.zeros_like(stage)
    for x in range(8):
        t = t2[x * 40 : (x + 1) * 40]
        raw2[x] = t
        if 1 <= x < 7:
            stage[x % 4, pl.ds(0, 40), :] = t
            flat = stage[x % 4].T
            for a in range(6):
                turned2[x - 1, pl.ds(a * 4, 4), :] = flat[a * 8 + 2 : a * 8 + 6]
                yhi2[x - 1, pl.ds(a * H2, H2), :] = flat[a * 8 + 1 : a * 8 + 1 + H2]
                ylo2[x - 1, pl.ds(a * H2, H2), :] = flat[a * 8 + 2 : a * 8 + 2 + H2]


def down2_kernel(raw2, block, rsum, csum, beta2, root2, w2, stage):
    for x in range(8):
        root_x, inv_x = roots_of(four_fields(raw2[x], 8))
        root2[x] = root_x
        beta2[x, pl.ds(8, 40), :] = TAU * raw2[x] * inv_x
        for ref in (beta2, w2):
            ref[x, pl.ds(0, 8), :] = jnp.zeros((8, LANES), F32)
            ref[x, pl.ds(48, 8), :] = jnp.zeros((8, LANES), F32)
    for x in range(1, 7):
        mid, total = around(beta2, x, 8, 40)
        w2[x, pl.ds(8, 40), :] = jnp.where(root2[x] > 0.0, 1.2 * mid + TAU * total, 0.0)
    for k in range(2):
        x = 2 + 2 * k
        res, coef = jnp.zeros((32, LANES), F32), jnp.zeros((32, LANES), F32)
        for i in range(2):
            res_i, coef_i = residual(w2, beta2, root2, x + i, 12, 32, around(w2, x + i, 12, 32))
            res, coef = res + res_i, coef + coef_i
        rsum[k] = res
        csum[k] = coef
    rows = [jnp.concatenate([fold_rows(ref, k, 16) for k in range(2)], axis=0) for ref in (rsum, csum)]
    t3 = mm(((rows[0], pair_lanes(8, 2, 2, 0, 0.5)), (rows[1], pair_lanes(8, 2, 2, 8, 0.125, 2, 3))))

    stage[0, pl.ds(0, 32), :] = t3
    stage[0, pl.ds(32, 96), :] = jnp.zeros((96, LANES), F32)
    flat = stage[0].T[0:16]
    lane = lane_of(1)
    turns = [lane_roll(flat, 32 * g) for g in range(4)]
    packed = []
    for r in range(3):
        row = turns[0][4 * r : 4 * r + 1]
        for g in range(1, 4):
            row = jnp.where((lane >= 32 * g) & (lane < 32 * g + 32), turns[g][4 * r + g : 4 * r + g + 1], row)
        packed.append(row)
    packed = jnp.concatenate(packed, axis=0)
    for i in range(block.shape[0]):
        block[i] = packed


def join2_kernel(own, ylo, yhi, turned, low, high, stage):
    stage[...] = jnp.zeros_like(stage)
    for x in range(6):
        slot = x % 4
        for a in range(6):
            stage[slot, pl.ds(a * Y2 + H2, 4), :] = own[x, pl.ds(a * 4, 4), :]
            stage[slot, pl.ds(a * Y2, H2), :] = ylo[x, pl.ds(a * H2, H2), :]
            stage[slot, pl.ds(a * Y2 + H2 + 4, H2), :] = yhi[x, pl.ds(a * H2, H2), :]
        t = stage[slot].T[4:36]
        if 1 <= x < 5:
            turned[x - 1] = t
        if x < 5:
            high[x] = t
        if x >= 1:
            low[x - 1] = t


def plane_kernel(gx, gy, got, own2, xlo2, xhi2, own, lo4, hi4, b2, up, down, turns, stage):
    width = 2 * gy
    size_x = 2 * gx
    for x in range(4 + 2 * H2):
        t = xlo2[x] if x < H2 else own2[x - H2] if x < H2 + 4 else xhi2[x - H2 - 4]
        b2[x] = t
        up[size_x + x // 2, pl.ds(8 * (x % 2), 8), :] = t[24:32]
        down[size_x + x // 2, pl.ds(8 * (x % 2), 8), :] = t[0:8]
    for i in range(gx * gy):
        turns[0, pl.ds(3 * i, 3), :] = got[i]
    stage[...] = jnp.zeros_like(stage)
    for s in range(1, 4):
        turns[s] = lane_roll(turns[0], 32 * s)
    lane = lane_of(gy)
    for h in range(-(-gx // 4)):
        for i in range(12):
            r, g = i // 4, i % 4
            row = jnp.zeros((gy, LANES), F32)
            for q in range(min(4, gx - 4 * h)):
                part = turns[(q - g) % 4, pl.ds((4 * h + q) * gy * 3 + r, gy, stride=3), :]
                row = jnp.where((lane >= 32 * q) & (lane < 32 * q + 32), part, row)
            stage[h, pl.ds((i // 2) * width + i % 2, gy, stride=2), :] = row
        t = stage[h].T
        for q in range(min(4, gx - 4 * h)):
            for x in range(2):
                at = 2 * (4 * h + q) + x
                rows = t[32 * q + 16 * x : 32 * q + 16 * x + 16]
                own[at] = rows
                up[at] = rows
                down[at] = rows
                lo4[at] = rows[0:4]
                hi4[at] = rows[12:16]


def restrict_whole(size_x, off, width, w, beta, root, rsum, csum, rz, cz):
    def body(k):
        for r, n in chunks(64, 32):
            x = 2 * k + off
            res_a, coef_a = residual(w, beta, root, x, 8 + r, n, around_whole(w, x, 8 + r, n, width))
            res_b, coef_b = residual(w, beta, root, x + 1, 8 + r, n, around_whole(w, x + 1, 8 + r, n, width))
            rsum[k, pl.ds(r, n), :] = res_a + res_b
            csum[k, pl.ds(r, n), :] = coef_a + coef_b

    loop(0, size_x // 2, body, 4 if size_x % 8 == 0 else 2)
    for k in range(size_x // 2):
        rz[pl.ds(k * 32, 32), :] = fold_rows(rsum, k, 32)
        cz[pl.ds(k * 32, 32), :] = fold_rows(csum, k, 32)


def relax_whole(first, planes, begin, depth, width, src, dst, beta, root, unroll):
    def body(x):
        for r, n in chunks(depth, 32):
            r = r + begin
            mid, total = around_whole(src, x, 8 + r, n, width)
            live = root[x, pl.ds(r, n), :] > 0.0
            dst[x, pl.ds(8 + r, n), :] = jacobi(live, mid, beta[x, pl.ds(8 + r, n), :], total)

    loop(first, first + planes, body, unroll)


def coarse_kernel(gx, gy, own, below, above, below2, above2, e3, beta3, w3, v3, root3, beta4, w4, v4, root4, rsum, csum, rz, cz, fine3):
    size_x, width = 2 * gx, 2 * gy
    for ref in (beta3, w3, v3, root3, beta4, w4, v4):
        ref[...] = jnp.zeros_like(ref)

    def prepare(x, row, t):
        n = t.shape[0]
        root_x, inv_x = roots_of(four_fields(t, width))
        root3[x + OFF3, pl.ds(row, n), :] = root_x
        beta3[x + OFF3, pl.ds(8 + row, n), :] = TAU * t * inv_x

    def setup(x):
        prepare(x, 4, below2[x])
        prepare(x, 8, below[x])
        prepare(x, 24, own[x])
        prepare(x, 40, above[x])
        prepare(x, 56, above2[x])

    loop(0, size_x, setup, 4)

    def smooth(x):
        for r, n in chunks(64, 32):
            mid, total = around_whole(beta3, x, 8 + r, n, width)
            w3[x, pl.ds(8 + r, n), :] = jnp.where(root3[x, pl.ds(r, n), :] > 0.0, 1.2 * mid + TAU * total, 0.0)

    loop(OFF3, size_x + OFF3, smooth, 4)
    restrict_whole(size_x, OFF3, width, w3, beta3, root3, rsum, csum, rz, cz)
    t = mm(((rz[...], pair_lanes(width, 0, gy, 0, 0.5)), (cz[...], pair_lanes(width, 0, gy, 64, 0.125))))
    for x in range(gx):
        t_x = t[x * 32 : (x + 1) * 32]
        root_x, inv_x = roots_of(jnp.where(lane_of(32) < 4 * gy, lane_roll(t_x, 64), 0.0))
        root4[x + 1] = root_x
        beta4[x + 1, pl.ds(8, 32), :] = TAU * t_x * inv_x
        w4[x + 1, pl.ds(8, 32), :] = TAU * t_x * inv_x
    here, there = w4, v4
    for step in range(COARSE_ITERS - 1):
        relax_whole(1, gx, 0, 32, gy, here, there, beta4, root4, gx)
        here, there = there, here

    e4 = [here[x + 1, pl.ds(16, 16), :] * inverse(root4[x + 1, pl.ds(8, 16), :]) for x in range(gx)]
    e4 = mm(((jnp.concatenate(e4, axis=0), repeat_lanes(gy, width)),))
    for x in range(gx):
        unfold_rows(fine3, x, 16, e4[x * 16 : (x + 1) * 16])
        for i in range(2):
            at = 2 * x + i + OFF3
            w3[at, pl.ds(24, 32), :] = w3[at, pl.ds(24, 32), :] + root3[at, pl.ds(16, 32), :] * fine3[x]
    relax_whole(OFF3, size_x, 16, 32, width, w3, v3, beta3, root3, 4)
    relax_whole(OFF3, size_x, 16, 32, width, v3, w3, beta3, root3, 4)

    first3 = 2 * position("gx") - 2 + OFF3
    for k in range(6):
        e3[k] = w3[first3 + k, pl.ds(28, 24), :] * inverse(root3[first3 + k, pl.ds(20, 24), :])


def up_kernel(gx, gy, e3, b2, below, above, kept1, beta0, root0, out, beta2, root2, w2, v2, fine2, w1b, v1, w0b, v0, fine1, fine0, turned):
    w1, beta1, root1 = thirds(kept1)
    for ref in (w2, v2):
        ref[...] = jnp.zeros_like(ref)

    def prepare(x, row, t):
        n = t.shape[0]
        root_x, inv_x = roots_of(four_fields(t, Y2))
        root2[x, pl.ds(row, n), :] = root_x
        beta2[x, pl.ds(8 + row, n), :] = TAU * t * inv_x

    def setup(k):
        for i in range(2):
            x = 2 * k + i
            beta2[x, pl.ds(0, 8), :] = jnp.zeros((8, LANES), F32)
            beta2[x, pl.ds(56, 8), :] = jnp.zeros((8, LANES), F32)
            prepare(x, 0, below[2 * gx + k, pl.ds(8 * i, 8), :])
            prepare(x, 8, b2[x])
            prepare(x, 40, above[2 * gx + k, pl.ds(8 * i, 8), :])

    loop(0, 2 + H2, setup, 7)

    repeat = repeat_local(2 * gy, 2 * position("gy") - 2, Y2, 1)
    e = mm(((jnp.concatenate([e3[k] for k in range(6)], axis=0), repeat),))
    for k in range(6):
        unfold_rows(fine2, k, 24, e[k * 24 : (k + 1) * 24])
    for x in range(1, 13):
        mid, total = around(beta2, x, 8, 48)
        root_x = root2[x]
        add = root_x * fine2[(x - 1) // 2]
        w2[x, pl.ds(8, 48), :] = jnp.where(root_x > 0.0, 1.2 * mid + TAU * total + add, 0.0)
    for src, dst, begin, end in ((w2, v2, 2, 12), (v2, w2, 3, 11)):
        for x in range(begin, end):
            mid, total = around(src, x, 8, 48)
            dst[x, pl.ds(8, 48), :] = jacobi(root2[x] > 0.0, mid, beta2[x, pl.ds(8, 48), :], total)

    u2 = repeat_local(Y2, 2, Y1, 0)
    for ref in (w1b, v1):
        for row in (0, 88):
            ref[:, pl.ds(row, 8), :] = jnp.zeros((20, 8, LANES), F32)
    for ref in (w0b, v0):
        for row in (0, 152):
            ref[:, pl.ds(row, 8), :] = jnp.zeros((20, 8, LANES), F32)
    for k in range(0, 8, 4):
        e2 = [w2[x, pl.ds(12, 40), :] * inverse(root2[x, pl.ds(4, 40), :]) for x in range(k + 3, k + 7)]
        e = mm(((jnp.concatenate(e2, axis=0), u2),))
        for i in range(4):
            unfold_rows(fine1, k + i, 40, e[i * 40 : (i + 1) * 40])
    for x in range(3, 17):
        w1b[x, pl.ds(8, 80), :] = w1[x, pl.ds(8, 80), :] + root1[x, pl.ds(0, 80), :] * fine1[x // 2 - 1]

    def relax1(src, dst, begin, end):
        def body(x):
            for r, n in chunks(80, 40):
                mid, total = around(src, x, 8 + r, n)
                live = root1[x, pl.ds(r, n), :] > 0.0
                dst[x, pl.ds(8 + r, n), :] = jacobi(live, mid, beta1[x, pl.ds(8 + r, n), :], total)

        loop(begin, end, body, end - begin)

    relax1(w1b, v1, 4, 16)
    relax1(v1, w1b, 5, 15)

    u1 = repeat_local(Y1, H1, Y0, HY0)
    for k in range(0, 10, 2):
        e = [w1b[x, pl.ds(12, 72), :] * inverse(root1[x, pl.ds(4, 72), :]) for x in (k + 5, k + 6)]
        e = mm(((jnp.concatenate(e, axis=0), u1),))
        for i in range(2):
            unfold_rows(fine0, k + i, 72, e[i * 72 : (i + 1) * 72])

    def up0(k):
        for i in range(2):
            x = 2 * k + i
            for r, n in chunks(144, 48):
                mid, total = around(beta0, x + 1, 16 + r, n)
                root_x = root0[x + 1, pl.ds(8 + r, n), :]
                add = root_x * fine0[k, pl.ds(r, n), :]
                w0b[x, pl.ds(8 + r, n), :] = jnp.where(root_x > 0.0, 1.2 * mid + TAU * total + add, 0.0)

    loop(0, 10, up0, 5)

    def first0(x):
        for r, n in chunks(144, 24):
            mid, total = around(w0b, x, 8 + r, n)
            live = root0[x + 1, pl.ds(8 + r, n), :] > 0.0
            v0[x, pl.ds(8 + r, n), :] = jacobi(live, mid, beta0[x + 1, pl.ds(16 + r, n), :], total)

    loop(1, 19, first0, 9)

    def last0(j):
        for slot in range(4):
            k = 4 * j + slot
            x = k + 2
            for r, n in chunks(128, 32):
                mid, total = around(v0, x, 16 + r, n)
                root_x = root0[x + 1, pl.ds(16 + r, n), :]
                new = jacobi(root_x > 0.0, mid, beta0[x + 1, pl.ds(24 + r, n), :], total)
                turned[slot, pl.ds(r, n), :] = new * inverse(root_x)
        for slot in range(4):
            t = turned[slot].T
            for f in range(4):
                out[f, 4 * j + slot] = t[f * Y0 + HY0 : f * Y0 + HY0 + 16]

    loop(0, 4, last0)


def call(kernel, args, outs, scratch):
    vmem = pl.BlockSpec(memory_space=pltpu.VMEM)
    sizes = [a.shape for a in args] + outs + scratch
    held = sum(4 * math.prod(s[:-2]) * -(-s[-2] // 8) * 8 * LANES for s in sizes if len(s) > 1)
    return pl.pallas_call(
        kernel,
        out_shape=[jax.ShapeDtypeStruct(s, F32) for s in outs],
        in_specs=[vmem] * len(args),
        out_specs=[vmem] * len(outs),
        scratch_shapes=[pltpu.VMEM(s, F32) for s in scratch],
        compiler_params=pltpu.CompilerParams(vmem_limit_bytes=held + 2 * 1024 * 1024),
    )(*args)


def swap(to_up, to_down, axis, far=1):
    n = lax.axis_size(axis)
    from_below = lax.ppermute(to_up, axis, [(i, i + far) for i in range(n - far)])
    from_above = lax.ppermute(to_down, axis, [(i + far, i) for i in range(n - far)])
    return from_below, from_above


def whole_plane(block):
    return lax.all_to_all(block, ("gx", "gy"), 0, 0, tiled=True)


def position(axis):
    return lax.axis_index(axis).astype(jnp.int32)


def shards(gx, gy, source, material_ids, material_table, roughness):
    anywhere = pl.BlockSpec(memory_space=pltpu.HBM)
    full, low, high = pl.pallas_call(
        prepare_kernel,
        out_shape=[jax.ShapeDtypeStruct((5, n, 16, LANES), F32) for n in (16, HX0, HX0)],
        in_specs=[anywhere] * 4,
        out_specs=[pl.BlockSpec(memory_space=pltpu.VMEM)] * 3,
        scratch_shapes=[
            pltpu.SMEM(material_table.shape, F32),
            pltpu.SMEM(material_ids.shape, jnp.int32),
            pltpu.VMEM(roughness.shape, F32),
            pltpu.SemaphoreType.DMA((4,)),
        ],
        compiler_params=pltpu.CompilerParams(vmem_limit_bytes=4 * 1024 * 1024),
    )(material_table, material_ids, source, roughness)
    xlo, xhi = swap(high, low, "gx")
    planes = 16 + 2 * HX0
    ysend_lo, ysend_hi = call(edge_kernel, (xlo, full, xhi), [(planes, 15, LANES)] * 2, [])
    ylo, yhi = swap(ysend_hi, ysend_lo, "gy")
    turned, zsend_lo, zsend_hi = call(
        turn_kernel,
        (xlo, full, xhi, ylo, yhi),
        [(planes, 128, LANES)] + [(planes, HZ0, LANES)] * 2,
        [(4, LANES, LANES)],
    )
    zlo, zhi = swap(zsend_hi, zsend_lo, "gz")

    depth = 128 + 2 * HZ0
    own1, ysend_lo, ysend_hi, beta0, root0 = call(
        down0_kernel,
        (turned, zlo, zhi),
        [(8, 48, LANES)] + [(8, 6 * H1, LANES)] * 2 + [(planes, depth + 16, LANES), (planes, depth, LANES)],
        [(planes, depth + 16, LANES)] + [(8, depth, LANES)] * 2 + [(4 * depth, LANES)] * 2 + [(8, LANES, LANES)],
    )
    ylo, yhi = swap(ysend_hi, ysend_lo, "gy")
    turned1, low, high = call(
        join1_kernel, (own1, ylo, yhi), [(8, 80, LANES)] + [(H1, 80, LANES)] * 2, [(4, LANES, LANES)]
    )
    xlo, xhi = swap(high, low, "gx")

    x1, x2, x3 = 8 + 2 * H1, 4 + 2 * H2, 2 * gx
    raw2, turned2, ysend_lo, ysend_hi, kept1 = call(
        down1_kernel,
        (turned1, xlo, xhi),
        [(8, 40, LANES), (6, 24, LANES)] + [(6, 6 * H2, LANES)] * 2 + [(3 * x1, 96, LANES)],
        [(8, 80, LANES)] * 2
        + [(320, LANES)] * 2
        + [(4, LANES, LANES)],
    )
    ylo, yhi = swap(ysend_hi, ysend_lo, "gy")
    (block,) = call(
        down2_kernel,
        (raw2,),
        [(gx * gy, 3, LANES)],
        [(2, 32, LANES)] * 2 + [(8, 56, LANES), (8, 40, LANES), (8, 56, LANES), (1, LANES, LANES)],
    )
    got = whole_plane(block)
    turned2, low, high = call(
        join2_kernel, (turned2, ylo, yhi), [(4, 32, LANES)] + [(H2, 32, LANES)] * 2, [(4, LANES, LANES)]
    )
    xlo, xhi = swap(high, low, "gx")
    own3, lo4, hi4, b2, to_up, to_down = call(
        functools.partial(plane_kernel, gx, gy),
        (got, turned2, xlo, xhi),
        [(x3, 16, LANES)] + [(x3, 4, LANES)] * 2 + [(x2, 32, LANES)] + [(x3 + x2 // 2, 16, LANES)] * 2,
        [(4, 3 * gx * gy, LANES), (2, LANES, LANES)],
    )
    below, above = swap(to_up, to_down, "gz")
    below2, above2 = swap(hi4, lo4, "gz", 2)
    (e3,) = call(
        functools.partial(coarse_kernel, gx, gy),
        (own3, below, above, below2, above2),
        [(6, 24, LANES)],
        [(x3 + 2 * OFF3, 80, LANES)] * 3
        + [(x3 + 2 * OFF3, 64, LANES)]
        + [(gx + 2, 48, LANES)] * 3
        + [(gx + 2, 32, LANES)]
        + [(gx, 64, LANES)] * 2
        + [(gx * 32, LANES)] * 2
        + [(gx, 32, LANES)],
    )

    (correction,) = call(
        functools.partial(up_kernel, gx, gy),
        (e3, b2, below, above, kept1, beta0, root0),
        [(4, 16, 16, LANES)],
        [(x2, 64, LANES), (x2, 48, LANES), (x2, 64, LANES), (x2, 64, LANES), (6, 48, LANES)]
        + [(x1, 96, LANES)] * 2
        + [(20, 160, LANES)] * 2
        + [(8, 80, LANES), (10, 144, LANES), (4, LANES, LANES)],
    )
    return correction


def solution(mesh):
    return jax.shard_map(
        functools.partial(shards, mesh.shape["gx"], mesh.shape["gy"]),
        mesh=mesh,
        in_specs=(P(None, "gx", "gy", "gz"), P("gx", "gy", "gz"), P(), P("gx", "gy", "gz")),
        out_specs=P(None, "gx", "gy", "gz"),
        check_vma=False,
    )
```
